32 devices in a mesh: group: 2 (over x), expert: 16 (over z, y, core).
Axes of the slice: x: 2, y: 2, z: 4, core: 2. Of those that a mesh axis runs over, the one named last changes fastest.
Arguments:
- tokens: bfloat16 [2, 128, 2048], P('group', 'expert'), may hold values from -6 to 6
- norm_gain: float32 [2048], replicated, may hold values from 0.1 to 1.9
- routes: int32 [2, 2, 128, 8], P(None, 'group', 'expert'), may hold values from 0 to 15, all different within a row; in each aligned block of 8 rows (0 to 7, 8 to 15, ..., all dimensions but the last counted through in order) at most 8 rows name the same one
- route_scale: float32 [2, 2, 128, 8], P(None, 'group', 'expert'), may hold values from 0.1 to 1
- changed: int32 [2, 4], P('group'), may hold values from 0 to 15, as said below
- rollout_up: bfloat16 [16, 768, 2048], P('expert'), may hold values from -0.125 to 0.125
- rollout_down: bfloat16 [16, 768, 2048], P('expert'), may hold values from -0.21875 to 0.21875
- learner_up: bfloat16 [16, 768, 2048], P('expert', 'group'), may hold values from -0.125 to 0.125
- learner_down: bfloat16 [16, 768, 2048], P('expert', 'group'), may hold values from -0.21875 to 0.21875
Outputs:
- updated: bfloat16 [2, 128, 2048], P('group', 'expert')
The draws below stay inside these ranges and needn't reach their ends.
Inputs may be any that keep to these rules, and one draw needn't show every extreme that they name: `routes`: at one step, no expert is named by more than 8 of the 8 rows of one device; some aligned block of 8 rows reaches 8. `changed`: each group's row lists 4 different experts.
All inputs are finite; a program needn't handle non-finite values.
Results may differ from the reference program's by a relative error of at most 0.0062.
Values may be sent and summed in bfloat16 or wider, within the bound.
No kernel may reach another device: no remote copies, remote signals or barrier semaphores. Data moves between devices by JAX's collectives and lax.ppermute only.
A program may use at most 64 MiB of HBM per device.

```python
import math
import jax
import jax.numpy as jnp
import numpy as np
from jax import lax

D = 2048
H = 768
TOPK = 8
STEPS = 2
ROW_DEV = 8
EXPERTS = 16
GROUPS = 2
ROWS = 128
CAP = 8
CHANGED_COUNT = 4
N_EXPERT = 16


def pick_changed(group_key):
    return jax.random.permutation(group_key, EXPERTS)[:CHANGED_COUNT]


def draw_changed(key, part):
    group_keys = jax.random.split(jax.random.fold_in(key, 17), GROUPS)
    return jax.vmap(pick_changed)(group_keys).astype(jnp.int32)


def levels(own_key, extent, pieces, smallest, high):
    def one(axis_at, parts):
        draws = jax.random.uniform(jax.random.fold_in(jax.random.fold_in(own_key, 6), axis_at), (parts,), jnp.float32, smallest / len(pieces), high / len(pieces))
        return jnp.repeat(jnp.exp(draws), extent[axis_at] // parts).reshape((-1,) + (1,) * (len(extent) - axis_at - 1))

    factor_of = one(*pieces[0])
    for cut in pieces[1:]:
        factor_of = factor_of * one(*cut)
    return factor_of


def routed_block(stream_key, own, number, rows, count, top, reach, skew):
    order = jax.random.permutation(stream_key, count)
    heavy_load, usual = portions_of(count, rows * top, reach, skew, True), portions_of(count, rows * top, reach, skew, False)
    places = jnp.arange(count)

    def named(sizes, turn):
        used = int((sizes > 0).sum())
        fixed = max(1, used // 4)
        moved = fixed + (places - fixed + turn * (used - fixed)) % max(1, count - fixed)
        return jnp.zeros((count,), jnp.int32).at[order[jnp.where(places < fixed, places, moved)]].set(jnp.asarray(sizes, jnp.int32))

    sizes = jnp.where(number % 4 == 0, named(heavy_load, number // 4), named(usual, number - number // 4 - 1))
    mixed = jax.random.permutation(jax.random.fold_in(own, 3), count)
    source_of, sink = mixed[0:count // 2 * 2:2], mixed[1:count // 2 * 2:2]
    slack = jnp.minimum(sizes[source_of] - 1, reach - sizes[sink]) // 2
    slack = jnp.where((source_of == order[0]) | (sink == order[0]) | (sizes[sink] == 0), 0, jnp.maximum(slack, 0))
    moved = jax.random.randint(jax.random.fold_in(own, 4), (count // 2,), 0, 1 << 20) % (slack + 1)
    sizes = sizes.at[source_of].add(-moved).at[sink].add(moved)
    items = jnp.searchsorted(jnp.cumsum(sizes), jnp.arange(rows * top), side="right").astype(jnp.int32)
    table = items.reshape(top, rows).T
    table = table[jax.random.permutation(jax.random.fold_in(own, 1), rows)]
    turn = jax.random.randint(jax.random.fold_in(own, 2), (rows, 1), 0, top)
    return jnp.take_along_axis(table, (jnp.arange(top)[None, :] + turn) % top, axis=1)


def portions_of(count, total, limit, lean, full):
    loads = [(1 << 20) // math.isqrt(standing ** lean) + 1 for standing in range(1, count + 1)]
    largest = limit if full else min(limit, max(-(-total // count), total * loads[0] // sum(loads)))
    least = 1 if total - largest >= count - 1 else 0
    counts, spare = [largest] + [least] * (count - 1), total - largest - least * (count - 1)
    while spare > 0:
        free = [i for i in range(1, count) if counts[i] < largest] or [i for i in range(1, count) if counts[i] < limit]
        mass, budget = sum([loads[i] for i in free]), spare
        for i in free:
            addition = min(limit - counts[i], max(1, budget * loads[i] // mass), spare)
            counts[i] = counts[i] + addition
            spare = spare - addition
    return np.array(counts)


def scatter_about(key, shape, width, most, shards=(), kind=jnp.bfloat16):
    result = jax.random.normal(key, shape, jnp.float32) * width
    if len(shards) > 0:
        result = levels(key, shape, shards, -0.22, 0.18) * result
    return jnp.clip(result, min=-most, max=most).astype(kind)


def setup_inputs(seed: int = 0) -> dict:
    streams_of = jax.random.split(jax.random.key(seed), 10)
    tokens = scatter_about(streams_of[0], (GROUPS, ROWS, D), 1.0, 6.0, ((0, 2), (1, 16)))
    norm_gain = jnp.clip(1.0 + 0.18 * jax.random.normal(streams_of[1], (D,), jnp.float32), 0.1, 1.9)
    routes_keys = jax.random.split(jax.random.fold_in(streams_of[2], 1), STEPS * GROUPS * ROWS // ROW_DEV)
    routes_turns = jax.random.permutation(jax.random.fold_in(streams_of[2], 3), STEPS * GROUPS * ROWS // ROW_DEV)
    routes = jax.vmap(lambda own, number: routed_block(jax.random.fold_in(streams_of[2], 2), own, number, ROW_DEV, EXPERTS, TOPK, CAP, 2))(routes_keys, routes_turns).reshape((STEPS, GROUPS, ROWS, TOPK))
    route_scale = jnp.clip(jnp.exp(math.log(1.0) - 2.3025851 * jax.random.uniform(streams_of[3], (STEPS, GROUPS, ROWS, TOPK), jnp.float32) ** levels(streams_of[3], (STEPS, GROUPS, ROWS, TOPK), ((1, 2), (2, 16)), -0.2, 0.2)), 0.1, 1.0)
    changed = draw_changed(jax.random.fold_in(streams_of[9], 71), 0)
    rollout_up = scatter_about(streams_of[5], (EXPERTS, H, D), D ** -0.5, 0.125, ((0, 16),))
    rollout_down = scatter_about(streams_of[6], (EXPERTS, H, D), H ** -0.5, 0.21875, ((0, 16),))
    learner_up = scatter_about(streams_of[7], (EXPERTS, H, D), D ** -0.5, 0.125, ((0, 16), (1, 2)))
    learner_down = scatter_about(streams_of[8], (EXPERTS, H, D), H ** -0.5, 0.21875, ((0, 16), (1, 2)))
    return dict(tokens=tokens, norm_gain=norm_gain, routes=routes, route_scale=route_scale, changed=changed, rollout_up=rollout_up, rollout_down=rollout_down, learner_up=learner_up, learner_down=learner_down)


def normalize(state, norm_gain):
    scale = lax.rsqrt(lax.optimization_barrier(jnp.mean(state * state, axis=-1, keepdims=True)) + 1e-06)
    return (state * scale * norm_gain).astype(jnp.bfloat16)

def expert_apply(inputs, up_rows, down_rows):
    pre_act = lax.dot_general(inputs, up_rows, (((1,), (1,)), ((), ())), preferred_element_type=jnp.float32)
    hidden = jax.nn.silu(pre_act).astype(jnp.bfloat16)
    return jnp.dot(hidden, down_rows, preferred_element_type=jnp.float32)

def slot_table(chosen):
    blocks = chosen.reshape(N_EXPERT, ROW_DEV * TOPK)
    hits = (blocks[:, :, None] == jnp.arange(EXPERTS, dtype=jnp.int32)[None, None, :]).astype(jnp.int32)
    before = jnp.cumsum(hits, axis=1) - hits
    return lax.optimization_barrier(jnp.sum(before * hits, axis=2)).reshape(ROWS, TOPK).astype(jnp.int32)

def reference(tokens, norm_gain, routes, route_scale, changed, rollout_up, rollout_down, learner_up, learner_down):
    state = tokens.astype(jnp.float32)
    row_ids = jnp.arange(ROWS, dtype=jnp.int32)
    source = (row_ids // ROW_DEV).astype(jnp.int32)
    expert_ids = jnp.arange(EXPERTS, dtype=jnp.int32)
    for step in range(STEPS):

        def one_group(packed, step=step):
            group_state, chosen, weights, changed_ids = packed
            normed = normalize(group_state, norm_gain)
            column = (source[:, None] * CAP + slot_table(chosen)).astype(jnp.int32)
            filler = jnp.broadcast_to(row_ids[:, None], chosen.shape).astype(jnp.int32)
            table = jnp.full((EXPERTS, N_EXPERT * CAP), ROWS, jnp.int32).at[chosen, column].set(filler)
            padded = jnp.concatenate([normed, jnp.zeros((1, D), jnp.bfloat16)], axis=0)

            def one_expert(items):
                index_list, up_rows, down_rows, fresh_up, fresh_down, expert = items
                inputs = padded[index_list]
                if step > 0:
                    fresh = jnp.any(changed_ids == expert)
                    up_rows = jnp.where(fresh, fresh_up, up_rows)
                    down_rows = jnp.where(fresh, fresh_down, down_rows)
                return expert_apply(inputs, up_rows, down_rows).astype(jnp.bfloat16)
            outputs = lax.map(one_expert, (table, rollout_up, rollout_down, learner_up, learner_down, expert_ids))
            picked = outputs[chosen, column].astype(jnp.float32)
            return group_state + lax.optimization_barrier(jnp.sum(weights[:, :, None] * picked, axis=1))
        state = lax.map(one_group, (state, routes[step], route_scale[step], changed))
    return state.astype(jnp.bfloat16)
```

```python
import jax
import jax.numpy as jnp
from jax import lax
from jax.sharding import PartitionSpec as P


def normalize(state, norm_gain):
    scale = lax.rsqrt(jnp.mean(state * state, axis=-1, keepdims=True) + 1e-06)
    return (state * scale * norm_gain).astype(jnp.bfloat16)


def expert_apply(inputs, up_rows, down_rows):
    pre_act = lax.dot_general(
        inputs, up_rows, (((1,), (1,)), ((), ())), preferred_element_type=jnp.float32
    )
    hidden = jax.nn.silu(pre_act).astype(jnp.bfloat16)
    return jnp.dot(hidden, down_rows, preferred_element_type=jnp.float32)


def split_parts(value):
    parts = []
    rest = value
    for _ in range(3):
        part = lax.reduce_precision(rest, 8, 7)
        parts.append(part.astype(jnp.bfloat16))
        rest = rest - part
    return parts


def dense_weights(chosen, weights, expert_ids):
    hit = chosen[:, :, None] == expert_ids[None, None, :]
    return jnp.sum(jnp.where(hit, weights[:, :, None], 0.0), axis=1)


def pack(normed, tables):
    columns = [part for table in tables for part in split_parts(table)]
    width = sum(column.shape[1] for column in columns)
    padding = -width % 128
    columns.append(jnp.zeros((normed.shape[0], padding), jnp.bfloat16))
    return jnp.concatenate([normed] + columns, axis=1)


def unpack(gathered, width, experts, owner, index):
    start = width + 3 * index * experts
    parts = gathered[:, start : start + 3 * experts].astype(jnp.float32)
    parts = parts.reshape(-1, 3, experts)
    total = parts[:, 0] + parts[:, 1] + parts[:, 2]
    mine = jnp.arange(experts, dtype=jnp.int32)[None, :] == owner
    return jnp.sum(jnp.where(mine, total, 0.0), axis=1, keepdims=True)


def local(
    tokens,
    norm_gain,
    routes,
    route_scale,
    changed,
    rollout_up,
    rollout_down,
    learner_up,
    learner_down,
):
    experts = lax.axis_size("expert")
    groups = lax.axis_size("group")
    owner = lax.axis_index("expert")
    group = lax.axis_index("group")
    row_count, width = tokens.shape[1], tokens.shape[2]
    steps_total = routes.shape[0]
    stale_up = rollout_up[0]
    stale_down = rollout_down[0]
    expert_ids = jnp.arange(experts, dtype=jnp.int32)
    fresh_expert = jnp.any(changed[0][:, None] == expert_ids[None, :], axis=0)
    rows_all = row_count * experts
    split = rows_all < learner_up.shape[1]
    if not split:
        is_fresh = jnp.any(changed[0] == owner)
        newer_up = jnp.where(
            is_fresh, lax.all_gather(learner_up, "group", axis=1, tiled=True)[0], stale_up
        )
        newer_down = jnp.where(
            is_fresh, lax.all_gather(learner_down, "group", axis=1, tiled=True)[0], stale_down
        )
    state = tokens[0].astype(jnp.float32)
    for step in range(steps_total):
        normed = normalize(state, norm_gain)
        weights = dense_weights(routes[step, 0], route_scale[step, 0], expert_ids)
        if step == 0 or not split:
            packed = pack(normed, [weights])
            gathered = lax.all_gather(packed, "expert", axis=0, tiled=True)
            scale = unpack(gathered, width, experts, owner, 0)
            if step == 0:
                result = expert_apply(gathered[:, :width], stale_up, stale_down)
            else:
                result = expert_apply(gathered[:, :width], newer_up, newer_down)
            share = (result * scale).astype(jnp.bfloat16)
            delta = lax.psum_scatter(share, "expert", scatter_dimension=0, tiled=True)
        else:
            fresh = jnp.where(fresh_expert[None, :], weights, 0.0)
            packed = pack(normed, [weights - fresh, fresh])
            gathered = lax.all_gather(packed, ("group", "expert"), axis=0, tiled=True)
            own = lax.dynamic_slice_in_dim(gathered, group * rows_all, rows_all, 0)
            stale_scale = unpack(own, width, experts, owner, 0)
            fresh_scale = unpack(gathered, width, experts, owner, 1)
            stale = expert_apply(own[:, :width], stale_up, stale_down) * stale_scale
            newer = expert_apply(gathered[:, :width], learner_up[0], learner_down[0]) * fresh_scale
            newer = newer.reshape(groups, rows_all, width)
            at_home = (jnp.arange(groups) == group)[:, None, None]
            share = jnp.where(at_home, newer + stale[None], newer).astype(jnp.bfloat16)
            share = share.reshape(groups * rows_all, width)
            delta = lax.psum_scatter(share, ("group", "expert"), scatter_dimension=0, tiled=True)
        state = state + delta.astype(jnp.float32)
    return state.astype(jnp.bfloat16)[None]


def solution(mesh):
    placed = (
        P("group", "expert", None),
        P(),
        P(None, "group", "expert", None),
        P(None, "group", "expert", None),
        P("group", None),
        P("expert", None, None),
        P("expert", None, None),
        P("expert", "group", None),
        P("expert", "group", None),
    )
    return jax.shard_map(
        local, mesh=mesh, in_specs=placed, out_specs=P("group", "expert", None), check_vma=False
    )
```

```python
import jax
import jax.numpy as jnp
from jax import lax
from jax.sharding import PartitionSpec as P


def normalize(state, norm_gain):
    scale = lax.rsqrt(jnp.mean(state * state, axis=-1, keepdims=True) + 1e-06)
    return (state * scale * norm_gain).astype(jnp.bfloat16)


def expert_apply(inputs, up_rows, down_rows):
    pre_act = lax.dot_general(
        inputs, up_rows, (((1,), (1,)), ((), ())), preferred_element_type=jnp.float32
    )
    hidden = jax.nn.silu(pre_act).astype(jnp.bfloat16)
    return jnp.dot(hidden, down_rows, preferred_element_type=jnp.float32)


def split_parts(value):
    parts = []
    rest = value
    for _ in range(3):
        part = lax.reduce_precision(rest, 8, 7)
        parts.append(part.astype(jnp.bfloat16))
        rest = rest - part
    return parts


def dense_weights(chosen, weights, expert_ids):
    hit = chosen[:, :, None] == expert_ids[None, None, :]
    return jnp.sum(jnp.where(hit, weights[:, :, None], 0.0), axis=1)


def pack(normed, tables):
    columns = [part for table in tables for part in split_parts(table)]
    width = sum(column.shape[1] for column in columns)
    padding = -width % 128
    columns.append(jnp.zeros((normed.shape[0], padding), jnp.bfloat16))
    return jnp.concatenate([normed] + columns, axis=1)


def unpack(gathered, width, experts, owner, index):
    start = width + 3 * index * experts
    parts = gathered[:, start : start + 3 * experts].astype(jnp.float32)
    total = parts[:, :experts] + parts[:, experts : 2 * experts] + parts[:, 2 * experts :]
    mine = jnp.arange(experts, dtype=jnp.int32)[None, :] == owner
    return jnp.sum(jnp.where(mine, total, 0.0), axis=1, keepdims=True)


def swap(value, axis, distance):
    size = lax.axis_size(axis)
    return lax.ppermute(value, axis, [(i, i ^ distance) for i in range(size)])


def gather_rows(block):
    count = lax.axis_size("expert") // 2
    parts = [block] + [swap(block, "expert", 2 * j) for j in range(1, count)]
    half = jnp.concatenate(parts, axis=0)
    return half, swap(half, "expert", 1)


def return_rows(near, far):
    count = lax.axis_size("expert") // 2
    total = near + swap(far.astype(jnp.bfloat16), "expert", 1).astype(jnp.float32)
    total = total.reshape(count, -1, total.shape[-1])
    sent = total.astype(jnp.bfloat16)
    result = total[0]
    for j in range(1, count):
        result = result + swap(sent[j], "expert", 2 * j).astype(jnp.float32)
    return result


def exchange_plan(tokens, norm_gain, routes, route_scale, changed, stale, learner):
    experts = lax.axis_size("expert")
    groups = lax.axis_size("group")
    owner = lax.axis_index("expert")
    row_count, width = tokens.shape[1], tokens.shape[2]
    expert_ids = jnp.arange(experts, dtype=jnp.int32)
    fresh_expert = jnp.any(changed[0][:, None] == expert_ids[None, :], axis=0)
    state = tokens[0].astype(jnp.float32)
    for step in range(routes.shape[0]):
        normed = normalize(state, norm_gain)
        weights = dense_weights(routes[step, 0], route_scale[step, 0], expert_ids)
        if step == 0:
            shares = []
            for rows in gather_rows(pack(normed, [weights])):
                scale = unpack(rows, width, experts, owner, 0)
                shares.append(expert_apply(rows[:, :width], *stale) * scale)
            state = state + return_rows(*shares)
        else:
            fresh = jnp.where(fresh_expert[None, :], weights, 0.0)
            block = pack(normed, [weights - fresh, fresh])
            blocks = [block] + [swap(block, "group", d) for d in range(1, groups)]
            shares = []
            for rows in gather_rows(jnp.concatenate(blocks, axis=0)):
                new = expert_apply(rows[:, :width], *learner)
                new = new * unpack(rows, width, experts, owner, 1)
                new = new.reshape(-1, groups, row_count, width)
                own = rows.reshape(-1, groups, row_count, rows.shape[-1])[:, 0]
                own = own.reshape(-1, rows.shape[-1])
                old = expert_apply(own[:, :width], *stale)
                old = old * unpack(own, width, experts, owner, 0)
                old = old.reshape(-1, 1, row_count, width)
                both = jnp.concatenate([new[:, :1] + old, new[:, 1:]], axis=1)
                shares.append(both.reshape(-1, width))
            total = return_rows(*shares).reshape(groups, row_count, width)
            delta = total[0]
            for d in range(1, groups):
                sent = total[d].astype(jnp.bfloat16)
                delta = delta + swap(sent, "group", d).astype(jnp.float32)
            state = state + delta
    return state.astype(jnp.bfloat16)[None]


def gather_plan(tokens, norm_gain, routes, route_scale, changed, stale, learner):
    experts = lax.axis_size("expert")
    owner_index = lax.axis_index("expert")
    row_count = tokens.shape[1]
    top_count = routes.shape[3]
    capacity = min(row_count, max(2, 2 * row_count * top_count // experts))
    is_fresh = jnp.any(changed[0] == owner_index)
    fresh = [lax.all_gather(part, "group", axis=0, tiled=True) for part in learner]
    newer = [jnp.where(is_fresh, new, old) for new, old in zip(fresh, stale)]
    state = tokens[0].astype(jnp.float32)
    buffer_ids = jnp.arange(experts * capacity, dtype=jnp.int32)
    expert_ids = jnp.arange(experts, dtype=jnp.int32)
    for step in range(routes.shape[0]):
        normed = normalize(state, norm_gain)
        chosen = routes[step, 0]
        weights = route_scale[step, 0]
        hits = (chosen.reshape(-1)[:, None] == expert_ids[None, :]).astype(jnp.int32)
        before = jnp.cumsum(hits, axis=0) - hits
        slot_pos = jnp.sum(before * hits, axis=1).reshape(chosen.shape)
        target = chosen * capacity + slot_pos
        placed = (target[:, :, None] == buffer_ids[None, None, :]).astype(jnp.float32)
        merge_weights = jnp.sum(placed * weights[:, :, None], axis=1)
        send_matrix = jnp.sum(placed, axis=1).astype(jnp.bfloat16)
        outgoing = lax.dot_general(
            send_matrix, normed, (((0,), (0,)), ((), ())), preferred_element_type=jnp.float32
        )
        outgoing = outgoing.astype(jnp.bfloat16).reshape(experts, capacity, -1)
        received = lax.all_to_all(outgoing, "expert", split_axis=0, concat_axis=0, tiled=True)
        flat = received.reshape(-1, received.shape[-1])
        result = expert_apply(flat, *(stale if step == 0 else newer))
        answer = result.astype(jnp.bfloat16).reshape(received.shape)
        returned = lax.all_to_all(answer, "expert", split_axis=0, concat_axis=0, tiled=True)
        flat_back = returned.reshape(experts * capacity, -1).astype(jnp.float32)
        state = state + jnp.dot(merge_weights, flat_back, precision=lax.Precision.HIGHEST)
    return state.astype(jnp.bfloat16)[None]


def local(
    tokens,
    norm_gain,
    routes,
    route_scale,
    changed,
    rollout_up,
    rollout_down,
    learner_up,
    learner_down,
):
    experts = lax.axis_size("expert")
    groups = lax.axis_size("group")
    fewer = tokens.shape[1] * experts < learner_up.shape[1]
    paired = experts & (experts - 1) == 0 and groups & (groups - 1) == 0 and experts > 1
    plan = exchange_plan if fewer and paired else gather_plan
    stale = (rollout_up[0], rollout_down[0])
    learner = (learner_up[0], learner_down[0])
    return plan(tokens, norm_gain, routes, route_scale, changed, stale, learner)


def solution(mesh):
    placed = (
        P("group", "expert", None),
        P(),
        P(None, "group", "expert", None),
        P(None, "group", "expert", None),
        P("group", None),
        P("expert", None, None),
        P("expert", None, None),
        P("expert", "group", None),
        P("expert", "group", None),
    )
    return jax.shard_map(
        local, mesh=mesh, in_specs=placed, out_specs=P("group", "expert", None), check_vma=False
    )
```

```python
import functools
import jax
import jax.numpy as jnp
from jax import lax
from jax.experimental import pallas as pl
from jax.experimental.pallas import tpu as pltpu
from jax.sharding import PartitionSpec as P

LANES = 128
MIB = 1 << 20


def normalize(state, norm_gain):
    scale = lax.rsqrt(jnp.mean(state * state, axis=-1, keepdims=True) + 1e-06)
    return (state * scale * norm_gain).astype(jnp.bfloat16)


def expert_apply(inputs, up_rows, down_rows):
    pre_act = lax.dot_general(
        inputs, up_rows, (((1,), (1,)), ((), ())), preferred_element_type=jnp.float32
    )
    hidden = jax.nn.silu(pre_act).astype(jnp.bfloat16)
    return jnp.dot(hidden, down_rows, preferred_element_type=jnp.float32)


def table_width(experts):
    return -(-6 * experts // LANES) * LANES


def weight_table(experts, chosen, weights, changed):
    shape = (chosen.shape[0], table_width(experts))
    lane = lax.broadcasted_iota(jnp.int32, shape, 1)
    section, expert = lane // experts, lane % experts
    dense = jnp.zeros(shape, jnp.float32)
    for k in range(chosen.shape[1]):
        dense = jnp.where(chosen[:, k : k + 1] == expert, weights[:, k : k + 1], dense)
    fresh = section < 0
    for item in changed:
        fresh = fresh | (expert == item)
    high = dense.astype(jnp.bfloat16).astype(jnp.float32)
    rest = dense - high
    middle = rest.astype(jnp.bfloat16).astype(jnp.float32)
    low = rest - middle
    part = section % 3
    value = jnp.where(part == 0, high, jnp.where(part == 1, middle, low))
    value = jnp.where(fresh, jnp.where(section < 3, 0.0, value), jnp.where(section < 3, value, 0.0))
    return jnp.where(section < 6, value, 0.0).astype(jnp.bfloat16)


def row_weights(experts, table, fresh):
    owner = lax.axis_index("expert")
    lane = lax.broadcasted_iota(jnp.int32, table.shape, 1)
    section = lane // experts
    first = 3 if fresh else 0
    mine = (lane % experts == owner) & (section >= first) & (section < first + 3)
    return jnp.sum(jnp.where(mine, table.astype(jnp.float32), 0.0), axis=1, keepdims=True)


def first_kernel(experts, tokens, gain, routes, scales, out):
    width = tokens.shape[1]
    normed = normalize(tokens[...].astype(jnp.float32), gain[...])
    table = weight_table(experts, routes[...], scales[...], [])
    for j in range(out.shape[0]):
        out[j, :, :width] = normed
        out[j, :, width:] = table


def next_kernel(experts, changed_count, previous, returned, gain, routes, scales, changed, state_out, out):
    width = previous.shape[1]
    state = previous[...].astype(jnp.float32) + jnp.sum(returned[...].astype(jnp.float32), axis=0)
    state_out[...] = state
    normed = normalize(state, gain[...])
    items = [changed[0, i] for i in range(changed_count)]
    table = weight_table(experts, routes[...], scales[...], items)
    for j in range(out.shape[0]):
        out[j, :, :width] = normed
        out[j, :, width:] = table


def last_kernel(previous, returned, out):
    state = previous[...] + jnp.sum(returned[...].astype(jnp.float32), axis=0)
    out[...] = state.astype(jnp.bfloat16)


def mlp_kernel(experts, fresh_flags, near, far, *refs):
    count = len(fresh_flags)
    sources = refs[: 2 * count]
    near_out, far_out = refs[2 * count : 2 * count + 2]
    buffers = refs[2 * count + 2 : 4 * count + 2]
    sems = refs[4 * count + 2]
    copies = [
        pltpu.make_async_copy(source, buffer, sems.at[i])
        for i, (source, buffer) in enumerate(zip(sources, buffers))
    ]
    for copy in copies:
        copy.start()
    half, width = near_out.shape
    inputs = jnp.concatenate([near[:, :width], far[:, :width]], axis=0)
    table = jnp.concatenate([near[:, width:], far[:, width:]], axis=0)
    total = None
    for i, fresh in enumerate(fresh_flags):
        copies[2 * i].wait()
        pre_act = lax.dot_general(
            inputs,
            buffers[2 * i][...],
            (((1,), (1,)), ((), ())),
            preferred_element_type=jnp.float32,
        )
        hidden = (pre_act / (1.0 + jnp.exp(-pre_act))).astype(jnp.bfloat16)
        copies[2 * i + 1].wait()
        result = jnp.dot(hidden, buffers[2 * i + 1][...], preferred_element_type=jnp.float32)
        result = result * row_weights(experts, table, fresh)
        total = result if total is None else total + result
    near_out[...] = total[:half]
    far_out[...] = total[half:].astype(jnp.bfloat16)


def run_mlp(near, far, weights, fresh_flags):
    experts = lax.axis_size("expert")
    rows = near.shape[0]
    width = weights[0].shape[1]
    hidden = sum(part.shape[0] for part in weights)
    in_vmem = pl.BlockSpec(memory_space=pltpu.VMEM)
    return pl.pallas_call(
        functools.partial(mlp_kernel, experts, fresh_flags),
        out_shape=(
            jax.ShapeDtypeStruct((rows, width), jnp.float32),
            jax.ShapeDtypeStruct((rows, width), jnp.bfloat16),
        ),
        in_specs=[in_vmem] * 2 + [pl.BlockSpec(memory_space=pl.ANY)] * len(weights),
        out_specs=(in_vmem, in_vmem),
        scratch_shapes=[pltpu.VMEM(part.shape, part.dtype) for part in weights]
        + [pltpu.SemaphoreType.DMA((len(weights),))],
        compiler_params=pltpu.CompilerParams(vmem_limit_bytes=32 * MIB),
        cost_estimate=pl.CostEstimate(
            flops=4 * rows * hidden * width, bytes_accessed=2 * hidden * width, transcendentals=0
        ),
    )(near, far, *weights)


def chip_groups(experts):
    return [list(range(core, experts, 2)) for core in range(2)]


def spread(blocks):
    return lax.all_to_all(
        blocks, "expert", 0, 0, axis_index_groups=chip_groups(lax.axis_size("expert")), tiled=True
    )


def swap(value, axis):
    size = lax.axis_size(axis)
    return lax.ppermute(value, axis, [(i, i ^ 1) for i in range(size)])


def exchange_plan(tokens, norm_gain, routes, route_scale, changed, stale, learner):
    experts = lax.axis_size("expert")
    chips = experts // 2
    row_count, width = tokens.shape[1], tokens.shape[2]
    packed = width + table_width(experts)
    half = chips * row_count
    gain = norm_gain[None]
    blocks_shape = jax.ShapeDtypeStruct((chips, row_count, packed), jnp.bfloat16)
    state_shape = jax.ShapeDtypeStruct((row_count, width), jnp.float32)
    in_vmem = pl.BlockSpec(memory_space=pltpu.VMEM)
    state = tokens[0]
    for step in range(routes.shape[0]):
        if step == 0:
            blocks = pl.pallas_call(
                functools.partial(first_kernel, experts), out_shape=blocks_shape
            )(state, gain, routes[step, 0], route_scale[step, 0])
        else:
            state, blocks = pl.pallas_call(
                functools.partial(next_kernel, experts, changed.shape[1]),
                in_specs=[in_vmem] * 5 + [pl.BlockSpec(memory_space=pltpu.SMEM)],
                out_shape=(state_shape, blocks_shape),
            )(state, returned, gain, routes[step, 0], route_scale[step, 0], changed)
        near = spread(blocks).reshape(half, packed)
        if step == 0:
            near_share, far_share = run_mlp(near, swap(near, "expert"), stale, (False,))
            share = near_share + swap(far_share, "expert").astype(jnp.float32)
        else:
            other = swap(near, "group")
            near_share, far_share = run_mlp(
                near, swap(near, "expert"), stale + learner, (False, True)
            )
            near_away, far_away = run_mlp(other, swap(other, "expert"), learner, (True,))
            away = near_away + swap(far_away, "expert").astype(jnp.float32)
            share = near_share + swap(far_share, "expert").astype(jnp.float32)
            share = share + swap(away.astype(jnp.bfloat16), "group").astype(jnp.float32)
        returned = spread(share.astype(jnp.bfloat16).reshape(chips, row_count, width))
    return pl.pallas_call(
        last_kernel, out_shape=jax.ShapeDtypeStruct((row_count, width), jnp.bfloat16)
    )(state, returned)[None]


def gather_plan(tokens, norm_gain, routes, route_scale, changed, stale, learner):
    experts = lax.axis_size("expert")
    owner_index = lax.axis_index("expert")
    row_count = tokens.shape[1]
    top_count = routes.shape[3]
    capacity = min(row_count, max(2, 2 * row_count * top_count // experts))
    is_fresh = jnp.any(changed[0] == owner_index)
    fresh = [lax.all_gather(part, "group", axis=0, tiled=True) for part in learner]
    newer = [jnp.where(is_fresh, new, old) for new, old in zip(fresh, stale)]
    state = tokens[0].astype(jnp.float32)
    buffer_ids = jnp.arange(experts * capacity, dtype=jnp.int32)
    expert_ids = jnp.arange(experts, dtype=jnp.int32)
    for step in range(routes.shape[0]):
        normed = normalize(state, norm_gain)
        chosen = routes[step, 0]
        weights = route_scale[step, 0]
        hits = (chosen.reshape(-1)[:, None] == expert_ids[None, :]).astype(jnp.int32)
        before = jnp.cumsum(hits, axis=0) - hits
        slot_pos = jnp.sum(before * hits, axis=1).reshape(chosen.shape)
        target = chosen * capacity + slot_pos
        placed = (target[:, :, None] == buffer_ids[None, None, :]).astype(jnp.float32)
        merge_weights = jnp.sum(placed * weights[:, :, None], axis=1)
        send_matrix = jnp.sum(placed, axis=1).astype(jnp.bfloat16)
        outgoing = lax.dot_general(
            send_matrix, normed, (((0,), (0,)), ((), ())), preferred_element_type=jnp.float32
        )
        outgoing = outgoing.astype(jnp.bfloat16).reshape(experts, capacity, -1)
        received = lax.all_to_all(outgoing, "expert", split_axis=0, concat_axis=0, tiled=True)
        flat = received.reshape(-1, received.shape[-1])
        result = expert_apply(flat, *(stale if step == 0 else newer))
        answer = result.astype(jnp.bfloat16).reshape(received.shape)
        returned = lax.all_to_all(answer, "expert", split_axis=0, concat_axis=0, tiled=True)
        flat_back = returned.reshape(experts * capacity, -1).astype(jnp.float32)
        state = state + jnp.dot(merge_weights, flat_back, precision=lax.Precision.HIGHEST)
    return state.astype(jnp.bfloat16)[None]


def local(
    tokens,
    norm_gain,
    routes,
    route_scale,
    changed,
    rollout_up,
    rollout_down,
    learner_up,
    learner_down,
):
    experts = lax.axis_size("expert")
    groups = lax.axis_size("group")
    fewer = tokens.shape[1] * experts < learner_up.shape[1]
    paired = experts % 2 == 0 and groups == 2 and routes.shape[0] == 2
    plan = exchange_plan if fewer and paired else gather_plan
    stale = (rollout_up[0], rollout_down[0])
    learner = (learner_up[0], learner_down[0])
    return plan(tokens, norm_gain, routes, route_scale, changed, stale, learner)


def solution(mesh):
    placed = (
        P("group", "expert", None),
        P(),
        P(None, "group", "expert", None),
        P(None, "group", "expert", None),
        P("group", None),
        P("expert", None, None),
        P("expert", None, None),
        P("expert", "group", None),
        P("expert", "group", None),
    )
    return jax.shard_map(
        local, mesh=mesh, in_specs=placed, out_specs=P("group", "expert", None), check_vma=False
    )
```

```python
import functools
import jax
import jax.numpy as jnp
from jax import lax
from jax.experimental import pallas as pl
from jax.experimental.pallas import tpu as pltpu
from jax.sharding import PartitionSpec as P

LANES = 128
MIB = 1 << 20


def normalize(state, norm_gain):
    scale = lax.rsqrt(jnp.mean(state * state, axis=-1, keepdims=True) + 1e-06)
    return (state * scale * norm_gain).astype(jnp.bfloat16)


def expert_apply(inputs, up_rows, down_rows):
    pre_act = lax.dot_general(
        inputs, up_rows, (((1,), (1,)), ((), ())), preferred_element_type=jnp.float32
    )
    hidden = jax.nn.silu(pre_act).astype(jnp.bfloat16)
    return jnp.dot(hidden, down_rows, preferred_element_type=jnp.float32)


def table_width(experts):
    return -(-6 * experts // LANES) * LANES


def weight_table(experts, chosen, weights, changed):
    shape = (chosen.shape[0], table_width(experts))
    lane = lax.broadcasted_iota(jnp.int32, shape, 1)
    section, expert = lane // experts, lane % experts
    dense = jnp.zeros(shape, jnp.float32)
    for k in range(chosen.shape[1]):
        dense = jnp.where(chosen[:, k : k + 1] == expert, weights[:, k : k + 1], dense)
    fresh = section < 0
    for item in changed:
        fresh = fresh | (expert == item)
    high = dense.astype(jnp.bfloat16).astype(jnp.float32)
    rest = dense - high
    middle = rest.astype(jnp.bfloat16).astype(jnp.float32)
    low = rest - middle
    part = section % 3
    value = jnp.where(part == 0, high, jnp.where(part == 1, middle, low))
    value = jnp.where(fresh, jnp.where(section < 3, 0.0, value), jnp.where(section < 3, value, 0.0))
    return jnp.where(section < 6, value, 0.0).astype(jnp.bfloat16)


def row_weights(experts, table, fresh):
    owner = lax.axis_index("expert")
    lane = lax.broadcasted_iota(jnp.int32, table.shape, 1)
    section = lane // experts
    first = 3 if fresh else 0
    mine = (lane % experts == owner) & (section >= first) & (section < first + 3)
    return jnp.sum(jnp.where(mine, table.astype(jnp.float32), 0.0), axis=1, keepdims=True)


def first_kernel(experts, tokens, gain, routes, scales, out):
    width = tokens.shape[1]
    normed = normalize(tokens[...].astype(jnp.float32), gain[...])
    table = weight_table(experts, routes[0, 0], scales[0, 0], [])
    for j in range(out.shape[0]):
        out[j, :, :width] = normed
        out[j, :, width:] = table


def next_kernel(experts, step, previous, returned, gain, routes, scales, changed, state_out, out):
    width = previous.shape[1]
    state = previous[...].astype(jnp.float32) + jnp.sum(returned[...].astype(jnp.float32), axis=0)
    state_out[...] = state
    normed = normalize(state, gain[...])
    items = [changed[0, i] for i in range(changed.shape[1])]
    table = weight_table(experts, routes[step, 0], scales[step, 0], items)
    for j in range(out.shape[0]):
        out[j, :, :width] = normed
        out[j, :, width:] = table


def last_kernel(previous, returned, out):
    state = previous[...] + jnp.sum(returned[...].astype(jnp.float32), axis=0)
    out[...] = state.astype(jnp.bfloat16)


def mlp_kernel(experts, fresh_flags, chunks, near, far, *refs):
    count = len(fresh_flags)
    sources = refs[: 2 * count]
    near_out, far_out = refs[2 * count : 2 * count + 2]
    buffers = refs[2 * count + 2 : 4 * count + 2]
    sems = refs[4 * count + 2]

    def copy(i, c):
        size = sources[i].shape[0] // chunks[i]
        part = pl.ds(c * size, size)
        return pltpu.make_async_copy(sources[i].at[part], buffers[i].at[part], sems.at[i, c])

    for i in range(2 * count):
        for c in range(chunks[i]):
            copy(i, c).start()
    half, width = near_out.shape
    inputs = jnp.concatenate([near[:, :width], far[:, :width]], axis=0)
    table = jnp.concatenate([near[:, width:], far[:, width:]], axis=0)
    total = None
    for i, fresh in enumerate(fresh_flags):
        scale = row_weights(experts, table, fresh)
        hidden = []
        size = sources[2 * i].shape[0] // chunks[2 * i]
        for c in range(chunks[2 * i]):
            copy(2 * i, c).wait()
            pre_act = lax.dot_general(
                inputs,
                buffers[2 * i][c * size : (c + 1) * size],
                (((1,), (1,)), ((), ())),
                preferred_element_type=jnp.float32,
            )
            hidden.append((pre_act / (1.0 + jnp.exp(-pre_act))).astype(jnp.bfloat16))
        hidden = jnp.concatenate(hidden, axis=1)
        for c in range(chunks[2 * i + 1]):
            copy(2 * i + 1, c).wait()
        result = jnp.dot(hidden, buffers[2 * i + 1][...], preferred_element_type=jnp.float32)
        result = result * scale
        total = result if total is None else total + result
    near_out[...] = total[:half]
    far_out[...] = total[half:].astype(jnp.bfloat16)


def run_mlp(near, far, weights, fresh_flags):
    experts = lax.axis_size("expert")
    rows, width = near.shape[0], weights[0].shape[1]
    hidden = sum(part.shape[0] for part in weights) // 2
    chunks = [max(1, part.shape[0] // 384) if i % 2 == 0 else 1 for i, part in enumerate(weights)]
    in_vmem = pl.BlockSpec(memory_space=pltpu.VMEM)
    return pl.pallas_call(
        functools.partial(mlp_kernel, experts, fresh_flags, chunks),
        out_shape=(
            jax.ShapeDtypeStruct((rows, width), jnp.float32),
            jax.ShapeDtypeStruct((rows, width), jnp.bfloat16),
        ),
        in_specs=[in_vmem] * 2 + [pl.BlockSpec(memory_space=pl.ANY)] * len(weights),
        out_specs=(in_vmem, in_vmem),
        scratch_shapes=[pltpu.VMEM(part.shape, part.dtype) for part in weights]
        + [pltpu.SemaphoreType.DMA((len(weights), max(chunks)))],
        compiler_params=pltpu.CompilerParams(vmem_limit_bytes=20 * MIB),
        cost_estimate=pl.CostEstimate(
            flops=8 * rows * hidden * width, bytes_accessed=4 * hidden * width, transcendentals=0
        ),
    )(near, far, *weights)


def chip_groups(experts):
    return [list(range(core, experts, 2)) for core in range(2)]


def spread(blocks):
    return lax.all_to_all(
        blocks, "expert", 0, 0, axis_index_groups=chip_groups(lax.axis_size("expert")), tiled=True
    )


def swap(value, axis):
    size = lax.axis_size(axis)
    return lax.ppermute(value, axis, [(i, i ^ 1) for i in range(size)])


def exchange_plan(tokens, norm_gain, routes, route_scale, changed, stale, learner):
    experts = lax.axis_size("expert")
    chips = experts // 2
    row_count, width = tokens.shape[1], tokens.shape[2]
    packed = width + table_width(experts)
    half = chips * row_count
    gain = norm_gain[None]
    blocks_shape = jax.ShapeDtypeStruct((chips, row_count, packed), jnp.bfloat16)
    state_shape = jax.ShapeDtypeStruct((row_count, width), jnp.float32)
    in_vmem = pl.BlockSpec(memory_space=pltpu.VMEM)
    in_smem = pl.BlockSpec(memory_space=pltpu.SMEM)
    small = pltpu.CompilerParams(vmem_limit_bytes=4 * MIB)
    weight_bytes = 2 * sum(part.size for part in stale + learner)
    long = pl.CostEstimate(
        flops=640 * weight_bytes, bytes_accessed=2 * weight_bytes, transcendentals=0
    )
    state = tokens[0]
    for step in range(routes.shape[0]):
        if step == 0:
            blocks = pl.pallas_call(
                functools.partial(first_kernel, experts),
                in_specs=[in_vmem] * 4,
                out_specs=in_vmem,
                out_shape=blocks_shape,
                compiler_params=small,
                cost_estimate=long,
            )(state, gain, routes, route_scale)
        else:
            state, blocks = pl.pallas_call(
                functools.partial(next_kernel, experts, step),
                in_specs=[in_vmem] * 5 + [in_smem],
                out_specs=(in_vmem, in_vmem),
                out_shape=(state_shape, blocks_shape),
                compiler_params=small,
                cost_estimate=long,
            )(state, returned, gain, routes, route_scale, changed)
        near = spread(blocks).reshape(half, packed)
        far = swap(near, "expert")
        if step == 0:
            near_share, far_share = run_mlp(near, far, stale, (False,))
            share = near_share + swap(far_share, "expert").astype(jnp.float32)
        else:
            other = swap(near, "group")
            near_share, far_share = run_mlp(near, far, stale + learner, (False, True))
            other, far_share = lax.optimization_barrier((other, far_share))
            near_away, far_away = run_mlp(other, swap(other, "expert"), learner, (True,))
            away = near_away + swap(far_away, "expert").astype(jnp.float32)
            share = near_share + swap(far_share, "expert").astype(jnp.float32)
            share = share + swap(away.astype(jnp.bfloat16), "group").astype(jnp.float32)
        returned = spread(share.astype(jnp.bfloat16).reshape(chips, row_count, width))
    return pl.pallas_call(
        last_kernel,
        in_specs=[in_vmem] * 2,
        out_specs=in_vmem,
        out_shape=jax.ShapeDtypeStruct((row_count, width), jnp.bfloat16),
        compiler_params=small,
    )(state, returned)[None]


def gather_plan(tokens, norm_gain, routes, route_scale, changed, stale, learner):
    experts = lax.axis_size("expert")
    owner_index = lax.axis_index("expert")
    row_count = tokens.shape[1]
    top_count = routes.shape[3]
    capacity = min(row_count, max(2, 2 * row_count * top_count // experts))
    is_fresh = jnp.any(changed[0] == owner_index)
    fresh = [lax.all_gather(part, "group", axis=0, tiled=True) for part in learner]
    newer = [jnp.where(is_fresh, new, old) for new, old in zip(fresh, stale)]
    state = tokens[0].astype(jnp.float32)
    buffer_ids = jnp.arange(experts * capacity, dtype=jnp.int32)
    expert_ids = jnp.arange(experts, dtype=jnp.int32)
    for step in range(routes.shape[0]):
        normed = normalize(state, norm_gain)
        chosen = routes[step, 0]
        weights = route_scale[step, 0]
        hits = (chosen.reshape(-1)[:, None] == expert_ids[None, :]).astype(jnp.int32)
        before = jnp.cumsum(hits, axis=0) - hits
        slot_pos = jnp.sum(before * hits, axis=1).reshape(chosen.shape)
        target = chosen * capacity + slot_pos
        placed = (target[:, :, None] == buffer_ids[None, None, :]).astype(jnp.float32)
        merge_weights = jnp.sum(placed * weights[:, :, None], axis=1)
        send_matrix = jnp.sum(placed, axis=1).astype(jnp.bfloat16)
        outgoing = lax.dot_general(
            send_matrix, normed, (((0,), (0,)), ((), ())), preferred_element_type=jnp.float32
        )
        outgoing = outgoing.astype(jnp.bfloat16).reshape(experts, capacity, -1)
        received = lax.all_to_all(outgoing, "expert", split_axis=0, concat_axis=0, tiled=True)
        flat = received.reshape(-1, received.shape[-1])
        result = expert_apply(flat, *(stale if step == 0 else newer))
        answer = result.astype(jnp.bfloat16).reshape(received.shape)
        returned = lax.all_to_all(answer, "expert", split_axis=0, concat_axis=0, tiled=True)
        flat_back = returned.reshape(experts * capacity, -1).astype(jnp.float32)
        state = state + jnp.dot(merge_weights, flat_back, precision=lax.Precision.HIGHEST)
    return state.astype(jnp.bfloat16)[None]


def local(
    tokens,
    norm_gain,
    routes,
    route_scale,
    changed,
    rollout_up,
    rollout_down,
    learner_up,
    learner_down,
):
    experts = lax.axis_size("expert")
    groups = lax.axis_size("group")
    fewer = tokens.shape[1] * experts < learner_up.shape[1]
    paired = experts % 2 == 0 and groups == 2 and routes.shape[0] == 2
    plan = exchange_plan if fewer and paired else gather_plan
    stale = (rollout_up[0], rollout_down[0])
    learner = (learner_up[0], learner_down[0])
    return plan(tokens, norm_gain, routes, route_scale, changed, stale, learner)


def solution(mesh):
    placed = (
        P("group", "expert", None),
        P(),
        P(None, "group", "expert", None),
        P(None, "group", "expert", None),
        P("group", None),
        P("expert", None, None),
        P("expert", None, None),
        P("expert", "group", None),
        P("expert", "group", None),
    )
    return jax.shard_map(
        local, mesh=mesh, in_specs=placed, out_specs=P("group", "expert", None), check_vma=False
    )
```

```python
import functools
import jax
import jax.numpy as jnp
from jax import lax
from jax.experimental import pallas as pl
from jax.experimental.pallas import tpu as pltpu
from jax.sharding import PartitionSpec as P

LANES = 128
MIB = 1 << 20


def normalize(state, norm_gain):
    scale = lax.rsqrt(jnp.mean(state * state, axis=-1, keepdims=True) + 1e-06)
    return (state * scale * norm_gain).astype(jnp.bfloat16)


def expert_apply(inputs, up_rows, down_rows):
    pre_act = lax.dot_general(
        inputs, up_rows, (((1,), (1,)), ((), ())), preferred_element_type=jnp.float32
    )
    hidden = jax.nn.silu(pre_act).astype(jnp.bfloat16)
    return jnp.dot(hidden, down_rows, preferred_element_type=jnp.float32)


def table_width(experts):
    return -(-6 * experts // LANES) * LANES


def weight_table(experts, chosen, weights, changed):
    shape = (chosen.shape[0], table_width(experts))
    lane = lax.broadcasted_iota(jnp.int32, shape, 1)
    section, expert = lane // experts, lane % experts
    dense = jnp.zeros(shape, jnp.float32)
    for k in range(chosen.shape[1]):
        dense = jnp.where(chosen[:, k : k + 1] == expert, weights[:, k : k + 1], dense)
    fresh = section < 0
    for item in changed:
        fresh = fresh | (expert == item)
    high = dense.astype(jnp.bfloat16).astype(jnp.float32)
    rest = dense - high
    middle = rest.astype(jnp.bfloat16).astype(jnp.float32)
    low = rest - middle
    part = section % 3
    value = jnp.where(part == 0, high, jnp.where(part == 1, middle, low))
    value = jnp.where(fresh, jnp.where(section < 3, 0.0, value), jnp.where(section < 3, value, 0.0))
    return jnp.where(section < 6, value, 0.0).astype(jnp.bfloat16)


def row_weights(experts, table, fresh):
    owner = lax.axis_index("expert")
    lane = lax.broadcasted_iota(jnp.int32, table.shape, 1)
    section = lane // experts
    first = 3 if fresh else 0
    mine = (lane % experts == owner) & (section >= first) & (section < first + 3)
    return jnp.sum(jnp.where(mine, table.astype(jnp.float32), 0.0), axis=1, keepdims=True)


def first_kernel(tokens, out):
    state = tokens[...].astype(jnp.float32)
    out[...] = state * lax.rsqrt(jnp.mean(state * state, axis=-1, keepdims=True) + 1e-06)


def pack_kernel(experts, scaled, gain, routes, scales, out):
    width = scaled.shape[1]
    normed = (scaled[...] * gain[...]).astype(jnp.bfloat16)
    table = weight_table(experts, routes[0, 0], scales[0, 0], [])
    for j in range(out.shape[0]):
        out[j, :, :width] = normed
        out[j, :, width:] = table


def next_kernel(experts, step, previous, returned, gain, routes, scales, changed, state_out, out):
    width = previous.shape[1]
    state = previous[...].astype(jnp.float32) + jnp.sum(returned[...].astype(jnp.float32), axis=0)
    state_out[...] = state
    normed = normalize(state, gain[...])
    items = [changed[0, i] for i in range(changed.shape[1])]
    table = weight_table(experts, routes[step, 0], scales[step, 0], items)
    for j in range(out.shape[0]):
        out[j, :, :width] = normed
        out[j, :, width:] = table


def last_kernel(previous, returned, out):
    state = previous[...] + jnp.sum(returned[...].astype(jnp.float32), axis=0)
    out[...] = state.astype(jnp.bfloat16)


def mlp_kernel(experts, fresh_flags, near, far, *refs):
    near_out, far_out = refs[-2:]
    half, width = near_out.shape
    inputs = jnp.concatenate([near[:, :width], far[:, :width]], axis=0)
    table = jnp.concatenate([near[:, width:], far[:, width:]], axis=0)
    total = None
    for i, fresh in enumerate(fresh_flags):
        up, down = refs[2 * i : 2 * i + 2]
        pre_act = lax.dot_general(
            inputs, up[...], (((1,), (1,)), ((), ())), preferred_element_type=jnp.float32
        )
        hidden = (pre_act / (1.0 + jnp.exp(-pre_act))).astype(jnp.bfloat16)
        result = jnp.dot(hidden, down[...], preferred_element_type=jnp.float32)
        result = result * row_weights(experts, table, fresh)
        total = result if total is None else total + result
    near_out[...] = total[:half]
    far_out[...] = total[half:].astype(jnp.bfloat16)


def run_mlp(near, far, weights, fresh_flags):
    experts = lax.axis_size("expert")
    rows, width = near.shape[0], weights[0].shape[1]
    hidden = sum(part.shape[0] for part in weights) // 2
    in_vmem = pl.BlockSpec(memory_space=pltpu.VMEM)
    return pl.pallas_call(
        functools.partial(mlp_kernel, experts, fresh_flags),
        out_shape=(
            jax.ShapeDtypeStruct((rows, width), jnp.float32),
            jax.ShapeDtypeStruct((rows, width), jnp.bfloat16),
        ),
        in_specs=[in_vmem] * (2 + len(weights)),
        out_specs=(in_vmem, in_vmem),
        compiler_params=pltpu.CompilerParams(vmem_limit_bytes=20 * MIB),
        cost_estimate=pl.CostEstimate(
            flops=8 * rows * hidden * width, bytes_accessed=4 * hidden * width, transcendentals=0
        ),
    )(near, far, *weights)


def chip_groups(experts):
    return [list(range(core, experts, 2)) for core in range(2)]


def spread(blocks):
    return lax.all_to_all(
        blocks, "expert", 0, 0, axis_index_groups=chip_groups(lax.axis_size("expert")), tiled=True
    )


def swap(value, axis):
    size = lax.axis_size(axis)
    return lax.ppermute(value, axis, [(i, i ^ 1) for i in range(size)])


def exchange_plan(tokens, norm_gain, routes, route_scale, changed, stale, learner):
    experts = lax.axis_size("expert")
    chips = experts // 2
    row_count, width = tokens.shape[1], tokens.shape[2]
    packed = width + table_width(experts)
    half = chips * row_count
    gain = norm_gain[None]
    blocks_shape = jax.ShapeDtypeStruct((chips, row_count, packed), jnp.bfloat16)
    state_shape = jax.ShapeDtypeStruct((row_count, width), jnp.float32)
    in_vmem = pl.BlockSpec(memory_space=pltpu.VMEM)
    in_smem = pl.BlockSpec(memory_space=pltpu.SMEM)
    small = pltpu.CompilerParams(vmem_limit_bytes=4 * MIB)
    weight_bytes = 2 * sum(part.size for part in stale + learner)
    long = pl.CostEstimate(
        flops=640 * weight_bytes, bytes_accessed=2 * weight_bytes, transcendentals=0
    )
    state = tokens[0]
    for step in range(routes.shape[0]):
        if step == 0:
            scaled = pl.pallas_call(
                first_kernel,
                in_specs=[in_vmem],
                out_specs=in_vmem,
                out_shape=state_shape,
                compiler_params=small,
                cost_estimate=long,
            )(state)
            blocks = pl.pallas_call(
                functools.partial(pack_kernel, experts),
                in_specs=[in_vmem] * 4,
                out_specs=in_vmem,
                out_shape=blocks_shape,
                compiler_params=small,
            )(scaled, gain, routes, route_scale)
        else:
            state, blocks = pl.pallas_call(
                functools.partial(next_kernel, experts, step),
                in_specs=[in_vmem] * 5 + [in_smem],
                out_specs=(in_vmem, in_vmem),
                out_shape=(state_shape, blocks_shape),
                compiler_params=small,
                cost_estimate=long,
            )(state, returned, gain, routes, route_scale, changed)
        near = spread(blocks).reshape(half, packed)
        far = swap(near, "expert")
        if step == 0:
            near_share, far_share = run_mlp(near, far, stale, (False,))
            share = near_share + swap(far_share, "expert").astype(jnp.float32)
        else:
            other = swap(near, "group")
            near_share, far_share = run_mlp(near, far, stale + learner, (False, True))
            other, far_share = lax.optimization_barrier((other, far_share))
            near_away, far_away = run_mlp(other, swap(other, "expert"), learner, (True,))
            away = near_away + swap(far_away, "expert").astype(jnp.float32)
            share = near_share + swap(far_share, "expert").astype(jnp.float32)
            share = share + swap(away.astype(jnp.bfloat16), "group").astype(jnp.float32)
        returned = spread(share.astype(jnp.bfloat16).reshape(chips, row_count, width))
    return pl.pallas_call(
        last_kernel,
        in_specs=[in_vmem] * 2,
        out_specs=in_vmem,
        out_shape=jax.ShapeDtypeStruct((row_count, width), jnp.bfloat16),
        compiler_params=small,
    )(state, returned)[None]


def gather_plan(tokens, norm_gain, routes, route_scale, changed, stale, learner):
    experts = lax.axis_size("expert")
    owner_index = lax.axis_index("expert")
    row_count = tokens.shape[1]
    top_count = routes.shape[3]
    capacity = min(row_count, max(2, 2 * row_count * top_count // experts))
    is_fresh = jnp.any(changed[0] == owner_index)
    fresh = [lax.all_gather(part, "group", axis=0, tiled=True) for part in learner]
    newer = [jnp.where(is_fresh, new, old) for new, old in zip(fresh, stale)]
    state = tokens[0].astype(jnp.float32)
    buffer_ids = jnp.arange(experts * capacity, dtype=jnp.int32)
    expert_ids = jnp.arange(experts, dtype=jnp.int32)
    for step in range(routes.shape[0]):
        normed = normalize(state, norm_gain)
        chosen = routes[step, 0]
        weights = route_scale[step, 0]
        hits = (chosen.reshape(-1)[:, None] == expert_ids[None, :]).astype(jnp.int32)
        before = jnp.cumsum(hits, axis=0) - hits
        slot_pos = jnp.sum(before * hits, axis=1).reshape(chosen.shape)
        target = chosen * capacity + slot_pos
        placed = (target[:, :, None] == buffer_ids[None, None, :]).astype(jnp.float32)
        merge_weights = jnp.sum(placed * weights[:, :, None], axis=1)
        send_matrix = jnp.sum(placed, axis=1).astype(jnp.bfloat16)
        outgoing = lax.dot_general(
            send_matrix, normed, (((0,), (0,)), ((), ())), preferred_element_type=jnp.float32
        )
        outgoing = outgoing.astype(jnp.bfloat16).reshape(experts, capacity, -1)
        received = lax.all_to_all(outgoing, "expert", split_axis=0, concat_axis=0, tiled=True)
        flat = received.reshape(-1, received.shape[-1])
        result = expert_apply(flat, *(stale if step == 0 else newer))
        answer = result.astype(jnp.bfloat16).reshape(received.shape)
        returned = lax.all_to_all(answer, "expert", split_axis=0, concat_axis=0, tiled=True)
        flat_back = returned.reshape(experts * capacity, -1).astype(jnp.float32)
        state = state + jnp.dot(merge_weights, flat_back, precision=lax.Precision.HIGHEST)
    return state.astype(jnp.bfloat16)[None]


def local(
    tokens,
    norm_gain,
    routes,
    route_scale,
    changed,
    rollout_up,
    rollout_down,
    learner_up,
    learner_down,
):
    experts = lax.axis_size("expert")
    groups = lax.axis_size("group")
    fewer = tokens.shape[1] * experts < learner_up.shape[1]
    paired = experts % 2 == 0 and groups == 2 and routes.shape[0] == 2
    plan = exchange_plan if fewer and paired else gather_plan
    stale = (rollout_up[0], rollout_down[0])
    learner = (learner_up[0], learner_down[0])
    return plan(tokens, norm_gain, routes, route_scale, changed, stale, learner)


def solution(mesh):
    placed = (
        P("group", "expert", None),
        P(),
        P(None, "group", "expert", None),
        P(None, "group", "expert", None),
        P("group", None),
        P("expert", None, None),
        P("expert", None, None),
        P("expert", "group", None),
        P("expert", "group", None),
    )
    return jax.shard_map(
        local, mesh=mesh, in_specs=placed, out_specs=P("group", "expert", None), check_vma=False
    )
```

```python
import functools
import jax
import jax.numpy as jnp
from jax import lax
from jax.experimental import pallas as pl
from jax.experimental.pallas import tpu as pltpu
from jax.sharding import PartitionSpec as P

LANES = 128
MIB = 1 << 20


def normalize(state, norm_gain):
    scale = lax.rsqrt(jnp.mean(state * state, axis=-1, keepdims=True) + 1e-06)
    return (state * scale * norm_gain).astype(jnp.bfloat16)


def expert_apply(inputs, up_rows, down_rows):
    pre_act = lax.dot_general(
        inputs, up_rows, (((1,), (1,)), ((), ())), preferred_element_type=jnp.float32
    )
    hidden = jax.nn.silu(pre_act).astype(jnp.bfloat16)
    return jnp.dot(hidden, down_rows, preferred_element_type=jnp.float32)


def table_width(experts):
    return -(-6 * experts // LANES) * LANES


def weight_table(experts, chosen, weights, changed):
    shape = (chosen.shape[0], table_width(experts))
    lane = lax.broadcasted_iota(jnp.int32, shape, 1)
    section, expert = lane // experts, lane % experts
    dense = jnp.zeros(shape, jnp.float32)
    for k in range(chosen.shape[1]):
        dense = jnp.where(chosen[:, k : k + 1] == expert, weights[:, k : k + 1], dense)
    fresh = section < 0
    for item in changed:
        fresh = fresh | (expert == item)
    high = dense.astype(jnp.bfloat16).astype(jnp.float32)
    rest = dense - high
    middle = rest.astype(jnp.bfloat16).astype(jnp.float32)
    low = rest - middle
    part = section % 3
    value = jnp.where(part == 0, high, jnp.where(part == 1, middle, low))
    value = jnp.where(fresh, jnp.where(section < 3, 0.0, value), jnp.where(section < 3, value, 0.0))
    return jnp.where(section < 6, value, 0.0).astype(jnp.bfloat16)


def row_weights(experts, table, fresh):
    owner = lax.axis_index("expert")
    lane = lax.broadcasted_iota(jnp.int32, table.shape, 1)
    section = lane // experts
    first = 3 if fresh else 0
    mine = (lane % experts == owner) & (section >= first) & (section < first + 3)
    return jnp.sum(jnp.where(mine, table.astype(jnp.float32), 0.0), axis=1, keepdims=True)


def first_kernel(tokens, out):
    state = tokens[...].astype(jnp.float32)
    out[...] = state * lax.rsqrt(jnp.mean(state * state, axis=-1, keepdims=True) + 1e-06)


def pack_kernel(experts, scaled, gain, routes, scales, out):
    width = scaled.shape[1]
    normed = (scaled[...] * gain[...]).astype(jnp.bfloat16)
    table = weight_table(experts, routes[0, 0], scales[0, 0], [])
    out[:, :width] = normed
    out[:, width:] = table


def next_kernel(experts, step, previous, returned, gain, routes, scales, changed, state_out, out):
    width = previous.shape[1]
    state = previous[...].astype(jnp.float32) + jnp.sum(returned[...].astype(jnp.float32), axis=0)
    state_out[...] = state
    normed = normalize(state, gain[...])
    items = [changed[0, i] for i in range(changed.shape[1])]
    table = weight_table(experts, routes[step, 0], scales[step, 0], items)
    out[:, :width] = normed
    out[:, width:] = table


def last_kernel(previous, returned, out):
    state = previous[...] + jnp.sum(returned[...].astype(jnp.float32), axis=0)
    out[...] = state.astype(jnp.bfloat16)


def mlp_kernel(experts, fresh_flags, near, far, *refs):
    near_out, far_out = refs[-2:]
    half, width = near_out.shape
    inputs = jnp.concatenate([near[:, :width], far[:, :width]], axis=0)
    table = jnp.concatenate([near[:, width:], far[:, width:]], axis=0)
    total = None
    for i, fresh in enumerate(fresh_flags):
        up, down = refs[2 * i : 2 * i + 2]
        pre_act = lax.dot_general(
            inputs, up[...], (((1,), (1,)), ((), ())), preferred_element_type=jnp.float32
        )
        hidden = (pre_act / (1.0 + jnp.exp(-pre_act))).astype(jnp.bfloat16)
        result = jnp.dot(hidden, down[...], preferred_element_type=jnp.float32)
        result = result * row_weights(experts, table, fresh)
        total = result if total is None else total + result
    near_out[...] = total[:half]
    far_out[...] = total[half:].astype(jnp.bfloat16)


def run_mlp(near, far, weights, fresh_flags):
    experts = lax.axis_size("expert")
    rows, width = near.shape[0], weights[0].shape[1]
    hidden = sum(part.shape[0] for part in weights) // 2
    in_vmem = pl.BlockSpec(memory_space=pltpu.VMEM)
    return pl.pallas_call(
        functools.partial(mlp_kernel, experts, fresh_flags),
        out_shape=(
            jax.ShapeDtypeStruct((rows, width), jnp.float32),
            jax.ShapeDtypeStruct((rows, width), jnp.bfloat16),
        ),
        in_specs=[in_vmem] * (2 + len(weights)),
        out_specs=(in_vmem, in_vmem),
        compiler_params=pltpu.CompilerParams(vmem_limit_bytes=20 * MIB),
        cost_estimate=pl.CostEstimate(
            flops=8 * rows * hidden * width, bytes_accessed=4 * hidden * width, transcendentals=0
        ),
    )(near, far, *weights)


def chip_groups(experts):
    return [list(range(core, experts, 2)) for core in range(2)]


def spread(blocks):
    return lax.all_to_all(
        blocks, "expert", 0, 0, axis_index_groups=chip_groups(lax.axis_size("expert")), tiled=True
    )


def gather(block):
    return lax.all_gather(
        block, "expert", axis_index_groups=chip_groups(lax.axis_size("expert")), tiled=True
    )


def swap(value, axis):
    size = lax.axis_size(axis)
    return lax.ppermute(value, axis, [(i, i ^ 1) for i in range(size)])


def exchange_plan(tokens, norm_gain, routes, route_scale, changed, stale, learner):
    experts = lax.axis_size("expert")
    chips = experts // 2
    row_count, width = tokens.shape[1], tokens.shape[2]
    packed = width + table_width(experts)
    gain = norm_gain[None]
    block_shape = jax.ShapeDtypeStruct((row_count, packed), jnp.bfloat16)
    state_shape = jax.ShapeDtypeStruct((row_count, width), jnp.float32)
    in_vmem = pl.BlockSpec(memory_space=pltpu.VMEM)
    in_smem = pl.BlockSpec(memory_space=pltpu.SMEM)
    small = pltpu.CompilerParams(vmem_limit_bytes=4 * MIB)
    weight_bytes = 2 * sum(part.size for part in stale + learner)
    long = pl.CostEstimate(
        flops=640 * weight_bytes, bytes_accessed=2 * weight_bytes, transcendentals=0
    )
    state = tokens[0]
    for step in range(routes.shape[0]):
        if step == 0:
            scaled = pl.pallas_call(
                first_kernel,
                in_specs=[in_vmem],
                out_specs=in_vmem,
                out_shape=state_shape,
                compiler_params=small,
                cost_estimate=long,
            )(state)
            block = pl.pallas_call(
                functools.partial(pack_kernel, experts),
                in_specs=[in_vmem] * 4,
                out_specs=in_vmem,
                out_shape=block_shape,
                compiler_params=small,
            )(scaled, gain, routes, route_scale)
        else:
            state, block = pl.pallas_call(
                functools.partial(next_kernel, experts, step),
                in_specs=[in_vmem] * 5 + [in_smem],
                out_specs=(in_vmem, in_vmem),
                out_shape=(state_shape, block_shape),
                compiler_params=small,
                cost_estimate=long,
            )(state, returned, gain, routes, route_scale, changed)
        near = gather(block)
        far = swap(near, "expert")
        if step == 0:
            near_share, far_share = run_mlp(near, far, stale, (False,))
            share = near_share + swap(far_share, "expert").astype(jnp.float32)
        else:
            other = swap(near, "group")
            near_share, far_share = run_mlp(near, far, stale + learner, (False, True))
            other, far_share = lax.optimization_barrier((other, far_share))
            near_away, far_away = run_mlp(other, swap(other, "expert"), learner, (True,))
            away = near_away + swap(far_away, "expert").astype(jnp.float32)
            share = near_share + swap(far_share, "expert").astype(jnp.float32)
            share = share + swap(away.astype(jnp.bfloat16), "group").astype(jnp.float32)
        returned = spread(share.astype(jnp.bfloat16).reshape(chips, row_count, width))
    return pl.pallas_call(
        last_kernel,
        in_specs=[in_vmem] * 2,
        out_specs=in_vmem,
        out_shape=jax.ShapeDtypeStruct((row_count, width), jnp.bfloat16),
        compiler_params=small,
    )(state, returned)[None]


def gather_plan(tokens, norm_gain, routes, route_scale, changed, stale, learner):
    experts = lax.axis_size("expert")
    owner_index = lax.axis_index("expert")
    row_count = tokens.shape[1]
    top_count = routes.shape[3]
    capacity = min(row_count, max(2, 2 * row_count * top_count // experts))
    is_fresh = jnp.any(changed[0] == owner_index)
    fresh = [lax.all_gather(part, "group", axis=0, tiled=True) for part in learner]
    newer = [jnp.where(is_fresh, new, old) for new, old in zip(fresh, stale)]
    state = tokens[0].astype(jnp.float32)
    buffer_ids = jnp.arange(experts * capacity, dtype=jnp.int32)
    expert_ids = jnp.arange(experts, dtype=jnp.int32)
    for step in range(routes.shape[0]):
        normed = normalize(state, norm_gain)
        chosen = routes[step, 0]
        weights = route_scale[step, 0]
        hits = (chosen.reshape(-1)[:, None] == expert_ids[None, :]).astype(jnp.int32)
        before = jnp.cumsum(hits, axis=0) - hits
        slot_pos = jnp.sum(before * hits, axis=1).reshape(chosen.shape)
        target = chosen * capacity + slot_pos
        placed = (target[:, :, None] == buffer_ids[None, None, :]).astype(jnp.float32)
        merge_weights = jnp.sum(placed * weights[:, :, None], axis=1)
        send_matrix = jnp.sum(placed, axis=1).astype(jnp.bfloat16)
        outgoing = lax.dot_general(
            send_matrix, normed, (((0,), (0,)), ((), ())), preferred_element_type=jnp.float32
        )
        outgoing = outgoing.astype(jnp.bfloat16).reshape(experts, capacity, -1)
        received = lax.all_to_all(outgoing, "expert", split_axis=0, concat_axis=0, tiled=True)
        flat = received.reshape(-1, received.shape[-1])
        result = expert_apply(flat, *(stale if step == 0 else newer))
        answer = result.astype(jnp.bfloat16).reshape(received.shape)
        returned = lax.all_to_all(answer, "expert", split_axis=0, concat_axis=0, tiled=True)
        flat_back = returned.reshape(experts * capacity, -1).astype(jnp.float32)
        state = state + jnp.dot(merge_weights, flat_back, precision=lax.Precision.HIGHEST)
    return state.astype(jnp.bfloat16)[None]


def local(
    tokens,
    norm_gain,
    routes,
    route_scale,
    changed,
    rollout_up,
    rollout_down,
    learner_up,
    learner_down,
):
    experts = lax.axis_size("expert")
    groups = lax.axis_size("group")
    fewer = tokens.shape[1] * experts < learner_up.shape[1]
    paired = experts % 2 == 0 and groups == 2 and routes.shape[0] == 2
    plan = exchange_plan if fewer and paired else gather_plan
    stale = (rollout_up[0], rollout_down[0])
    learner = (learner_up[0], learner_down[0])
    return plan(tokens, norm_gain, routes, route_scale, changed, stale, learner)


def solution(mesh):
    placed = (
        P("group", "expert", None),
        P(),
        P(None, "group", "expert", None),
        P(None, "group", "expert", None),
        P("group", None),
        P("expert", None, None),
        P("expert", None, None),
        P("expert", "group", None),
        P("expert", "group", None),
    )
    return jax.shard_map(
        local, mesh=mesh, in_specs=placed, out_specs=P("group", "expert", None), check_vma=False
    )
```

```python
import functools
import jax
import jax.numpy as jnp
from jax import lax
from jax.experimental import pallas as pl
from jax.experimental.pallas import tpu as pltpu
from jax.sharding import PartitionSpec as P

LANES = 128
MIB = 1 << 20


def normalize(state, norm_gain):
    scale = lax.rsqrt(jnp.mean(state * state, axis=-1, keepdims=True) + 1e-06)
    return (state * scale * norm_gain).astype(jnp.bfloat16)


def expert_apply(inputs, up_rows, down_rows):
    pre_act = lax.dot_general(
        inputs, up_rows, (((1,), (1,)), ((), ())), preferred_element_type=jnp.float32
    )
    hidden = jax.nn.silu(pre_act).astype(jnp.bfloat16)
    return jnp.dot(hidden, down_rows, preferred_element_type=jnp.float32)


def table_width(experts):
    return -(-6 * experts // LANES) * LANES


def weight_table(experts, chosen, weights, changed):
    shape = (chosen.shape[0], table_width(experts))
    lane = lax.broadcasted_iota(jnp.int32, shape, 1)
    section, expert = lane // experts, lane % experts
    dense = jnp.zeros(shape, jnp.float32)
    for k in range(chosen.shape[1]):
        dense = jnp.where(chosen[:, k : k + 1] == expert, weights[:, k : k + 1], dense)
    fresh = section < 0
    for item in changed:
        fresh = fresh | (expert == item)
    high = dense.astype(jnp.bfloat16).astype(jnp.float32)
    rest = dense - high
    middle = rest.astype(jnp.bfloat16).astype(jnp.float32)
    low = rest - middle
    part = section % 3
    value = jnp.where(part == 0, high, jnp.where(part == 1, middle, low))
    value = jnp.where(fresh, jnp.where(section < 3, 0.0, value), jnp.where(section < 3, value, 0.0))
    return jnp.where(section < 6, value, 0.0).astype(jnp.bfloat16)


def row_weights(experts, table, owner, fresh):
    lane = lax.broadcasted_iota(jnp.int32, table.shape, 1)
    section = lane // experts
    first = 3 if fresh else 0
    mine = (lane % experts == owner) & (section >= first) & (section < first + 3)
    return jnp.sum(jnp.where(mine, table.astype(jnp.float32), 0.0), axis=1, keepdims=True)


def first_kernel(tokens, out):
    state = tokens[...].astype(jnp.float32)
    out[...] = state * lax.rsqrt(jnp.mean(state * state, axis=-1, keepdims=True) + 1e-06)


def pack_kernel(experts, scaled, gain, routes, scales, out):
    width = scaled.shape[1]
    normed = (scaled[...] * gain[...]).astype(jnp.bfloat16)
    table = weight_table(experts, routes[0, 0], scales[0, 0], [])
    for j in range(out.shape[0]):
        out[j, :, :width] = normed
        out[j, :, width:] = table


def next_kernel(experts, step, previous, returned, gain, routes, scales, changed, state_out, out):
    width = previous.shape[1]
    state = previous[...].astype(jnp.float32) + jnp.sum(returned[...].astype(jnp.float32), axis=0)
    state_out[...] = state
    normed = normalize(state, gain[...])
    items = [changed[0, i] for i in range(changed.shape[1])]
    table = weight_table(experts, routes[step, 0], scales[step, 0], items)
    for j in range(out.shape[0]):
        out[j, :, :width] = normed
        out[j, :, width:] = table


def last_kernel(previous, returned, out):
    state = previous[...] + jnp.sum(returned[...].astype(jnp.float32), axis=0)
    out[...] = state.astype(jnp.bfloat16)


def mlp_kernel(experts, fresh_flags, rows, *refs):
    out = refs[-1]
    width = out.shape[1]
    inputs, table = rows[:, :width], rows[:, width:]
    own = lax.axis_index("expert")
    total = None
    for i, fresh in enumerate(fresh_flags):
        for core in range(2):
            up, down = refs[4 * i + 2 * core : 4 * i + 2 * core + 2]
            owner = own if core == 0 else own + 1 - 2 * lax.rem(own, 2)
            pre_act = lax.dot_general(
                inputs, up[...], (((1,), (1,)), ((), ())), preferred_element_type=jnp.float32
            )
            hidden = (pre_act / (1.0 + jnp.exp(-pre_act))).astype(jnp.bfloat16)
            result = jnp.dot(hidden, down[...], preferred_element_type=jnp.float32)
            result = result * row_weights(experts, table, owner, fresh)
            total = result if total is None else total + result
    out[...] = total.astype(out.dtype)


def run_mlp(rows, weights, fresh_flags, out_type):
    experts = lax.axis_size("expert")
    count, width = rows.shape[0], weights[0].shape[1]
    hidden = sum(part.shape[0] for part in weights) // 2
    in_vmem = pl.BlockSpec(memory_space=pltpu.VMEM)
    return pl.pallas_call(
        functools.partial(mlp_kernel, experts, fresh_flags),
        out_shape=jax.ShapeDtypeStruct((count, width), out_type),
        in_specs=[in_vmem] * (1 + len(weights)),
        out_specs=in_vmem,
        compiler_params=pltpu.CompilerParams(vmem_limit_bytes=16 * MIB),
        cost_estimate=pl.CostEstimate(
            flops=8 * count * hidden * width, bytes_accessed=4 * hidden * width, transcendentals=0
        ),
    )(rows, *weights)


def chip_groups(experts):
    return [list(range(core, experts, 2)) for core in range(2)]


def spread(blocks):
    return lax.all_to_all(
        blocks, "expert", 0, 0, axis_index_groups=chip_groups(lax.axis_size("expert")), tiled=True
    )


def swap(value, axis):
    size = lax.axis_size(axis)
    return lax.ppermute(value, axis, [(i, i ^ 1) for i in range(size)])


def exchange_plan(tokens, norm_gain, routes, route_scale, changed, stale, learner):
    experts = lax.axis_size("expert")
    chips = experts // 2
    row_count, width = tokens.shape[1], tokens.shape[2]
    packed = width + table_width(experts)
    half = chips * row_count
    gain = norm_gain[None]
    blocks_shape = jax.ShapeDtypeStruct((chips, row_count, packed), jnp.bfloat16)
    state_shape = jax.ShapeDtypeStruct((row_count, width), jnp.float32)
    in_vmem = pl.BlockSpec(memory_space=pltpu.VMEM)
    in_smem = pl.BlockSpec(memory_space=pltpu.SMEM)
    small = pltpu.CompilerParams(vmem_limit_bytes=4 * MIB)
    weight_bytes = 2 * sum(part.size for part in stale + learner)
    long = pl.CostEstimate(
        flops=640 * weight_bytes, bytes_accessed=2 * weight_bytes, transcendentals=0
    )
    stale = stale + tuple(swap(part, "expert") for part in stale)
    learner = learner + tuple(swap(part, "expert") for part in learner)
    state = tokens[0]
    for step in range(routes.shape[0]):
        if step == 0:
            scaled = pl.pallas_call(
                first_kernel,
                in_specs=[in_vmem],
                out_specs=in_vmem,
                out_shape=state_shape,
                compiler_params=small,
                cost_estimate=long,
            )(state)
            blocks = pl.pallas_call(
                functools.partial(pack_kernel, experts),
                in_specs=[in_vmem] * 4,
                out_specs=in_vmem,
                out_shape=blocks_shape,
                compiler_params=small,
            )(scaled, gain, routes, route_scale)
        else:
            state, blocks = pl.pallas_call(
                functools.partial(next_kernel, experts, step),
                in_specs=[in_vmem] * 5 + [in_smem],
                out_specs=(in_vmem, in_vmem),
                out_shape=(state_shape, blocks_shape),
                compiler_params=small,
                cost_estimate=long,
            )(state, returned, gain, routes, route_scale, changed)
        rows = spread(blocks).reshape(half, packed)
        if step == 0:
            share = run_mlp(rows, stale, (False,), jnp.bfloat16)
        else:
            other = swap(rows, "group")
            share = run_mlp(rows, stale + learner, (False, True), jnp.float32)
            other, share = lax.optimization_barrier((other, share))
            away = run_mlp(other, learner, (True,), jnp.bfloat16)
            share = (share + swap(away, "group").astype(jnp.float32)).astype(jnp.bfloat16)
        returned = spread(share.reshape(chips, row_count, width))
    return pl.pallas_call(
        last_kernel,
        in_specs=[in_vmem] * 2,
        out_specs=in_vmem,
        out_shape=jax.ShapeDtypeStruct((row_count, width), jnp.bfloat16),
        compiler_params=small,
    )(state, returned)[None]


def gather_plan(tokens, norm_gain, routes, route_scale, changed, stale, learner):
    experts = lax.axis_size("expert")
    owner_index = lax.axis_index("expert")
    row_count = tokens.shape[1]
    top_count = routes.shape[3]
    capacity = min(row_count, max(2, 2 * row_count * top_count // experts))
    is_fresh = jnp.any(changed[0] == owner_index)
    fresh = [lax.all_gather(part, "group", axis=0, tiled=True) for part in learner]
    newer = [jnp.where(is_fresh, new, old) for new, old in zip(fresh, stale)]
    state = tokens[0].astype(jnp.float32)
    buffer_ids = jnp.arange(experts * capacity, dtype=jnp.int32)
    expert_ids = jnp.arange(experts, dtype=jnp.int32)
    for step in range(routes.shape[0]):
        normed = normalize(state, norm_gain)
        chosen = routes[step, 0]
        weights = route_scale[step, 0]
        hits = (chosen.reshape(-1)[:, None] == expert_ids[None, :]).astype(jnp.int32)
        before = jnp.cumsum(hits, axis=0) - hits
        slot_pos = jnp.sum(before * hits, axis=1).reshape(chosen.shape)
        target = chosen * capacity + slot_pos
        placed = (target[:, :, None] == buffer_ids[None, None, :]).astype(jnp.float32)
        merge_weights = jnp.sum(placed * weights[:, :, None], axis=1)
        send_matrix = jnp.sum(placed, axis=1).astype(jnp.bfloat16)
        outgoing = lax.dot_general(
            send_matrix, normed, (((0,), (0,)), ((), ())), preferred_element_type=jnp.float32
        )
        outgoing = outgoing.astype(jnp.bfloat16).reshape(experts, capacity, -1)
        received = lax.all_to_all(outgoing, "expert", split_axis=0, concat_axis=0, tiled=True)
        flat = received.reshape(-1, received.shape[-1])
        result = expert_apply(flat, *(stale if step == 0 else newer))
        answer = result.astype(jnp.bfloat16).reshape(received.shape)
        returned = lax.all_to_all(answer, "expert", split_axis=0, concat_axis=0, tiled=True)
        flat_back = returned.reshape(experts * capacity, -1).astype(jnp.float32)
        state = state + jnp.dot(merge_weights, flat_back, precision=lax.Precision.HIGHEST)
    return state.astype(jnp.bfloat16)[None]


def local(
    tokens,
    norm_gain,
    routes,
    route_scale,
    changed,
    rollout_up,
    rollout_down,
    learner_up,
    learner_down,
):
    experts = lax.axis_size("expert")
    groups = lax.axis_size("group")
    fewer = tokens.shape[1] * experts < learner_up.shape[1]
    paired = experts % 2 == 0 and groups == 2 and routes.shape[0] == 2
    plan = exchange_plan if fewer and paired else gather_plan
    stale = (rollout_up[0], rollout_down[0])
    learner = (learner_up[0], learner_down[0])
    return plan(tokens, norm_gain, routes, route_scale, changed, stale, learner)


def solution(mesh):
    placed = (
        P("group", "expert", None),
        P(),
        P(None, "group", "expert", None),
        P(None, "group", "expert", None),
        P("group", None),
        P("expert", None, None),
        P("expert", None, None),
        P("expert", "group", None),
        P("expert", "group", None),
    )
    return jax.shard_map(
        local, mesh=mesh, in_specs=placed, out_specs=P("group", "expert", None), check_vma=False
    )
```

```python
import functools
import jax
import jax.numpy as jnp
from jax import lax
from jax.experimental import pallas as pl
from jax.experimental.pallas import tpu as pltpu
from jax.sharding import PartitionSpec as P

LANES = 128
MATMUL_ROWS = 128
MIB = 1 << 20


def normalize(state, norm_gain):
    scale = lax.rsqrt(jnp.mean(state * state, axis=-1, keepdims=True) + 1e-06)
    return (state * scale * norm_gain).astype(jnp.bfloat16)


def expert_apply(inputs, up_rows, down_rows):
    pre_act = lax.dot_general(
        inputs, up_rows, (((1,), (1,)), ((), ())), preferred_element_type=jnp.float32
    )
    hidden = jax.nn.silu(pre_act).astype(jnp.bfloat16)
    return jnp.dot(hidden, down_rows, preferred_element_type=jnp.float32)


def table_width(experts):
    return -(-6 * experts // LANES) * LANES


def weight_table(experts, chosen, weights, changed):
    shape = (chosen.shape[0], table_width(experts))
    lane = lax.broadcasted_iota(jnp.int32, shape, 1)
    section, expert = lane // experts, lane % experts
    dense = jnp.zeros(shape, jnp.float32)
    for k in range(chosen.shape[1]):
        dense = jnp.where(chosen[:, k : k + 1] == expert, weights[:, k : k + 1], dense)
    fresh = section < 0
    for item in changed:
        fresh = fresh | (expert == item)
    high = dense.astype(jnp.bfloat16).astype(jnp.float32)
    rest = dense - high
    middle = rest.astype(jnp.bfloat16).astype(jnp.float32)
    low = rest - middle
    part = section % 3
    value = jnp.where(part == 0, high, jnp.where(part == 1, middle, low))
    value = jnp.where(fresh, jnp.where(section < 3, 0.0, value), jnp.where(section < 3, value, 0.0))
    return jnp.where(section < 6, value, 0.0).astype(jnp.bfloat16)


def row_weights(experts, table, owner, fresh):
    lane = lax.broadcasted_iota(jnp.int32, table.shape, 1)
    section = lane // experts
    first = 3 if fresh else 0
    mine = (lane % experts == owner) & (section >= first) & (section < first + 3)
    return jnp.sum(jnp.where(mine, table.astype(jnp.float32), 0.0), axis=1, keepdims=True)


def first_kernel(tokens, out):
    state = tokens[...].astype(jnp.float32)
    out[...] = state * lax.rsqrt(jnp.mean(state * state, axis=-1, keepdims=True) + 1e-06)


def pack_kernel(experts, scaled, gain, routes, scales, out):
    width = scaled.shape[1]
    normed = (scaled[...] * gain[...]).astype(jnp.bfloat16)
    table = weight_table(experts, routes[0, 0], scales[0, 0], [])
    for j in range(out.shape[0]):
        out[j, :, :width] = normed
        out[j, :, width:] = table


def next_kernel(experts, step, previous, returned, gain, routes, scales, changed, state_out, out):
    width = previous.shape[1]
    state = previous[...].astype(jnp.float32) + jnp.sum(returned[...].astype(jnp.float32), axis=0)
    state_out[...] = state
    normed = normalize(state, gain[...])
    items = [changed[0, i] for i in range(changed.shape[1])]
    table = weight_table(experts, routes[step, 0], scales[step, 0], items)
    for j in range(out.shape[0]):
        out[j, :, :width] = normed
        out[j, :, width:] = table


def last_kernel(previous, returned, out):
    state = previous[...] + jnp.sum(returned[...].astype(jnp.float32), axis=0)
    out[...] = state.astype(jnp.bfloat16)


def mlp_kernel(experts, fresh, row_sets, *refs):
    sources, refs = refs[:row_sets], refs[row_sets:]
    weights, outs = refs[:4], refs[4:]
    count, width = outs[0].shape
    rows = jnp.concatenate([source[...] for source in sources], axis=0)
    filled = jnp.concatenate([rows] * max(1, MATMUL_ROWS // rows.shape[0]), axis=0)
    inputs, table = filled[:, :width], rows[:, width:]
    own = lax.axis_index("expert")
    total = None
    for core in range(2):
        up, down = weights[2 * core : 2 * core + 2]
        owner = own if core == 0 else own + 1 - 2 * lax.rem(own, 2)
        pre_act = lax.dot_general(
            inputs, up[...], (((1,), (1,)), ((), ())), preferred_element_type=jnp.float32
        )
        hidden = (pre_act / (1.0 + jnp.exp(-pre_act))).astype(jnp.bfloat16)
        result = jnp.dot(hidden, down[...], preferred_element_type=jnp.float32)
        result = result[: rows.shape[0]] * row_weights(experts, table, owner, fresh)
        total = result if total is None else total + result
    for i, out in enumerate(outs):
        out[...] = total[i * count : (i + 1) * count].astype(out.dtype)


def run_mlp(row_sets, weights, fresh, out_types):
    experts = lax.axis_size("expert")
    count, width = row_sets[0].shape[0], weights[0].shape[1]
    hidden = sum(part.shape[0] for part in weights) // 2
    in_vmem = pl.BlockSpec(memory_space=pltpu.VMEM)
    return pl.pallas_call(
        functools.partial(mlp_kernel, experts, fresh, len(row_sets)),
        out_shape=[jax.ShapeDtypeStruct((count, width), out_type) for out_type in out_types],
        in_specs=[in_vmem] * (len(row_sets) + len(weights)),
        out_specs=[in_vmem] * len(out_types),
        compiler_params=pltpu.CompilerParams(vmem_limit_bytes=16 * MIB),
        cost_estimate=pl.CostEstimate(
            flops=8 * count * hidden * width, bytes_accessed=4 * hidden * width, transcendentals=0
        ),
    )(*row_sets, *weights)


def chip_groups(experts):
    return [list(range(core, experts, 2)) for core in range(2)]


def spread(blocks):
    return lax.all_to_all(
        blocks, "expert", 0, 0, axis_index_groups=chip_groups(lax.axis_size("expert")), tiled=True
    )


def swap(value, axis):
    size = lax.axis_size(axis)
    return lax.ppermute(value, axis, [(i, i ^ 1) for i in range(size)])


def exchange_plan(tokens, norm_gain, routes, route_scale, changed, stale, learner):
    experts = lax.axis_size("expert")
    chips = experts // 2
    row_count, width = tokens.shape[1], tokens.shape[2]
    packed = width + table_width(experts)
    half = chips * row_count
    gain = norm_gain[None]
    blocks_shape = jax.ShapeDtypeStruct((chips, row_count, packed), jnp.bfloat16)
    state_shape = jax.ShapeDtypeStruct((row_count, width), jnp.float32)
    in_vmem = pl.BlockSpec(memory_space=pltpu.VMEM)
    in_smem = pl.BlockSpec(memory_space=pltpu.SMEM)
    small = pltpu.CompilerParams(vmem_limit_bytes=4 * MIB)
    weight_bytes = 2 * sum(part.size for part in stale + learner)
    long = pl.CostEstimate(
        flops=1280 * weight_bytes, bytes_accessed=2 * weight_bytes, transcendentals=0
    )
    stale = stale + tuple(swap(part, "expert") for part in stale)
    learner = learner + tuple(swap(part, "expert") for part in learner)
    state = tokens[0]
    for step in range(routes.shape[0]):
        if step == 0:
            scaled = pl.pallas_call(
                first_kernel,
                in_specs=[in_vmem],
                out_specs=in_vmem,
                out_shape=state_shape,
                compiler_params=small,
                cost_estimate=long,
            )(state)
            blocks = pl.pallas_call(
                functools.partial(pack_kernel, experts),
                in_specs=[in_vmem] * 4,
                out_specs=in_vmem,
                out_shape=blocks_shape,
                compiler_params=small,
            )(scaled, gain, routes, route_scale)
        else:
            state, blocks = pl.pallas_call(
                functools.partial(next_kernel, experts, step),
                in_specs=[in_vmem] * 5 + [in_smem],
                out_specs=(in_vmem, in_vmem),
                out_shape=(state_shape, blocks_shape),
                compiler_params=small,
                cost_estimate=long,
            )(state, returned, gain, routes, route_scale, changed)
        rows = spread(blocks).reshape(half, packed)
        if step == 0:
            (share,) = run_mlp([rows], stale, False, [jnp.bfloat16])
        else:
            other = swap(rows, "group")
            (old,) = run_mlp([rows], stale, False, [jnp.float32])
            other, old = lax.optimization_barrier((other, old))
            new, away = run_mlp([rows, other], learner, True, [jnp.float32, jnp.bfloat16])
            share = old + new + swap(away, "group").astype(jnp.float32)
            share = share.astype(jnp.bfloat16)
        returned = spread(share.reshape(chips, row_count, width))
    return pl.pallas_call(
        last_kernel,
        in_specs=[in_vmem] * 2,
        out_specs=in_vmem,
        out_shape=jax.ShapeDtypeStruct((row_count, width), jnp.bfloat16),
        compiler_params=small,
    )(state, returned)[None]


def gather_plan(tokens, norm_gain, routes, route_scale, changed, stale, learner):
    experts = lax.axis_size("expert")
    owner_index = lax.axis_index("expert")
    row_count = tokens.shape[1]
    top_count = routes.shape[3]
    capacity = min(row_count, max(2, 2 * row_count * top_count // experts))
    is_fresh = jnp.any(changed[0] == owner_index)
    fresh = [lax.all_gather(part, "group", axis=0, tiled=True) for part in learner]
    newer = [jnp.where(is_fresh, new, old) for new, old in zip(fresh, stale)]
    state = tokens[0].astype(jnp.float32)
    buffer_ids = jnp.arange(experts * capacity, dtype=jnp.int32)
    expert_ids = jnp.arange(experts, dtype=jnp.int32)
    for step in range(routes.shape[0]):
        normed = normalize(state, norm_gain)
        chosen = routes[step, 0]
        weights = route_scale[step, 0]
        hits = (chosen.reshape(-1)[:, None] == expert_ids[None, :]).astype(jnp.int32)
        before = jnp.cumsum(hits, axis=0) - hits
        slot_pos = jnp.sum(before * hits, axis=1).reshape(chosen.shape)
        target = chosen * capacity + slot_pos
        placed = (target[:, :, None] == buffer_ids[None, None, :]).astype(jnp.float32)
        merge_weights = jnp.sum(placed * weights[:, :, None], axis=1)
        send_matrix = jnp.sum(placed, axis=1).astype(jnp.bfloat16)
        outgoing = lax.dot_general(
            send_matrix, normed, (((0,), (0,)), ((), ())), preferred_element_type=jnp.float32
        )
        outgoing = outgoing.astype(jnp.bfloat16).reshape(experts, capacity, -1)
        received = lax.all_to_all(outgoing, "expert", split_axis=0, concat_axis=0, tiled=True)
        flat = received.reshape(-1, received.shape[-1])
        result = expert_apply(flat, *(stale if step == 0 else newer))
        answer = result.astype(jnp.bfloat16).reshape(received.shape)
        returned = lax.all_to_all(answer, "expert", split_axis=0, concat_axis=0, tiled=True)
        flat_back = returned.reshape(experts * capacity, -1).astype(jnp.float32)
        state = state + jnp.dot(merge_weights, flat_back, precision=lax.Precision.HIGHEST)
    return state.astype(jnp.bfloat16)[None]


def local(
    tokens,
    norm_gain,
    routes,
    route_scale,
    changed,
    rollout_up,
    rollout_down,
    learner_up,
    learner_down,
):
    experts = lax.axis_size("expert")
    groups = lax.axis_size("group")
    fewer = tokens.shape[1] * experts < learner_up.shape[1]
    paired = experts % 2 == 0 and groups == 2 and routes.shape[0] == 2
    plan = exchange_plan if fewer and paired else gather_plan
    stale = (rollout_up[0], rollout_down[0])
    learner = (learner_up[0], learner_down[0])
    return plan(tokens, norm_gain, routes, route_scale, changed, stale, learner)


def solution(mesh):
    placed = (
        P("group", "expert", None),
        P(),
        P(None, "group", "expert", None),
        P(None, "group", "expert", None),
        P("group", None),
        P("expert", None, None),
        P("expert", None, None),
        P("expert", "group", None),
        P("expert", "group", None),
    )
    return jax.shard_map(
        local, mesh=mesh, in_specs=placed, out_specs=P("group", "expert", None), check_vma=False
    )
```

```python
import functools
import jax
import jax.numpy as jnp
from jax import lax
from jax.experimental import pallas as pl
from jax.experimental.pallas import tpu as pltpu
from jax.sharding import PartitionSpec as P

LANES = 128
MATMUL_ROWS = 128
MIB = 1 << 20


def normalize(state, norm_gain):
    scale = lax.rsqrt(jnp.mean(state * state, axis=-1, keepdims=True) + 1e-06)
    return (state * scale * norm_gain).astype(jnp.bfloat16)


def expert_apply(inputs, up_rows, down_rows):
    pre_act = lax.dot_general(
        inputs, up_rows, (((1,), (1,)), ((), ())), preferred_element_type=jnp.float32
    )
    hidden = jax.nn.silu(pre_act).astype(jnp.bfloat16)
    return jnp.dot(hidden, down_rows, preferred_element_type=jnp.float32)


def table_width(experts):
    return -(-6 * experts // LANES) * LANES


def weight_table(experts, chosen, weights, changed):
    shape = (chosen.shape[0], table_width(experts))
    lane = lax.broadcasted_iota(jnp.int32, shape, 1)
    section, expert = lane // experts, lane % experts
    dense = jnp.zeros(shape, jnp.float32)
    for k in range(chosen.shape[1]):
        dense = jnp.where(chosen[:, k : k + 1] == expert, weights[:, k : k + 1], dense)
    fresh = section < 0
    for item in changed:
        fresh = fresh | (expert == item)
    high = dense.astype(jnp.bfloat16).astype(jnp.float32)
    rest = dense - high
    middle = rest.astype(jnp.bfloat16).astype(jnp.float32)
    low = rest - middle
    part = section % 3
    value = jnp.where(part == 0, high, jnp.where(part == 1, middle, low))
    value = jnp.where(fresh, jnp.where(section < 3, 0.0, value), jnp.where(section < 3, value, 0.0))
    return jnp.where(section < 6, value, 0.0).astype(jnp.bfloat16)


def row_weights(experts, table, owner, fresh):
    lane = lax.broadcasted_iota(jnp.int32, table.shape, 1)
    section = lane // experts
    first = 3 if fresh else 0
    mine = (lane % experts == owner) & (section >= first) & (section < first + 3)
    return jnp.sum(jnp.where(mine, table.astype(jnp.float32), 0.0), axis=1, keepdims=True)


def first_kernel(tokens, out):
    state = tokens[...].astype(jnp.float32)
    out[...] = state * lax.rsqrt(jnp.mean(state * state, axis=-1, keepdims=True) + 1e-06)


def pack_kernel(experts, scaled, gain, routes, scales, out):
    width = scaled.shape[1]
    out[:, :width] = (scaled[...] * gain[...]).astype(jnp.bfloat16)
    out[:, width:] = weight_table(experts, routes[0, 0], scales[0, 0], [])


def next_kernel(experts, step, previous, kept, received, gain, routes, scales, changed, state_out, out):
    width = previous.shape[1]
    state = previous[...].astype(jnp.float32) + (kept[...] + received[...].astype(jnp.float32))
    state_out[...] = state
    items = [changed[:, i : i + 1] for i in range(changed.shape[1])]
    out[:, :width] = normalize(state, gain[...])
    out[:, width:] = weight_table(experts, routes[step, 0], scales[step, 0], items)


def last_kernel(previous, kept, received, out):
    state = previous[...] + (kept[...] + received[...].astype(jnp.float32))
    out[...] = state.astype(jnp.bfloat16)


def join_kernel(first, second, out):
    out[0] = first[...]
    out[1] = second[...]


def halve_kernel(kept, *refs):
    received, (kept_out, sent_out) = refs[:-2], refs[-2:]
    total = kept[...]
    for part in received:
        total = total + part[...].astype(jnp.float32)
    count = kept_out.shape[0]
    kept_out[...] = total[:count]
    sent_out[...] = total[count:].astype(jnp.bfloat16)


def mlp_kernel(experts, fresh, set_sizes, before, *refs):
    refs = list(refs)
    sources = [refs.pop(0) for _ in range(sum(set_sizes))]
    weights = [refs.pop(0) for _ in range(4)]
    earlier = refs.pop(0) if before else None
    rows = jnp.concatenate([source[...] for source in sources], axis=0)
    width = refs[0].shape[1]
    filled = jnp.concatenate([rows] * max(1, MATMUL_ROWS // rows.shape[0]), axis=0)
    inputs, table = filled[:, :width], rows[:, width:]
    own = lax.axis_index("expert")
    total = None
    for core in range(2):
        up, down = weights[2 * core : 2 * core + 2]
        owner = own if core == 0 else own + 1 - 2 * lax.rem(own, 2)
        pre_act = lax.dot_general(
            inputs, up[...], (((1,), (1,)), ((), ())), preferred_element_type=jnp.float32
        )
        hidden = (pre_act / (1.0 + jnp.exp(-pre_act))).astype(jnp.bfloat16)
        result = jnp.dot(hidden, down[...], preferred_element_type=jnp.float32)
        result = result[: rows.shape[0]] * row_weights(experts, table, owner, fresh)
        total = result if total is None else total + result
    start = 0
    for out in refs:
        count = out.shape[0]
        part = total[start : start + count]
        if before and start < earlier.shape[0]:
            part = part + earlier[start : start + count]
        out[...] = part.astype(out.dtype)
        start = start + count


def on_vmem(kernel, inputs, outputs, limit=2 * MIB, cost=None):
    in_vmem = pl.BlockSpec(memory_space=pltpu.VMEM)
    return pl.pallas_call(
        kernel,
        out_shape=[jax.ShapeDtypeStruct(shape, kind) for shape, kind in outputs],
        in_specs=[in_vmem] * len(inputs),
        out_specs=[in_vmem] * len(outputs),
        compiler_params=pltpu.CompilerParams(vmem_limit_bytes=limit),
        cost_estimate=cost,
    )(*inputs)


def run_mlp(row_sets, weights, fresh, outputs, before=()):
    width = weights[0].shape[1]
    count = sum(part.shape[0] for rows in row_sets for part in rows)
    hidden = sum(part.shape[0] for part in weights) // 2
    kernel = functools.partial(
        mlp_kernel,
        lax.axis_size("expert"),
        fresh,
        [len(rows) for rows in row_sets],
        len(before) > 0,
    )
    cost = pl.CostEstimate(
        flops=8 * count * hidden * width, bytes_accessed=4 * hidden * width, transcendentals=0
    )
    inputs = [part for rows in row_sets for part in rows] + list(weights) + list(before)
    outputs = [((rows, width), kind) for rows, kind in outputs]
    return on_vmem(kernel, inputs, outputs, 8 * MIB, cost)


def swap(value, axis, distance):
    size = lax.axis_size(axis)
    return lax.ppermute(value, axis, [(i, i ^ distance) for i in range(size)])


def swap_core(value):
    return swap(value, "expert", 1)


def swap_group(value):
    return swap(value, "group", 1)


def chip_distances():
    distances = [2]
    while 2 * distances[-1] < lax.axis_size("expert"):
        distances.append(2 * distances[-1])
    return distances


def gather(block):
    for distance in reversed(chip_distances()[1:]):
        rows, width = block.shape
        joined = ((2, rows, width), block.dtype)
        (block,) = on_vmem(join_kernel, (block, swap(block, "expert", distance)), [joined])
        block = block.reshape(2 * rows, width)
    return block


def halve(kept, *received):
    rows, width = kept.shape
    half = (rows // 2, width)
    return on_vmem(
        halve_kernel, (kept,) + received, [(half, jnp.float32), (half, jnp.bfloat16)], 4 * MIB
    )


def give_back(kept, *received):
    for distance in chip_distances()[1:]:
        kept, sent = halve(kept, *received)
        received = (swap(sent, "expert", distance),)
    return kept, received[0]


def exchange_plan(tokens, norm_gain, routes, route_scale, changed, stale, learner):
    experts = lax.axis_size("expert")
    row_count, width = tokens.shape[1], tokens.shape[2]
    line = experts // 4 * row_count
    near = chip_distances()[0]
    gain = norm_gain[None]
    block_shape = ((row_count, width + table_width(experts)), jnp.bfloat16)
    state_shape = ((row_count, width), jnp.float32)
    weight_bytes = 2 * sum(part.size for part in stale + learner)
    long = pl.CostEstimate(
        flops=1280 * weight_bytes, bytes_accessed=2 * weight_bytes, transcendentals=0
    )
    stale = stale + tuple(swap_core(part) for part in stale)
    learner = learner + tuple(swap_core(part) for part in learner)
    state = tokens[0]
    for step in range(routes.shape[0]):
        if step == 0:
            (scaled,) = on_vmem(first_kernel, (state,), [state_shape], cost=long)
            (block,) = on_vmem(
                functools.partial(pack_kernel, experts),
                (scaled, gain, routes, route_scale),
                [block_shape],
            )
        else:
            state, block = on_vmem(
                functools.partial(next_kernel, experts, step),
                (state, kept, received, gain, routes, route_scale, changed),
                [state_shape, block_shape],
            )
        rows = gather(block)
        across = swap(rows, "expert", near)
        mine = [(line, jnp.float32), (line, jnp.bfloat16)]
        if step == 0:
            kept, sent = run_mlp([(rows, across)], stale, False, mine)
            kept, received = give_back(kept, swap(sent, "expert", near))
        else:
            other, other_across = swap_group(rows), swap_group(across)
            (old,) = run_mlp([(rows, across)], stale, False, [(2 * line, jnp.float32)])
            other_across, old = lax.optimization_barrier((other_across, old))
            kept, sent, away_kept, away_sent = run_mlp(
                [(rows, across), (other, other_across)], learner, True, mine + mine, (old,)
            )
            away = away_kept + swap(away_sent, "expert", near).astype(jnp.float32)
            away = swap_group(away.astype(jnp.bfloat16))
            kept, received = give_back(kept, swap(sent, "expert", near), away)
    (updated,) = on_vmem(
        last_kernel, (state, kept, received), [((row_count, width), jnp.bfloat16)]
    )
    return updated[None]


def gather_plan(tokens, norm_gain, routes, route_scale, changed, stale, learner):
    experts = lax.axis_size("expert")
    owner_index = lax.axis_index("expert")
    row_count = tokens.shape[1]
    top_count = routes.shape[3]
    capacity = min(row_count, max(2, 2 * row_count * top_count // experts))
    is_fresh = jnp.any(changed[0] == owner_index)
    fresh = [lax.all_gather(part, "group", axis=0, tiled=True) for part in learner]
    newer = [jnp.where(is_fresh, new, old) for new, old in zip(fresh, stale)]
    state = tokens[0].astype(jnp.float32)
    buffer_ids = jnp.arange(experts * capacity, dtype=jnp.int32)
    expert_ids = jnp.arange(experts, dtype=jnp.int32)
    for step in range(routes.shape[0]):
        normed = normalize(state, norm_gain)
        chosen = routes[step, 0]
        weights = route_scale[step, 0]
        hits = (chosen.reshape(-1)[:, None] == expert_ids[None, :]).astype(jnp.int32)
        before = jnp.cumsum(hits, axis=0) - hits
        slot_pos = jnp.sum(before * hits, axis=1).reshape(chosen.shape)
        target = chosen * capacity + slot_pos
        placed = (target[:, :, None] == buffer_ids[None, None, :]).astype(jnp.float32)
        merge_weights = jnp.sum(placed * weights[:, :, None], axis=1)
        send_matrix = jnp.sum(placed, axis=1).astype(jnp.bfloat16)
        outgoing = lax.dot_general(
            send_matrix, normed, (((0,), (0,)), ((), ())), preferred_element_type=jnp.float32
        )
        outgoing = outgoing.astype(jnp.bfloat16).reshape(experts, capacity, -1)
        received = lax.all_to_all(outgoing, "expert", split_axis=0, concat_axis=0, tiled=True)
        flat = received.reshape(-1, received.shape[-1])
        result = expert_apply(flat, *(stale if step == 0 else newer))
        answer = result.astype(jnp.bfloat16).reshape(received.shape)
        returned = lax.all_to_all(answer, "expert", split_axis=0, concat_axis=0, tiled=True)
        flat_back = returned.reshape(experts * capacity, -1).astype(jnp.float32)
        state = state + jnp.dot(merge_weights, flat_back, precision=lax.Precision.HIGHEST)
    return state.astype(jnp.bfloat16)[None]


def local(
    tokens,
    norm_gain,
    routes,
    route_scale,
    changed,
    rollout_up,
    rollout_down,
    learner_up,
    learner_down,
):
    experts = lax.axis_size("expert")
    groups = lax.axis_size("group")
    fewer = tokens.shape[1] * experts < learner_up.shape[1]
    paired = experts & (experts - 1) == 0 and experts >= 8 and groups == 2
    plan = exchange_plan if fewer and paired else gather_plan
    stale = (rollout_up[0], rollout_down[0])
    learner = (learner_up[0], learner_down[0])
    return plan(tokens, norm_gain, routes, route_scale, changed, stale, learner)


def solution(mesh):
    placed = (
        P("group", "expert", None),
        P(),
        P(None, "group", "expert", None),
        P(None, "group", "expert", None),
        P("group", None),
        P("expert", None, None),
        P("expert", None, None),
        P("expert", "group", None),
        P("expert", "group", None),
    )
    return jax.shard_map(
        local, mesh=mesh, in_specs=placed, out_specs=P("group", "expert", None), check_vma=False
    )
```

```python
import functools
import jax
import jax.numpy as jnp
from jax import lax
from jax.experimental import pallas as pl
from jax.experimental.pallas import tpu as pltpu
from jax.sharding import PartitionSpec as P

LANES = 128
MATMUL_ROWS = 128
MIB = 1 << 20


def normalize(state, norm_gain):
    scale = lax.rsqrt(jnp.mean(state * state, axis=-1, keepdims=True) + 1e-06)
    return (state * scale * norm_gain).astype(jnp.bfloat16)


def expert_apply(inputs, up_rows, down_rows):
    pre_act = lax.dot_general(
        inputs, up_rows, (((1,), (1,)), ((), ())), preferred_element_type=jnp.float32
    )
    hidden = jax.nn.silu(pre_act).astype(jnp.bfloat16)
    return jnp.dot(hidden, down_rows, preferred_element_type=jnp.float32)


def table_width(experts):
    return -(-6 * experts // LANES) * LANES


def weight_table(experts, chosen, weights, changed):
    shape = (chosen.shape[0], table_width(experts))
    lane = lax.broadcasted_iota(jnp.int32, shape, 1)
    section, expert = lane // experts, lane % experts
    dense = jnp.zeros(shape, jnp.float32)
    for k in range(chosen.shape[1]):
        dense = jnp.where(chosen[:, k : k + 1] == expert, weights[:, k : k + 1], dense)
    fresh = section < 0
    for item in changed:
        fresh = fresh | (expert == item)
    high = dense.astype(jnp.bfloat16).astype(jnp.float32)
    rest = dense - high
    middle = rest.astype(jnp.bfloat16).astype(jnp.float32)
    low = rest - middle
    part = section % 3
    value = jnp.where(part == 0, high, jnp.where(part == 1, middle, low))
    value = jnp.where(fresh, jnp.where(section < 3, 0.0, value), jnp.where(section < 3, value, 0.0))
    return jnp.where(section < 6, value, 0.0).astype(jnp.bfloat16)


def row_weights(experts, table, owner, fresh):
    lane = lax.broadcasted_iota(jnp.int32, table.shape, 1)
    section = lane // experts
    first = 3 if fresh else 0
    mine = (lane % experts == owner) & (section >= first) & (section < first + 3)
    return jnp.sum(jnp.where(mine, table.astype(jnp.float32), 0.0), axis=1, keepdims=True)


def first_kernel(tokens, out):
    state = tokens[...].astype(jnp.float32)
    out[...] = state * lax.rsqrt(jnp.mean(state * state, axis=-1, keepdims=True) + 1e-06)


def pack_kernel(experts, scaled, gain, routes, scales, out):
    width = scaled.shape[1]
    out[:, :width] = (scaled[...] * gain[...]).astype(jnp.bfloat16)
    out[:, width:] = weight_table(experts, routes[0, 0], scales[0, 0], [])


def next_kernel(experts, step, previous, kept, received, gain, routes, scales, changed, state_out, out):
    width = previous.shape[1]
    state = previous[...].astype(jnp.float32) + (kept[...] + received[...].astype(jnp.float32))
    state_out[...] = state
    items = [changed[:, i : i + 1] for i in range(changed.shape[1])]
    out[:, :width] = normalize(state, gain[...])
    out[:, width:] = weight_table(experts, routes[step, 0], scales[step, 0], items)


def last_kernel(previous, kept, received, out):
    state = previous[...] + (kept[...] + received[...].astype(jnp.float32))
    out[...] = state.astype(jnp.bfloat16)


def join_kernel(first, second, out):
    out[0] = first[...]
    out[1] = second[...]


def halve_kernel(kept, *refs):
    received, (kept_out, sent_out) = refs[:-2], refs[-2:]
    total = kept[...]
    for part in received:
        total = total + part[...].astype(jnp.float32)
    count = kept_out.shape[0]
    kept_out[...] = total[:count]
    sent_out[...] = total[count:].astype(jnp.bfloat16)


def mlp_kernel(experts, fresh, set_sizes, before, *refs):
    refs = list(refs)
    sources = [refs.pop(0) for _ in range(sum(set_sizes))]
    weights = [refs.pop(0) for _ in range(4)]
    earlier = refs.pop(0) if before else None
    rows = jnp.concatenate([source[...] for source in sources], axis=0)
    width = refs[0].shape[1]
    filled = jnp.concatenate([rows] * max(1, MATMUL_ROWS // rows.shape[0]), axis=0)
    inputs, table = filled[:, :width], rows[:, width:]
    own = lax.axis_index("expert")
    total = None
    for core in range(2):
        up, down = weights[2 * core : 2 * core + 2]
        owner = own if core == 0 else own + 1 - 2 * lax.rem(own, 2)
        pre_act = lax.dot_general(
            inputs, up[...], (((1,), (1,)), ((), ())), preferred_element_type=jnp.float32
        )
        hidden = (pre_act / (1.0 + jnp.exp(-pre_act))).astype(jnp.bfloat16)
        result = jnp.dot(hidden, down[...], preferred_element_type=jnp.float32)
        result = result[: rows.shape[0]] * row_weights(experts, table, owner, fresh)
        total = result if total is None else total + result
    start = 0
    for out in refs:
        count = out.shape[0]
        part = total[start : start + count]
        if before and start < earlier.shape[0]:
            part = part + earlier[start : start + count]
        out[...] = part.astype(out.dtype)
        start = start + count


def on_vmem(kernel, inputs, outputs, limit=2 * MIB, cost=None):
    in_vmem = pl.BlockSpec(memory_space=pltpu.VMEM)
    return pl.pallas_call(
        kernel,
        out_shape=[jax.ShapeDtypeStruct(shape, kind) for shape, kind in outputs],
        in_specs=[in_vmem] * len(inputs),
        out_specs=[in_vmem] * len(outputs),
        compiler_params=pltpu.CompilerParams(vmem_limit_bytes=limit),
        cost_estimate=cost,
    )(*inputs)


def run_mlp(row_sets, weights, fresh, outputs, before=()):
    width = weights[0].shape[1]
    count = sum(part.shape[0] for rows in row_sets for part in rows)
    hidden = sum(part.shape[0] for part in weights) // 2
    kernel = functools.partial(
        mlp_kernel,
        lax.axis_size("expert"),
        fresh,
        [len(rows) for rows in row_sets],
        len(before) > 0,
    )
    cost = pl.CostEstimate(
        flops=8 * count * hidden * width, bytes_accessed=4 * hidden * width, transcendentals=0
    )
    inputs = [part for rows in row_sets for part in rows] + list(weights) + list(before)
    outputs = [((rows, width), kind) for rows, kind in outputs]
    return on_vmem(kernel, inputs, outputs, 8 * MIB, cost)


def swap_core(value):
    size = lax.axis_size("expert")
    return lax.ppermute(value, "expert", [(i, i ^ 1) for i in range(size)])


def swap_chip(value, distance):
    size = lax.axis_size("expert")
    return lax.ppermute(value, "expert", [(i, i ^ distance ^ 1) for i in range(size)])


def swap_group(value):
    size = lax.axis_size("expert")
    pairs = [(i, i ^ size ^ 1) for i in range(2 * size)]
    return lax.ppermute(value, ("group", "expert"), pairs)


def chip_distances():
    distances = [2]
    while 2 * distances[-1] < lax.axis_size("expert"):
        distances.append(2 * distances[-1])
    return distances


def gather(block):
    for distance in reversed(chip_distances()[1:]):
        rows, width = block.shape
        joined = ((2, rows, width), block.dtype)
        (block,) = on_vmem(join_kernel, (block, swap_chip(block, distance)), [joined])
        block = block.reshape(2 * rows, width)
    return block


def halve(kept, *received):
    rows, width = kept.shape
    half = (rows // 2, width)
    return on_vmem(
        halve_kernel, (kept,) + received, [(half, jnp.float32), (half, jnp.bfloat16)], 4 * MIB
    )


def give_back(kept, *received):
    for distance in chip_distances()[1:]:
        kept, sent = halve(kept, *received)
        received = (swap_chip(sent, distance),)
    return kept, received[0]


def exchange_plan(tokens, norm_gain, routes, route_scale, changed, stale, learner):
    experts = lax.axis_size("expert")
    row_count, width = tokens.shape[1], tokens.shape[2]
    line = experts // 4 * row_count
    near = chip_distances()[0]
    gain = norm_gain[None]
    block_shape = ((row_count, width + table_width(experts)), jnp.bfloat16)
    state_shape = ((row_count, width), jnp.float32)
    weight_bytes = 2 * sum(part.size for part in stale + learner)
    long = pl.CostEstimate(
        flops=1280 * weight_bytes, bytes_accessed=2 * weight_bytes, transcendentals=0
    )
    stale = stale + tuple(swap_core(part) for part in stale)
    learner = learner + tuple(swap_core(part) for part in learner)
    state = tokens[0]
    for step in range(routes.shape[0]):
        if step == 0:
            (scaled,) = on_vmem(first_kernel, (state,), [state_shape], cost=long)
            (block,) = on_vmem(
                functools.partial(pack_kernel, experts),
                (scaled, gain, routes, route_scale),
                [block_shape],
            )
        else:
            state, block = on_vmem(
                functools.partial(next_kernel, experts, step),
                (state, kept, received, gain, routes, route_scale, changed),
                [state_shape, block_shape],
            )
        rows = gather(block)
        across = swap_chip(rows, near)
        mine = [(line, jnp.float32), (line, jnp.bfloat16)]
        if step == 0:
            kept, sent = run_mlp([(rows, across)], stale, False, mine)
            kept, received = give_back(kept, swap_chip(sent, near))
        else:
            other, other_across = swap_group(rows), swap_group(across)
            (old,) = run_mlp([(rows, across)], stale, False, [(2 * line, jnp.float32)])
            other_across, old = lax.optimization_barrier((other_across, old))
            kept, sent, away_kept, away_sent = run_mlp(
                [(rows, across), (other, other_across)], learner, True, mine + mine, (old,)
            )
            away = away_kept + swap_chip(away_sent, near).astype(jnp.float32)
            away = swap_group(away.astype(jnp.bfloat16))
            kept, received = give_back(kept, swap_chip(sent, near), away)
    (updated,) = on_vmem(
        last_kernel, (state, kept, received), [((row_count, width), jnp.bfloat16)]
    )
    return updated[None]


def gather_plan(tokens, norm_gain, routes, route_scale, changed, stale, learner):
    experts = lax.axis_size("expert")
    owner_index = lax.axis_index("expert")
    row_count = tokens.shape[1]
    top_count = routes.shape[3]
    capacity = min(row_count, max(2, 2 * row_count * top_count // experts))
    is_fresh = jnp.any(changed[0] == owner_index)
    fresh = [lax.all_gather(part, "group", axis=0, tiled=True) for part in learner]
    newer = [jnp.where(is_fresh, new, old) for new, old in zip(fresh, stale)]
    state = tokens[0].astype(jnp.float32)
    buffer_ids = jnp.arange(experts * capacity, dtype=jnp.int32)
    expert_ids = jnp.arange(experts, dtype=jnp.int32)
    for step in range(routes.shape[0]):
        normed = normalize(state, norm_gain)
        chosen = routes[step, 0]
        weights = route_scale[step, 0]
        hits = (chosen.reshape(-1)[:, None] == expert_ids[None, :]).astype(jnp.int32)
        before = jnp.cumsum(hits, axis=0) - hits
        slot_pos = jnp.sum(before * hits, axis=1).reshape(chosen.shape)
        target = chosen * capacity + slot_pos
        placed = (target[:, :, None] == buffer_ids[None, None, :]).astype(jnp.float32)
        merge_weights = jnp.sum(placed * weights[:, :, None], axis=1)
        send_matrix = jnp.sum(placed, axis=1).astype(jnp.bfloat16)
        outgoing = lax.dot_general(
            send_matrix, normed, (((0,), (0,)), ((), ())), preferred_element_type=jnp.float32
        )
        outgoing = outgoing.astype(jnp.bfloat16).reshape(experts, capacity, -1)
        received = lax.all_to_all(outgoing, "expert", split_axis=0, concat_axis=0, tiled=True)
        flat = received.reshape(-1, received.shape[-1])
        result = expert_apply(flat, *(stale if step == 0 else newer))
        answer = result.astype(jnp.bfloat16).reshape(received.shape)
        returned = lax.all_to_all(answer, "expert", split_axis=0, concat_axis=0, tiled=True)
        flat_back = returned.reshape(experts * capacity, -1).astype(jnp.float32)
        state = state + jnp.dot(merge_weights, flat_back, precision=lax.Precision.HIGHEST)
    return state.astype(jnp.bfloat16)[None]


def local(
    tokens,
    norm_gain,
    routes,
    route_scale,
    changed,
    rollout_up,
    rollout_down,
    learner_up,
    learner_down,
):
    experts = lax.axis_size("expert")
    groups = lax.axis_size("group")
    fewer = tokens.shape[1] * experts < learner_up.shape[1]
    paired = experts & (experts - 1) == 0 and experts >= 8 and groups == 2
    plan = exchange_plan if fewer and paired else gather_plan
    stale = (rollout_up[0], rollout_down[0])
    learner = (learner_up[0], learner_down[0])
    return plan(tokens, norm_gain, routes, route_scale, changed, stale, learner)


def solution(mesh):
    placed = (
        P("group", "expert", None),
        P(),
        P(None, "group", "expert", None),
        P(None, "group", "expert", None),
        P("group", None),
        P("expert", None, None),
        P("expert", None, None),
        P("expert", "group", None),
        P("expert", "group", None),
    )
    return jax.shard_map(
        local, mesh=mesh, in_specs=placed, out_specs=P("group", "expert", None), check_vma=False
    )
```

```python
import functools
import jax
import jax.numpy as jnp
from jax import lax
from jax.experimental import pallas as pl
from jax.experimental.pallas import tpu as pltpu
from jax.sharding import PartitionSpec as P

LANES = 128
MATMUL_ROWS = 128
MIB = 1 << 20


def normalize(state, norm_gain):
    scale = lax.rsqrt(jnp.mean(state * state, axis=-1, keepdims=True) + 1e-06)
    return (state * scale * norm_gain).astype(jnp.bfloat16)


def expert_apply(inputs, up_rows, down_rows):
    pre_act = lax.dot_general(
        inputs, up_rows, (((1,), (1,)), ((), ())), preferred_element_type=jnp.float32
    )
    hidden = jax.nn.silu(pre_act).astype(jnp.bfloat16)
    return jnp.dot(hidden, down_rows, preferred_element_type=jnp.float32)


def table_width(experts):
    return -(-6 * experts // LANES) * LANES


def weight_table(experts, chosen, weights, changed):
    shape = (chosen.shape[0], table_width(experts))
    lane = lax.broadcasted_iota(jnp.int32, shape, 1)
    section, expert = lane // experts, lane % experts
    dense = jnp.zeros(shape, jnp.float32)
    for k in range(chosen.shape[1]):
        dense = jnp.where(chosen[:, k : k + 1] == expert, weights[:, k : k + 1], dense)
    fresh = section < 0
    for item in changed:
        fresh = fresh | (expert == item)
    high = dense.astype(jnp.bfloat16).astype(jnp.float32)
    rest = dense - high
    middle = rest.astype(jnp.bfloat16).astype(jnp.float32)
    low = rest - middle
    part = section % 3
    value = jnp.where(part == 0, high, jnp.where(part == 1, middle, low))
    value = jnp.where(fresh, jnp.where(section < 3, 0.0, value), jnp.where(section < 3, value, 0.0))
    return jnp.where(section < 6, value, 0.0).astype(jnp.bfloat16)


def row_weights(experts, table, owner, fresh):
    lane = lax.broadcasted_iota(jnp.int32, table.shape, 1)
    section = lane // experts
    first = 3 if fresh else 0
    mine = (lane % experts == owner) & (section >= first) & (section < first + 3)
    return jnp.sum(jnp.where(mine, table.astype(jnp.float32), 0.0), axis=1, keepdims=True)


def first_kernel(tokens, out):
    state = tokens[...].astype(jnp.float32)
    out[...] = state * lax.rsqrt(jnp.mean(state * state, axis=-1, keepdims=True) + 1e-06)


def pack_kernel(experts, scaled, gain, routes, scales, changed, out):
    width, span = scaled.shape[1], table_width(experts)
    normed = (scaled[...] * gain[...]).astype(jnp.bfloat16)
    for chip in range(out.shape[0]):
        out[chip, :, :width] = normed
    for step in range(routes.shape[0]):
        items = [changed[:, i : i + 1] for i in range(changed.shape[1])] if step > 0 else []
        table = weight_table(experts, routes[step, 0], scales[step, 0], items)
        for chip in range(out.shape[0]):
            out[chip, :, width + step * span : width + (step + 1) * span] = table


def sum_blocks(blocks):
    total = blocks[0].astype(jnp.float32)
    for chip in range(1, blocks.shape[0]):
        total = total + blocks[chip].astype(jnp.float32)
    return total


def next_kernel(previous, returned, gain, state_out, out):
    state = previous[...].astype(jnp.float32) + sum_blocks(returned)
    state_out[...] = state
    normed = normalize(state, gain[...])
    for chip in range(out.shape[0]):
        out[chip] = normed


def last_kernel(previous, returned, out):
    out[...] = (previous[...] + sum_blocks(returned)).astype(jnp.bfloat16)


def fill(rows):
    return jnp.concatenate([rows] * max(1, MATMUL_ROWS // rows.shape[0]), axis=0)


def join_kernel(first, rows, tables, out):
    width = rows.shape[1]
    out[:, :width] = rows[...]
    out[:, width:] = tables[:, first : first + out.shape[1] - width]


def mlp_kernel(experts, fresh, set_count, *refs):
    sources, refs = refs[:set_count], refs[set_count:]
    weights, outs = refs[:4], refs[4:]
    count, width = outs[0].shape
    span = table_width(experts)
    rows = jnp.concatenate([source[:, :width] for source in sources], axis=0)
    table = jnp.concatenate([source[:, width : width + span] for source in sources], axis=0)
    inputs = jnp.concatenate([rows] * max(1, MATMUL_ROWS // rows.shape[0]), axis=0)
    own = lax.axis_index("expert")
    total = None
    for core in range(2):
        up, down = weights[2 * core : 2 * core + 2]
        owner = own if core == 0 else own + 1 - 2 * lax.rem(own, 2)
        pre_act = lax.dot_general(
            inputs, up[...], (((1,), (1,)), ((), ())), preferred_element_type=jnp.float32
        )
        hidden = (pre_act / (1.0 + jnp.exp(-pre_act))).astype(jnp.bfloat16)
        result = jnp.dot(hidden, down[...], preferred_element_type=jnp.float32)
        result = result[: rows.shape[0]] * row_weights(experts, table, owner, fresh)
        total = result if total is None else total + result
    for i, out in enumerate(outs):
        out[...] = total[i * count : (i + 1) * count].astype(out.dtype)


def on_vmem(kernel, inputs, outputs, limit=4 * MIB, cost=None, after=()):
    in_vmem = pl.BlockSpec(memory_space=pltpu.VMEM)
    count = len(inputs)

    def body(*refs):
        kernel(*refs[:count], *refs[count + len(after) :])

    return pl.pallas_call(
        body,
        out_shape=[jax.ShapeDtypeStruct(shape, kind) for shape, kind in outputs],
        in_specs=[in_vmem] * count + [pl.BlockSpec(memory_space=pl.ANY)] * len(after),
        out_specs=[in_vmem] * len(outputs),
        compiler_params=pltpu.CompilerParams(vmem_limit_bytes=limit),
        cost_estimate=cost,
    )(*inputs, *after)


def run_mlp(row_sets, weights, fresh, out_types, after=()):
    count, width = row_sets[0].shape[0], weights[0].shape[1]
    size = sum(part.size for part in weights)
    cost = pl.CostEstimate(
        flops=4 * MATMUL_ROWS * size, bytes_accessed=4 * size, transcendentals=0
    )
    kernel = functools.partial(mlp_kernel, lax.axis_size("expert"), fresh, len(row_sets))
    outputs = [((count, width), out_type) for out_type in out_types]
    return on_vmem(kernel, tuple(row_sets) + tuple(weights), outputs, 8 * MIB, cost, after)


def swap_core(value):
    size = lax.axis_size("expert")
    return lax.ppermute(value, "expert", [(i, i ^ 1) for i in range(size)])


def swap_group(value):
    return lax.ppermute(value, "group", [(0, 1), (1, 0)])


def spread(blocks):
    size = lax.axis_size("expert")
    groups = [list(range(core, size, 2)) for core in range(2)]
    return lax.all_to_all(blocks, "expert", 0, 0, axis_index_groups=groups, tiled=True)


def exchange_plan(tokens, norm_gain, routes, route_scale, changed, stale, learner):
    experts = lax.axis_size("expert")
    chips = experts // 2
    row_count, width = tokens.shape[1], tokens.shape[2]
    half = chips * row_count
    steps_total = routes.shape[0]
    packed = width + steps_total * table_width(experts)
    gain = norm_gain[None]
    state_shape = ((row_count, width), jnp.float32)
    weight_bytes = 2 * sum(part.size for part in stale + learner)
    long = pl.CostEstimate(
        flops=1280 * weight_bytes, bytes_accessed=2 * weight_bytes, transcendentals=0
    )
    stale = stale + tuple(swap_core(part) for part in stale)
    learner = learner + tuple(swap_core(part) for part in learner)
    (scaled,) = on_vmem(first_kernel, (tokens[0],), [state_shape], cost=long)
    (blocks,) = on_vmem(
        functools.partial(pack_kernel, experts),
        (scaled, gain, routes, route_scale, changed),
        [((chips, row_count, packed), jnp.bfloat16)],
    )
    tables = spread(blocks).reshape(half, packed)
    rows, state = tables, tokens[0]
    for step in range(steps_total):
        if step == 0:
            (share,) = run_mlp([rows], stale, False, [jnp.bfloat16], learner[2:])
        else:
            state, blocks = on_vmem(
                next_kernel,
                (state, returned, gain),
                [state_shape, ((chips, row_count, width), jnp.bfloat16)],
            )
            rows = spread(blocks).reshape(half, width)
            span = table_width(experts)
            (rows,) = on_vmem(
                functools.partial(join_kernel, width + step * span),
                (rows, tables),
                [((half, width + span), jnp.bfloat16)],
            )
            other = swap_group(rows)
            (old,) = run_mlp([rows], stale, False, [jnp.float32])
            other, old = lax.optimization_barrier((other, old))
            new, away = run_mlp([rows, other], learner, True, [jnp.float32, jnp.bfloat16])
            share = old + new + swap_group(away).astype(jnp.float32)
            share = share.astype(jnp.bfloat16)
        returned = spread(share.reshape(chips, row_count, width))
    (updated,) = on_vmem(last_kernel, (state, returned), [((row_count, width), jnp.bfloat16)])
    return updated[None]


def gather_plan(tokens, norm_gain, routes, route_scale, changed, stale, learner):
    experts = lax.axis_size("expert")
    owner_index = lax.axis_index("expert")
    row_count = tokens.shape[1]
    top_count = routes.shape[3]
    capacity = min(row_count, max(2, 2 * row_count * top_count // experts))
    is_fresh = jnp.any(changed[0] == owner_index)
    fresh = [lax.all_gather(part, "group", axis=0, tiled=True) for part in learner]
    newer = [jnp.where(is_fresh, new, old) for new, old in zip(fresh, stale)]
    state = tokens[0].astype(jnp.float32)
    buffer_ids = jnp.arange(experts * capacity, dtype=jnp.int32)
    expert_ids = jnp.arange(experts, dtype=jnp.int32)
    for step in range(routes.shape[0]):
        normed = normalize(state, norm_gain)
        chosen = routes[step, 0]
        weights = route_scale[step, 0]
        hits = (chosen.reshape(-1)[:, None] == expert_ids[None, :]).astype(jnp.int32)
        before = jnp.cumsum(hits, axis=0) - hits
        slot_pos = jnp.sum(before * hits, axis=1).reshape(chosen.shape)
        target = chosen * capacity + slot_pos
        placed = (target[:, :, None] == buffer_ids[None, None, :]).astype(jnp.float32)
        merge_weights = jnp.sum(placed * weights[:, :, None], axis=1)
        send_matrix = jnp.sum(placed, axis=1).astype(jnp.bfloat16)
        outgoing = lax.dot_general(
            send_matrix, normed, (((0,), (0,)), ((), ())), preferred_element_type=jnp.float32
        )
        outgoing = outgoing.astype(jnp.bfloat16).reshape(experts, capacity, -1)
        received = lax.all_to_all(outgoing, "expert", split_axis=0, concat_axis=0, tiled=True)
        flat = received.reshape(-1, received.shape[-1])
        result = expert_apply(flat, *(stale if step == 0 else newer))
        answer = result.astype(jnp.bfloat16).reshape(received.shape)
        returned = lax.all_to_all(answer, "expert", split_axis=0, concat_axis=0, tiled=True)
        flat_back = returned.reshape(experts * capacity, -1).astype(jnp.float32)
        state = state + jnp.dot(merge_weights, flat_back, precision=lax.Precision.HIGHEST)
    return state.astype(jnp.bfloat16)[None]


def local(
    tokens,
    norm_gain,
    routes,
    route_scale,
    changed,
    rollout_up,
    rollout_down,
    learner_up,
    learner_down,
):
    experts = lax.axis_size("expert")
    groups = lax.axis_size("group")
    fewer = tokens.shape[1] * experts < learner_up.shape[1]
    paired = experts % 2 == 0 and groups == 2
    plan = exchange_plan if fewer and paired else gather_plan
    stale = (rollout_up[0], rollout_down[0])
    learner = (learner_up[0], learner_down[0])
    return plan(tokens, norm_gain, routes, route_scale, changed, stale, learner)


def solution(mesh):
    placed = (
        P("group", "expert", None),
        P(),
        P(None, "group", "expert", None),
        P(None, "group", "expert", None),
        P("group", None),
        P("expert", None, None),
        P("expert", None, None),
        P("expert", "group", None),
        P("expert", "group", None),
    )
    return jax.shard_map(
        local, mesh=mesh, in_specs=placed, out_specs=P("group", "expert", None), check_vma=False
    )
```

```python
import functools
import jax
import jax.numpy as jnp
from jax import lax
from jax.experimental import pallas as pl
from jax.experimental.pallas import tpu as pltpu
from jax.sharding import PartitionSpec as P

LANES = 128
MATMUL_ROWS = 128
MIB = 1 << 20


def normalize(state, norm_gain):
    scale = lax.rsqrt(jnp.mean(state * state, axis=-1, keepdims=True) + 1e-06)
    return (state * scale * norm_gain).astype(jnp.bfloat16)


def expert_apply(inputs, up_rows, down_rows):
    pre_act = lax.dot_general(
        inputs, up_rows, (((1,), (1,)), ((), ())), preferred_element_type=jnp.float32
    )
    hidden = jax.nn.silu(pre_act).astype(jnp.bfloat16)
    return jnp.dot(hidden, down_rows, preferred_element_type=jnp.float32)


def table_width(experts, steps_total):
    sections = 2 + 4 * (steps_total - 1)
    return -(-sections * experts // LANES) * LANES


def first_section(step, fresh):
    return 0 if step == 0 else 4 * step - 2 + 2 * fresh


def weight_table(experts, chosen, weights, changed):
    steps_total, _, rows, top_count = chosen.shape
    shape = (rows, table_width(experts, steps_total))
    lane = lax.broadcasted_iota(jnp.int32, shape, 1)
    section, expert = lane // experts, lane % experts
    fresh = section < 0
    for i in range(changed.shape[1]):
        fresh = fresh | (expert == changed[:, i : i + 1])
    table = jnp.zeros(shape, jnp.float32)
    for step in range(steps_total):
        dense = jnp.zeros(shape, jnp.float32)
        for k in range(top_count):
            hit = chosen[step, 0, :, k : k + 1] == expert
            dense = jnp.where(hit, weights[step, 0, :, k : k + 1], dense)
        high = dense.astype(jnp.bfloat16).astype(jnp.float32)
        value = jnp.where(section % 2 == 0, high, dense - high)
        start = first_section(step, False)
        if step == 0:
            table = jnp.where(section < 2, value, table)
        else:
            old = jnp.where(fresh, 0.0, value)
            new = jnp.where(fresh, value, 0.0)
            table = jnp.where((section >= start) & (section < start + 2), old, table)
            table = jnp.where((section >= start + 2) & (section < start + 4), new, table)
    return table.astype(jnp.bfloat16)


def row_weights(experts, table, owner, step, fresh):
    lane = lax.broadcasted_iota(jnp.int32, table.shape, 1)
    section = lane // experts
    first = first_section(step, fresh)
    mine = (lane % experts == owner) & (section >= first) & (section < first + 2)
    return jnp.sum(jnp.where(mine, table.astype(jnp.float32), 0.0), axis=1, keepdims=True)


def first_kernel(tokens, out):
    state = tokens[...].astype(jnp.float32)
    out[...] = state * lax.rsqrt(jnp.mean(state * state, axis=-1, keepdims=True) + 1e-06)


def pack_kernel(experts, scaled, gain, routes, scales, changed, out):
    width = scaled.shape[1]
    normed = (scaled[...] * gain[...]).astype(jnp.bfloat16)
    table = weight_table(experts, routes, scales, changed)
    for chip in range(out.shape[0]):
        out[chip, :, :width] = normed
        out[chip, :, width:] = table


def sum_blocks(blocks):
    total = blocks[0].astype(jnp.float32)
    for chip in range(1, blocks.shape[0]):
        total = total + blocks[chip].astype(jnp.float32)
    return total


def next_kernel(previous, returned, gain, state_out, out):
    state = previous[...].astype(jnp.float32) + sum_blocks(returned)
    state_out[...] = state
    normed = normalize(state, gain[...])
    for chip in range(out.shape[0]):
        out[chip] = normed


def last_kernel(previous, returned, out):
    out[...] = (previous[...] + sum_blocks(returned)).astype(jnp.bfloat16)


def join_kernel(rows, tables, out):
    width = rows.shape[1]
    out[:, :width] = rows[...]
    out[:, width:] = tables[:, width:]


def mlp_kernel(experts, step, fresh, set_count, *refs):
    sources, refs = refs[:set_count], refs[set_count:]
    weights, outs = refs[:4], refs[4:]
    count, width = outs[0].shape
    rows = jnp.concatenate([source[:, :width] for source in sources], axis=0)
    table = jnp.concatenate([source[:, width:] for source in sources], axis=0)
    inputs = jnp.concatenate([rows] * max(1, MATMUL_ROWS // rows.shape[0]), axis=0)
    own = lax.axis_index("expert")
    total = None
    for core in range(2):
        up, down = weights[2 * core : 2 * core + 2]
        owner = own if core == 0 else own + 1 - 2 * lax.rem(own, 2)
        pre_act = lax.dot_general(
            inputs, up[...], (((1,), (1,)), ((), ())), preferred_element_type=jnp.float32
        )
        hidden = (pre_act / (1.0 + jnp.exp(-pre_act))).astype(jnp.bfloat16)
        result = jnp.dot(hidden, down[...], preferred_element_type=jnp.float32)
        result = result[: rows.shape[0]] * row_weights(experts, table, owner, step, fresh)
        total = result if total is None else total + result
    for i, out in enumerate(outs):
        out[...] = total[i * count : (i + 1) * count].astype(out.dtype)


def on_vmem(kernel, inputs, outputs, limit=4 * MIB, cost=None, after=()):
    in_vmem = pl.BlockSpec(memory_space=pltpu.VMEM)
    count = len(inputs)

    def body(*refs):
        kernel(*refs[:count], *refs[count + len(after) :])

    return pl.pallas_call(
        body,
        out_shape=[jax.ShapeDtypeStruct(shape, kind) for shape, kind in outputs],
        in_specs=[in_vmem] * count + [pl.BlockSpec(memory_space=pl.ANY)] * len(after),
        out_specs=[in_vmem] * len(outputs),
        compiler_params=pltpu.CompilerParams(vmem_limit_bytes=limit),
        cost_estimate=cost,
    )(*inputs, *after)


def run_mlp(row_sets, weights, step, fresh, out_types, after=()):
    count, width = row_sets[0].shape[0], weights[0].shape[1]
    size = sum(part.size for part in weights)
    cost = pl.CostEstimate(
        flops=4 * MATMUL_ROWS * size, bytes_accessed=4 * size, transcendentals=0
    )
    kernel = functools.partial(mlp_kernel, lax.axis_size("expert"), step, fresh, len(row_sets))
    outputs = [((count, width), out_type) for out_type in out_types]
    return on_vmem(kernel, tuple(row_sets) + tuple(weights), outputs, 8 * MIB, cost, after)


def swap_core(value):
    size = lax.axis_size("expert")
    return lax.ppermute(value, "expert", [(i, i ^ 1) for i in range(size)])


def swap_group(value):
    return lax.ppermute(value, "group", [(0, 1), (1, 0)])


def spread(blocks):
    size = lax.axis_size("expert")
    groups = [
        [start + core for y in range(2) for start in range(2 * y, size, 4)] for core in range(2)
    ]
    return lax.all_to_all(blocks, "expert", 0, 0, axis_index_groups=groups, tiled=True)


def exchange_plan(tokens, norm_gain, routes, route_scale, changed, stale, learner):
    experts = lax.axis_size("expert")
    chips = experts // 2
    row_count, width = tokens.shape[1], tokens.shape[2]
    half = chips * row_count
    steps_total = routes.shape[0]
    packed = width + table_width(experts, steps_total)
    gain = norm_gain[None]
    state_shape = ((row_count, width), jnp.float32)
    weight_bytes = 2 * sum(part.size for part in stale + learner)
    long = pl.CostEstimate(
        flops=1280 * weight_bytes, bytes_accessed=2 * weight_bytes, transcendentals=0
    )
    stale = stale + tuple(swap_core(part) for part in stale)
    learner = learner + tuple(swap_core(part) for part in learner)
    (scaled,) = on_vmem(first_kernel, (tokens[0],), [state_shape], cost=long)
    (blocks,) = on_vmem(
        functools.partial(pack_kernel, experts),
        (scaled, gain, routes, route_scale, changed),
        [((chips, row_count, packed), jnp.bfloat16)],
    )
    tables = spread(blocks).reshape(half, packed)
    rows, state = tables, tokens[0]
    for step in range(steps_total):
        if step == 0:
            (share,) = run_mlp([rows], stale, step, False, [jnp.bfloat16], learner[2:])
        else:
            state, blocks = on_vmem(
                next_kernel,
                (state, returned, gain),
                [state_shape, ((chips, row_count, width), jnp.bfloat16)],
            )
            rows = spread(blocks).reshape(half, width)
            (rows,) = on_vmem(join_kernel, (rows, tables), [((half, packed), jnp.bfloat16)])
            other = swap_group(rows)
            (old,) = run_mlp([rows], stale, step, False, [jnp.float32])
            other, old = lax.optimization_barrier((other, old))
            new, away = run_mlp([rows, other], learner, step, True, [jnp.float32, jnp.bfloat16])
            share = old + new + swap_group(away).astype(jnp.float32)
            share = share.astype(jnp.bfloat16)
        returned = spread(share.reshape(chips, row_count, width))
    (updated,) = on_vmem(last_kernel, (state, returned), [((row_count, width), jnp.bfloat16)])
    return updated[None]


def gather_plan(tokens, norm_gain, routes, route_scale, changed, stale, learner):
    experts = lax.axis_size("expert")
    owner_index = lax.axis_index("expert")
    row_count = tokens.shape[1]
    top_count = routes.shape[3]
    capacity = min(row_count, max(2, 2 * row_count * top_count // experts))
    is_fresh = jnp.any(changed[0] == owner_index)
    fresh = [lax.all_gather(part, "group", axis=0, tiled=True) for part in learner]
    newer = [jnp.where(is_fresh, new, old) for new, old in zip(fresh, stale)]
    state = tokens[0].astype(jnp.float32)
    buffer_ids = jnp.arange(experts * capacity, dtype=jnp.int32)
    expert_ids = jnp.arange(experts, dtype=jnp.int32)
    for step in range(routes.shape[0]):
        normed = normalize(state, norm_gain)
        chosen = routes[step, 0]
        weights = route_scale[step, 0]
        hits = (chosen.reshape(-1)[:, None] == expert_ids[None, :]).astype(jnp.int32)
        before = jnp.cumsum(hits, axis=0) - hits
        slot_pos = jnp.sum(before * hits, axis=1).reshape(chosen.shape)
        target = chosen * capacity + slot_pos
        placed = (target[:, :, None] == buffer_ids[None, None, :]).astype(jnp.float32)
        merge_weights = jnp.sum(placed * weights[:, :, None], axis=1)
        send_matrix = jnp.sum(placed, axis=1).astype(jnp.bfloat16)
        outgoing = lax.dot_general(
            send_matrix, normed, (((0,), (0,)), ((), ())), preferred_element_type=jnp.float32
        )
        outgoing = outgoing.astype(jnp.bfloat16).reshape(experts, capacity, -1)
        received = lax.all_to_all(outgoing, "expert", split_axis=0, concat_axis=0, tiled=True)
        flat = received.reshape(-1, received.shape[-1])
        result = expert_apply(flat, *(stale if step == 0 else newer))
        answer = result.astype(jnp.bfloat16).reshape(received.shape)
        returned = lax.all_to_all(answer, "expert", split_axis=0, concat_axis=0, tiled=True)
        flat_back = returned.reshape(experts * capacity, -1).astype(jnp.float32)
        state = state + jnp.dot(merge_weights, flat_back, precision=lax.Precision.HIGHEST)
    return state.astype(jnp.bfloat16)[None]


def local(
    tokens,
    norm_gain,
    routes,
    route_scale,
    changed,
    rollout_up,
    rollout_down,
    learner_up,
    learner_down,
):
    experts = lax.axis_size("expert")
    groups = lax.axis_size("group")
    fewer = tokens.shape[1] * experts < learner_up.shape[1]
    paired = experts % 4 == 0 and groups == 2
    plan = exchange_plan if fewer and paired else gather_plan
    stale = (rollout_up[0], rollout_down[0])
    learner = (learner_up[0], learner_down[0])
    return plan(tokens, norm_gain, routes, route_scale, changed, stale, learner)


def solution(mesh):
    placed = (
        P("group", "expert", None),
        P(),
        P(None, "group", "expert", None),
        P(None, "group", "expert", None),
        P("group", None),
        P("expert", None, None),
        P("expert", None, None),
        P("expert", "group", None),
        P("expert", "group", None),
    )
    return jax.shard_map(
        local, mesh=mesh, in_specs=placed, out_specs=P("group", "expert", None), check_vma=False
    )
```

```python
import functools
import jax
import jax.numpy as jnp
from jax import lax
from jax.experimental import pallas as pl
from jax.experimental.pallas import tpu as pltpu
from jax.sharding import PartitionSpec as P

LANES = 128
MATMUL_ROWS = 128
MIB = 1 << 20


def normalize(state, norm_gain):
    scale = lax.rsqrt(jnp.mean(state * state, axis=-1, keepdims=True) + 1e-06)
    return (state * scale * norm_gain).astype(jnp.bfloat16)


def expert_apply(inputs, up_rows, down_rows):
    pre_act = lax.dot_general(
        inputs, up_rows, (((1,), (1,)), ((), ())), preferred_element_type=jnp.float32
    )
    hidden = jax.nn.silu(pre_act).astype(jnp.bfloat16)
    return jnp.dot(hidden, down_rows, preferred_element_type=jnp.float32)


def table_width(experts, steps_total):
    sections = 2 + 4 * (steps_total - 1)
    return -(-sections * experts // LANES) * LANES


def first_section(step, fresh):
    return 0 if step == 0 else 4 * step - 2 + 2 * fresh


def weight_table(experts, chosen, weights, changed):
    steps_total, _, rows, top_count = chosen.shape
    shape = (rows, table_width(experts, steps_total))
    lane = lax.broadcasted_iota(jnp.int32, shape, 1)
    section, expert = lane // experts, lane % experts
    fresh = section < 0
    for i in range(changed.shape[1]):
        fresh = fresh | (expert == changed[:, i : i + 1])
    table = jnp.zeros(shape, jnp.float32)
    for step in range(steps_total):
        dense = jnp.zeros(shape, jnp.float32)
        for k in range(top_count):
            hit = chosen[step, 0, :, k : k + 1] == expert
            dense = jnp.where(hit, weights[step, 0, :, k : k + 1], dense)
        high = dense.astype(jnp.bfloat16).astype(jnp.float32)
        value = jnp.where(section % 2 == 0, high, dense - high)
        start = first_section(step, False)
        if step == 0:
            table = jnp.where(section < 2, value, table)
        else:
            old = jnp.where(fresh, 0.0, value)
            new = jnp.where(fresh, value, 0.0)
            table = jnp.where((section >= start) & (section < start + 2), old, table)
            table = jnp.where((section >= start + 2) & (section < start + 4), new, table)
    return table.astype(jnp.bfloat16)


def row_weights(experts, table, owner, step, fresh):
    lane = lax.broadcasted_iota(jnp.int32, table.shape, 1)
    section = lane // experts
    first = first_section(step, fresh)
    mine = (lane % experts == owner) & (section >= first) & (section < first + 2)
    return jnp.sum(jnp.where(mine, table.astype(jnp.float32), 0.0), axis=1, keepdims=True)


def first_kernel(tokens, out):
    state = tokens[...].astype(jnp.float32)
    out[...] = state * lax.rsqrt(jnp.mean(state * state, axis=-1, keepdims=True) + 1e-06)


def pack_kernel(experts, scaled, gain, routes, scales, changed, out):
    width = scaled.shape[1]
    normed = (scaled[...] * gain[...]).astype(jnp.bfloat16)
    table = weight_table(experts, routes, scales, changed)
    for chip in range(out.shape[0]):
        out[chip, :, :width] = normed
        out[chip, :, width:] = table


def sum_blocks(blocks):
    total = blocks[0].astype(jnp.float32)
    for chip in range(1, blocks.shape[0]):
        total = total + blocks[chip].astype(jnp.float32)
    return total


def next_kernel(previous, returned, gain, state_out, out):
    state = previous[...].astype(jnp.float32) + sum_blocks(returned)
    state_out[...] = state
    normed = normalize(state, gain[...])
    for chip in range(out.shape[0]):
        out[chip] = normed


def last_kernel(previous, returned, out):
    out[...] = (previous[...] + sum_blocks(returned)).astype(jnp.bfloat16)


def join_kernel(rows, tables, out):
    width = rows.shape[1]
    out[:, :width] = rows[...]
    out[:, width:] = tables[:, width:]


def mlp_kernel(experts, step, fresh, set_count, *refs):
    sources, refs = refs[:set_count], refs[set_count:]
    weights, outs = refs[:4], refs[4:]
    count, width = outs[0].shape
    rows = jnp.concatenate([source[:, :width] for source in sources], axis=0)
    table = jnp.concatenate([source[:, width:] for source in sources], axis=0)
    inputs = jnp.concatenate([rows] * max(1, MATMUL_ROWS // rows.shape[0]), axis=0)
    own = lax.axis_index("expert")
    total = None
    for core in range(2):
        up, down = weights[2 * core : 2 * core + 2]
        owner = own if core == 0 else own + 1 - 2 * lax.rem(own, 2)
        pre_act = lax.dot_general(
            inputs, up[...], (((1,), (1,)), ((), ())), preferred_element_type=jnp.float32
        )
        hidden = (pre_act / (1.0 + jnp.exp(-pre_act))).astype(jnp.bfloat16)
        result = jnp.dot(hidden, down[...], preferred_element_type=jnp.float32)
        result = result[: rows.shape[0]] * row_weights(experts, table, owner, step, fresh)
        total = result if total is None else total + result
    for i, out in enumerate(outs):
        out[...] = total[i * count : (i + 1) * count].astype(out.dtype)


def on_vmem(kernel, inputs, outputs, limit=4 * MIB, cost=None, after=()):
    in_vmem = pl.BlockSpec(memory_space=pltpu.VMEM)
    count = len(inputs)

    def body(*refs):
        kernel(*refs[:count], *refs[count + len(after) :])

    return pl.pallas_call(
        body,
        out_shape=[jax.ShapeDtypeStruct(shape, kind) for shape, kind in outputs],
        in_specs=[in_vmem] * count + [pl.BlockSpec(memory_space=pl.ANY)] * len(after),
        out_specs=[in_vmem] * len(outputs),
        compiler_params=pltpu.CompilerParams(vmem_limit_bytes=limit),
        cost_estimate=cost,
    )(*inputs, *after)


def run_mlp(row_sets, weights, step, fresh, out_types, after=()):
    count, width = row_sets[0].shape[0], weights[0].shape[1]
    size = sum(part.size for part in weights)
    cost = pl.CostEstimate(
        flops=4 * MATMUL_ROWS * size, bytes_accessed=4 * size, transcendentals=0
    )
    kernel = functools.partial(mlp_kernel, lax.axis_size("expert"), step, fresh, len(row_sets))
    outputs = [((count, width), out_type) for out_type in out_types]
    return on_vmem(kernel, tuple(row_sets) + tuple(weights), outputs, 8 * MIB, cost, after)


def swap_core(value):
    size = lax.axis_size("expert")
    return lax.ppermute(value, "expert", [(i, i ^ 1) for i in range(size)])


def swap_group(value):
    return lax.ppermute(value, "group", [(0, 1), (1, 0)])


def spread(blocks):
    size = lax.axis_size("expert")
    chips = [chip for y in range(2) for chip in range(y, size // 2, 2)]
    groups = [[2 * chip + (core ^ (4 * chip >= size)) for chip in chips] for core in range(2)]
    return lax.all_to_all(blocks, "expert", 0, 0, axis_index_groups=groups, tiled=True)


def exchange_plan(tokens, norm_gain, routes, route_scale, changed, stale, learner):
    experts = lax.axis_size("expert")
    chips = experts // 2
    row_count, width = tokens.shape[1], tokens.shape[2]
    half = chips * row_count
    steps_total = routes.shape[0]
    packed = width + table_width(experts, steps_total)
    gain = norm_gain[None]
    state_shape = ((row_count, width), jnp.float32)
    weight_bytes = 2 * sum(part.size for part in stale + learner)
    long = pl.CostEstimate(
        flops=1280 * weight_bytes, bytes_accessed=2 * weight_bytes, transcendentals=0
    )
    stale = stale + tuple(swap_core(part) for part in stale)
    learner = learner + tuple(swap_core(part) for part in learner)
    (scaled,) = on_vmem(first_kernel, (tokens[0],), [state_shape], cost=long)
    (blocks,) = on_vmem(
        functools.partial(pack_kernel, experts),
        (scaled, gain, routes, route_scale, changed),
        [((chips, row_count, packed), jnp.bfloat16)],
    )
    tables = spread(blocks).reshape(half, packed)
    rows, state = tables, tokens[0]
    for step in range(steps_total):
        if step == 0:
            (share,) = run_mlp([rows], stale, step, False, [jnp.bfloat16], learner[2:])
        else:
            state, blocks = on_vmem(
                next_kernel,
                (state, returned, gain),
                [state_shape, ((chips, row_count, width), jnp.bfloat16)],
            )
            rows = spread(blocks).reshape(half, width)
            (rows,) = on_vmem(join_kernel, (rows, tables), [((half, packed), jnp.bfloat16)])
            other = swap_group(rows)
            (old,) = run_mlp([rows], stale, step, False, [jnp.float32])
            other, old = lax.optimization_barrier((other, old))
            new, away = run_mlp([rows, other], learner, step, True, [jnp.float32, jnp.bfloat16])
            share = old + new + swap_group(away).astype(jnp.float32)
            share = share.astype(jnp.bfloat16)
        returned = spread(share.reshape(chips, row_count, width))
    (updated,) = on_vmem(last_kernel, (state, returned), [((row_count, width), jnp.bfloat16)])
    return updated[None]


def gather_plan(tokens, norm_gain, routes, route_scale, changed, stale, learner):
    experts = lax.axis_size("expert")
    owner_index = lax.axis_index("expert")
    row_count = tokens.shape[1]
    top_count = routes.shape[3]
    capacity = min(row_count, max(2, 2 * row_count * top_count // experts))
    is_fresh = jnp.any(changed[0] == owner_index)
    fresh = [lax.all_gather(part, "group", axis=0, tiled=True) for part in learner]
    newer = [jnp.where(is_fresh, new, old) for new, old in zip(fresh, stale)]
    state = tokens[0].astype(jnp.float32)
    buffer_ids = jnp.arange(experts * capacity, dtype=jnp.int32)
    expert_ids = jnp.arange(experts, dtype=jnp.int32)
    for step in range(routes.shape[0]):
        normed = normalize(state, norm_gain)
        chosen = routes[step, 0]
        weights = route_scale[step, 0]
        hits = (chosen.reshape(-1)[:, None] == expert_ids[None, :]).astype(jnp.int32)
        before = jnp.cumsum(hits, axis=0) - hits
        slot_pos = jnp.sum(before * hits, axis=1).reshape(chosen.shape)
        target = chosen * capacity + slot_pos
        placed = (target[:, :, None] == buffer_ids[None, None, :]).astype(jnp.float32)
        merge_weights = jnp.sum(placed * weights[:, :, None], axis=1)
        send_matrix = jnp.sum(placed, axis=1).astype(jnp.bfloat16)
        outgoing = lax.dot_general(
            send_matrix, normed, (((0,), (0,)), ((), ())), preferred_element_type=jnp.float32
        )
        outgoing = outgoing.astype(jnp.bfloat16).reshape(experts, capacity, -1)
        received = lax.all_to_all(outgoing, "expert", split_axis=0, concat_axis=0, tiled=True)
        flat = received.reshape(-1, received.shape[-1])
        result = expert_apply(flat, *(stale if step == 0 else newer))
        answer = result.astype(jnp.bfloat16).reshape(received.shape)
        returned = lax.all_to_all(answer, "expert", split_axis=0, concat_axis=0, tiled=True)
        flat_back = returned.reshape(experts * capacity, -1).astype(jnp.float32)
        state = state + jnp.dot(merge_weights, flat_back, precision=lax.Precision.HIGHEST)
    return state.astype(jnp.bfloat16)[None]


def local(
    tokens,
    norm_gain,
    routes,
    route_scale,
    changed,
    rollout_up,
    rollout_down,
    learner_up,
    learner_down,
):
    experts = lax.axis_size("expert")
    groups = lax.axis_size("group")
    fewer = tokens.shape[1] * experts < learner_up.shape[1]
    paired = experts % 4 == 0 and groups == 2
    plan = exchange_plan if fewer and paired else gather_plan
    stale = (rollout_up[0], rollout_down[0])
    learner = (learner_up[0], learner_down[0])
    return plan(tokens, norm_gain, routes, route_scale, changed, stale, learner)


def solution(mesh):
    placed = (
        P("group", "expert", None),
        P(),
        P(None, "group", "expert", None),
        P(None, "group", "expert", None),
        P("group", None),
        P("expert", None, None),
        P("expert", None, None),
        P("expert", "group", None),
        P("expert", "group", None),
    )
    return jax.shard_map(
        local, mesh=mesh, in_specs=placed, out_specs=P("group", "expert", None), check_vma=False
    )
```

```python
import functools
import jax
import jax.numpy as jnp
from jax import lax
from jax.experimental import pallas as pl
from jax.experimental.pallas import tpu as pltpu
from jax.sharding import PartitionSpec as P

LANES = 128
MATMUL_ROWS = 128
MIB = 1 << 20


def normalize(state, norm_gain):
    scale = lax.rsqrt(jnp.mean(state * state, axis=-1, keepdims=True) + 1e-06)
    return (state * scale * norm_gain).astype(jnp.bfloat16)


def expert_apply(inputs, up_rows, down_rows):
    pre_act = lax.dot_general(
        inputs, up_rows, (((1,), (1,)), ((), ())), preferred_element_type=jnp.float32
    )
    hidden = jax.nn.silu(pre_act).astype(jnp.bfloat16)
    return jnp.dot(hidden, down_rows, preferred_element_type=jnp.float32)


def table_width(experts, steps_total):
    sections = 2 + 4 * (steps_total - 1)
    return -(-sections * experts // LANES) * LANES


def first_section(step, fresh):
    return 0 if step == 0 else 4 * step - 2 + 2 * fresh


def lane_kernel(experts, section_out, expert_out):
    lane = lax.broadcasted_iota(jnp.int32, section_out.shape, 1)
    section_out[...] = lane // experts
    expert_out[...] = lane % experts


def weight_table(section, expert, chosen, weights, changed):
    steps_total, _, _, top_count = chosen.shape
    shape = section.shape
    fresh = section < 0
    for i in range(changed.shape[1]):
        fresh = fresh | (expert == changed[:, i : i + 1])
    table = jnp.zeros(shape, jnp.float32)
    for step in range(steps_total):
        dense = jnp.zeros(shape, jnp.float32)
        for k in range(top_count):
            hit = chosen[step, 0, :, k : k + 1] == expert
            dense = jnp.where(hit, weights[step, 0, :, k : k + 1], dense)
        high = dense.astype(jnp.bfloat16).astype(jnp.float32)
        value = jnp.where(section % 2 == 0, high, dense - high)
        start = first_section(step, False)
        if step == 0:
            table = jnp.where(section < 2, value, table)
        else:
            old = jnp.where(fresh, 0.0, value)
            new = jnp.where(fresh, value, 0.0)
            table = jnp.where((section >= start) & (section < start + 2), old, table)
            table = jnp.where((section >= start + 2) & (section < start + 4), new, table)
    return table.astype(jnp.bfloat16)


def row_weights(experts, table, owner, step, fresh):
    lane = lax.broadcasted_iota(jnp.int32, table.shape, 1)
    section = lane // experts
    first = first_section(step, fresh)
    mine = (lane % experts == owner) & (section >= first) & (section < first + 2)
    return jnp.sum(jnp.where(mine, table.astype(jnp.float32), 0.0), axis=1, keepdims=True)


def pack_kernel(section, expert, tokens, gain, routes, scales, changed, out):
    width = tokens.shape[1]
    normed = normalize(tokens[...].astype(jnp.float32), gain[...])
    table = weight_table(section[...], expert[...], routes, scales, changed)
    for chip in range(out.shape[0]):
        out[chip, :, :width] = normed
        out[chip, :, width:] = table


def sum_blocks(blocks):
    total = blocks[0].astype(jnp.float32)
    for chip in range(1, blocks.shape[0]):
        total = total + blocks[chip].astype(jnp.float32)
    return total


def next_kernel(previous, returned, gain, state_out, out):
    state = previous[...].astype(jnp.float32) + sum_blocks(returned)
    state_out[...] = state
    normed = normalize(state, gain[...])
    for chip in range(out.shape[0]):
        out[chip] = normed


def last_kernel(previous, returned, out):
    out[...] = (previous[...] + sum_blocks(returned)).astype(jnp.bfloat16)


def join_kernel(rows, tables, out):
    width = rows.shape[1]
    out[:, :width] = rows[...]
    out[:, width:] = tables[:, width:]


def mlp_kernel(experts, step, fresh, set_count, *refs):
    sources, refs = refs[:set_count], refs[set_count:]
    weights, outs = refs[:4], refs[4:]
    count, width = outs[0].shape
    rows = jnp.concatenate([source[:, :width] for source in sources], axis=0)
    table = jnp.concatenate([source[:, width:] for source in sources], axis=0)
    inputs = jnp.concatenate([rows] * max(1, MATMUL_ROWS // rows.shape[0]), axis=0)
    own = lax.axis_index("expert")
    total = None
    for core in range(2):
        up, down = weights[2 * core : 2 * core + 2]
        owner = own if core == 0 else own + 1 - 2 * lax.rem(own, 2)
        pre_act = lax.dot_general(
            inputs, up[...], (((1,), (1,)), ((), ())), preferred_element_type=jnp.float32
        )
        hidden = (pre_act / (1.0 + jnp.exp(-pre_act))).astype(jnp.bfloat16)
        result = jnp.dot(hidden, down[...], preferred_element_type=jnp.float32)
        result = result[: rows.shape[0]] * row_weights(experts, table, owner, step, fresh)
        total = result if total is None else total + result
    for i, out in enumerate(outs):
        out[...] = total[i * count : (i + 1) * count].astype(out.dtype)


def on_vmem(kernel, inputs, outputs, limit=4 * MIB, cost=None, after=()):
    in_vmem = pl.BlockSpec(memory_space=pltpu.VMEM)
    count = len(inputs)

    def body(*refs):
        kernel(*refs[:count], *refs[count + len(after) :])

    return pl.pallas_call(
        body,
        out_shape=[jax.ShapeDtypeStruct(shape, kind) for shape, kind in outputs],
        in_specs=[in_vmem] * count + [pl.BlockSpec(memory_space=pl.ANY)] * len(after),
        out_specs=[in_vmem] * len(outputs),
        compiler_params=pltpu.CompilerParams(vmem_limit_bytes=limit),
        cost_estimate=cost,
    )(*inputs, *after)


def run_mlp(row_sets, weights, step, fresh, out_types, after=()):
    count, width = row_sets[0].shape[0], weights[0].shape[1]
    size = sum(part.size for part in weights)
    cost = pl.CostEstimate(
        flops=4 * MATMUL_ROWS * size, bytes_accessed=4 * size, transcendentals=0
    )
    kernel = functools.partial(mlp_kernel, lax.axis_size("expert"), step, fresh, len(row_sets))
    outputs = [((count, width), out_type) for out_type in out_types]
    return on_vmem(kernel, tuple(row_sets) + tuple(weights), outputs, 8 * MIB, cost, after)


def swap_core(value):
    size = lax.axis_size("expert")
    return lax.ppermute(value, "expert", [(i, i ^ 1) for i in range(size)])


def swap_group(value):
    return lax.ppermute(value, "group", [(0, 1), (1, 0)])


def spread(blocks):
    size = lax.axis_size("expert")
    groups = [
        [start + core for y in range(2) for start in range(2 * y, size, 4)] for core in range(2)
    ]
    return lax.all_to_all(blocks, "expert", 0, 0, axis_index_groups=groups, tiled=True)


def exchange_plan(tokens, norm_gain, routes, route_scale, changed, stale, learner):
    experts = lax.axis_size("expert")
    chips = experts // 2
    row_count, width = tokens.shape[1], tokens.shape[2]
    half = chips * row_count
    steps_total = routes.shape[0]
    packed = width + table_width(experts, steps_total)
    gain = norm_gain[None]
    state_shape = ((row_count, width), jnp.float32)
    weight_bytes = 2 * sum(part.size for part in stale + learner)
    long = pl.CostEstimate(
        flops=1280 * weight_bytes, bytes_accessed=2 * weight_bytes, transcendentals=0
    )
    lanes = ((row_count, table_width(experts, steps_total)), jnp.int32)
    section, expert = on_vmem(
        functools.partial(lane_kernel, experts), (), [lanes, lanes], cost=long
    )
    stale = stale + tuple(swap_core(part) for part in stale)
    learner = learner + tuple(swap_core(part) for part in learner)
    (blocks,) = on_vmem(
        pack_kernel,
        (section, expert, tokens[0], gain, routes, route_scale, changed),
        [((chips, row_count, packed), jnp.bfloat16)],
    )
    tables = spread(blocks).reshape(half, packed)
    rows, state = tables, tokens[0]
    for step in range(steps_total):
        if step == 0:
            (share,) = run_mlp([rows], stale, step, False, [jnp.bfloat16], learner[2:])
        else:
            state, blocks = on_vmem(
                next_kernel,
                (state, returned, gain),
                [state_shape, ((chips, row_count, width), jnp.bfloat16)],
            )
            rows = spread(blocks).reshape(half, width)
            (rows,) = on_vmem(join_kernel, (rows, tables), [((half, packed), jnp.bfloat16)])
            other = swap_group(rows)
            (old,) = run_mlp([rows], stale, step, False, [jnp.float32])
            other, old = lax.optimization_barrier((other, old))
            new, away = run_mlp([rows, other], learner, step, True, [jnp.float32, jnp.bfloat16])
            share = old + new + swap_group(away).astype(jnp.float32)
            share = share.astype(jnp.bfloat16)
        returned = spread(share.reshape(chips, row_count, width))
    (updated,) = on_vmem(last_kernel, (state, returned), [((row_count, width), jnp.bfloat16)])
    return updated[None]


def gather_plan(tokens, norm_gain, routes, route_scale, changed, stale, learner):
    experts = lax.axis_size("expert")
    owner_index = lax.axis_index("expert")
    row_count = tokens.shape[1]
    top_count = routes.shape[3]
    capacity = min(row_count, max(2, 2 * row_count * top_count // experts))
    is_fresh = jnp.any(changed[0] == owner_index)
    fresh = [lax.all_gather(part, "group", axis=0, tiled=True) for part in learner]
    newer = [jnp.where(is_fresh, new, old) for new, old in zip(fresh, stale)]
    state = tokens[0].astype(jnp.float32)
    buffer_ids = jnp.arange(experts * capacity, dtype=jnp.int32)
    expert_ids = jnp.arange(experts, dtype=jnp.int32)
    for step in range(routes.shape[0]):
        normed = normalize(state, norm_gain)
        chosen = routes[step, 0]
        weights = route_scale[step, 0]
        hits = (chosen.reshape(-1)[:, None] == expert_ids[None, :]).astype(jnp.int32)
        before = jnp.cumsum(hits, axis=0) - hits
        slot_pos = jnp.sum(before * hits, axis=1).reshape(chosen.shape)
        target = chosen * capacity + slot_pos
        placed = (target[:, :, None] == buffer_ids[None, None, :]).astype(jnp.float32)
        merge_weights = jnp.sum(placed * weights[:, :, None], axis=1)
        send_matrix = jnp.sum(placed, axis=1).astype(jnp.bfloat16)
        outgoing = lax.dot_general(
            send_matrix, normed, (((0,), (0,)), ((), ())), preferred_element_type=jnp.float32
        )
        outgoing = outgoing.astype(jnp.bfloat16).reshape(experts, capacity, -1)
        received = lax.all_to_all(outgoing, "expert", split_axis=0, concat_axis=0, tiled=True)
        flat = received.reshape(-1, received.shape[-1])
        result = expert_apply(flat, *(stale if step == 0 else newer))
        answer = result.astype(jnp.bfloat16).reshape(received.shape)
        returned = lax.all_to_all(answer, "expert", split_axis=0, concat_axis=0, tiled=True)
        flat_back = returned.reshape(experts * capacity, -1).astype(jnp.float32)
        state = state + jnp.dot(merge_weights, flat_back, precision=lax.Precision.HIGHEST)
    return state.astype(jnp.bfloat16)[None]


def local(
    tokens,
    norm_gain,
    routes,
    route_scale,
    changed,
    rollout_up,
    rollout_down,
    learner_up,
    learner_down,
):
    experts = lax.axis_size("expert")
    groups = lax.axis_size("group")
    fewer = tokens.shape[1] * experts < learner_up.shape[1]
    paired = experts % 4 == 0 and groups == 2
    plan = exchange_plan if fewer and paired else gather_plan
    stale = (rollout_up[0], rollout_down[0])
    learner = (learner_up[0], learner_down[0])
    return plan(tokens, norm_gain, routes, route_scale, changed, stale, learner)


def solution(mesh):
    placed = (
        P("group", "expert", None),
        P(),
        P(None, "group", "expert", None),
        P(None, "group", "expert", None),
        P("group", None),
        P("expert", None, None),
        P("expert", None, None),
        P("expert", "group", None),
        P("expert", "group", None),
    )
    return jax.shard_map(
        local, mesh=mesh, in_specs=placed, out_specs=P("group", "expert", None), check_vma=False
    )
```

```python
import functools
import jax
import jax.numpy as jnp
from jax import lax
from jax.experimental import pallas as pl
from jax.experimental.pallas import tpu as pltpu
from jax.sharding import PartitionSpec as P

LANES = 128
MATMUL_ROWS = 128
MIB = 1 << 20


def normalize(state, norm_gain):
    scale = lax.rsqrt(jnp.mean(state * state, axis=-1, keepdims=True) + 1e-06)
    return (state * scale * norm_gain).astype(jnp.bfloat16)


def expert_apply(inputs, up_rows, down_rows):
    pre_act = lax.dot_general(
        inputs, up_rows, (((1,), (1,)), ((), ())), preferred_element_type=jnp.float32
    )
    hidden = jax.nn.silu(pre_act).astype(jnp.bfloat16)
    return jnp.dot(hidden, down_rows, preferred_element_type=jnp.float32)


def table_width(experts, steps_total):
    sections = 2 + 4 * (steps_total - 1)
    return -(-sections * experts // LANES) * LANES


def first_section(step, fresh):
    return 0 if step == 0 else 4 * step - 2 + 2 * fresh


def lane_kernel(experts, section_out, expert_out):
    lane = lax.broadcasted_iota(jnp.int32, section_out.shape, 1)
    section_out[...] = lane // experts
    expert_out[...] = lane % experts


def weight_table(section, expert, chosen, weights, changed):
    steps_total, _, _, top_count = chosen.shape
    shape = section.shape
    fresh = section < 0
    for i in range(changed.shape[1]):
        fresh = fresh | (expert == changed[:, i : i + 1])
    table = jnp.zeros(shape, jnp.float32)
    for step in range(steps_total):
        dense = jnp.zeros(shape, jnp.float32)
        for k in range(top_count):
            hit = chosen[step, 0, :, k : k + 1] == expert
            dense = jnp.where(hit, weights[step, 0, :, k : k + 1], dense)
        high = dense.astype(jnp.bfloat16).astype(jnp.float32)
        value = jnp.where(section % 2 == 0, high, dense - high)
        start = first_section(step, False)
        if step == 0:
            table = jnp.where(section < 2, value, table)
        else:
            old = jnp.where(fresh, 0.0, value)
            new = jnp.where(fresh, value, 0.0)
            table = jnp.where((section >= start) & (section < start + 2), old, table)
            table = jnp.where((section >= start + 2) & (section < start + 4), new, table)
    return table.astype(jnp.bfloat16)


def row_weights(experts, table, owner, step, fresh):
    lane = lax.broadcasted_iota(jnp.int32, table.shape, 1)
    section = lane // experts
    first = first_section(step, fresh)
    mine = (lane % experts == owner) & (section >= first) & (section < first + 2)
    return jnp.sum(jnp.where(mine, table.astype(jnp.float32), 0.0), axis=1, keepdims=True)


def pack_kernel(section, expert, tokens, gain, routes, scales, changed, out):
    width = tokens.shape[1]
    normed = normalize(tokens[...].astype(jnp.float32), gain[...])
    table = weight_table(section[...], expert[...], routes, scales, changed)
    for chip in range(out.shape[0]):
        out[chip, :, :width] = normed
        out[chip, :, width:] = table


def sum_blocks(blocks):
    total = blocks[0].astype(jnp.float32)
    for chip in range(1, blocks.shape[0]):
        total = total + blocks[chip].astype(jnp.float32)
    return total


def next_kernel(previous, returned, gain, state_out, out):
    state = previous[...].astype(jnp.float32) + sum_blocks(returned)
    state_out[...] = state
    normed = normalize(state, gain[...])
    for chip in range(out.shape[0]):
        out[chip] = normed


def last_kernel(previous, returned, out):
    out[...] = (previous[...] + sum_blocks(returned)).astype(jnp.bfloat16)


def join_kernel(rows, tables, out):
    width = rows.shape[1]
    out[:, :width] = rows[...]
    out[:, width:] = tables[:, width:]


def mlp_kernel(experts, step, fresh, set_count, *refs):
    sources, refs = refs[:set_count], refs[set_count:]
    weights, outs = refs[:4], refs[4:]
    count, width = outs[0].shape
    rows = jnp.concatenate([source[:, :width] for source in sources], axis=0)
    table = jnp.concatenate([source[:, width:] for source in sources], axis=0)
    inputs = jnp.concatenate([rows] * max(1, MATMUL_ROWS // rows.shape[0]), axis=0)
    own = lax.axis_index("expert")
    total = None
    for core in range(2):
        up, down = weights[2 * core : 2 * core + 2]
        owner = own if core == 0 else own + 1 - 2 * lax.rem(own, 2)
        pre_act = lax.dot_general(
            inputs, up[...], (((1,), (1,)), ((), ())), preferred_element_type=jnp.float32
        )
        hidden = (pre_act / (1.0 + jnp.exp(-pre_act))).astype(jnp.bfloat16)
        result = jnp.dot(hidden, down[...], preferred_element_type=jnp.float32)
        result = result[: rows.shape[0]] * row_weights(experts, table, owner, step, fresh)
        total = result if total is None else total + result
    for i, out in enumerate(outs):
        out[...] = total[i * count : (i + 1) * count].astype(out.dtype)


def on_vmem(kernel, inputs, outputs, limit=4 * MIB, cost=None, after=()):
    in_vmem = pl.BlockSpec(memory_space=pltpu.VMEM)
    count = len(inputs)

    def body(*refs):
        kernel(*refs[:count], *refs[count + len(after) :])

    return pl.pallas_call(
        body,
        out_shape=[jax.ShapeDtypeStruct(shape, kind) for shape, kind in outputs],
        in_specs=[in_vmem] * count + [pl.BlockSpec(memory_space=pl.ANY)] * len(after),
        out_specs=[in_vmem] * len(outputs),
        compiler_params=pltpu.CompilerParams(vmem_limit_bytes=limit),
        cost_estimate=cost,
    )(*inputs, *after)


def run_mlp(row_sets, weights, step, fresh, out_types, after=()):
    count, width = row_sets[0].shape[0], weights[0].shape[1]
    size = sum(part.size for part in weights)
    cost = pl.CostEstimate(
        flops=4 * MATMUL_ROWS * size, bytes_accessed=4 * size, transcendentals=0
    )
    kernel = functools.partial(mlp_kernel, lax.axis_size("expert"), step, fresh, len(row_sets))
    outputs = [((count, width), out_type) for out_type in out_types]
    return on_vmem(kernel, tuple(row_sets) + tuple(weights), outputs, 8 * MIB, cost, after)


def swap_core(value):
    size = lax.axis_size("expert")
    return lax.ppermute(value, "expert", [(i, i ^ 1) for i in range(size)])


def swap_group(value):
    return lax.ppermute(value, "group", [(0, 1), (1, 0)])


def hop_group(value):
    size = lax.axis_size("expert")
    pairs = [(i, i ^ size) for i in range(1, 2 * size, 2)]
    return lax.ppermute(value, ("group", "expert"), pairs)


def spread(blocks):
    size = lax.axis_size("expert")
    groups = [
        [start + core for y in range(2) for start in range(2 * y, size, 4)] for core in range(2)
    ]
    return lax.all_to_all(blocks, "expert", 0, 0, axis_index_groups=groups, tiled=True)


def exchange_plan(tokens, norm_gain, routes, route_scale, changed, stale, learner):
    experts = lax.axis_size("expert")
    chips = experts // 2
    row_count, width = tokens.shape[1], tokens.shape[2]
    half = chips * row_count
    steps_total = routes.shape[0]
    packed = width + table_width(experts, steps_total)
    gain = norm_gain[None]
    state_shape = ((row_count, width), jnp.float32)
    weight_bytes = 2 * sum(part.size for part in stale + learner)
    long = pl.CostEstimate(
        flops=1280 * weight_bytes, bytes_accessed=2 * weight_bytes, transcendentals=0
    )
    lanes = ((row_count, table_width(experts, steps_total)), jnp.int32)
    section, expert = on_vmem(
        functools.partial(lane_kernel, experts), (), [lanes, lanes], cost=long
    )
    stale = stale + tuple(swap_core(part) for part in stale)
    learner = learner + tuple(swap_core(part) for part in learner)
    turn = hop_group(section.astype(jnp.bfloat16))
    (blocks,) = on_vmem(
        pack_kernel,
        (section, expert, tokens[0], gain, routes, route_scale, changed),
        [((chips, row_count, packed), jnp.bfloat16)],
        after=(turn,),
    )
    tables = spread(blocks).reshape(half, packed)
    rows, state = tables, tokens[0]
    for step in range(steps_total):
        if step == 0:
            (share,) = run_mlp([rows], stale, step, False, [jnp.bfloat16], learner[2:])
        else:
            state, blocks = on_vmem(
                next_kernel,
                (state, returned, gain),
                [state_shape, ((chips, row_count, width), jnp.bfloat16)],
            )
            rows = spread(blocks).reshape(half, width)
            (rows,) = on_vmem(join_kernel, (rows, tables), [((half, packed), jnp.bfloat16)])
            other = swap_group(rows)
            (old,) = run_mlp([rows], stale, step, False, [jnp.float32])
            other, old = lax.optimization_barrier((other, old))
            new, away = run_mlp([rows, other], learner, step, True, [jnp.float32, jnp.bfloat16])
            share = old + new + swap_group(away).astype(jnp.float32)
            share = share.astype(jnp.bfloat16)
        returned = spread(share.reshape(chips, row_count, width))
    (updated,) = on_vmem(last_kernel, (state, returned), [((row_count, width), jnp.bfloat16)])
    return updated[None]


def gather_plan(tokens, norm_gain, routes, route_scale, changed, stale, learner):
    experts = lax.axis_size("expert")
    owner_index = lax.axis_index("expert")
    row_count = tokens.shape[1]
    top_count = routes.shape[3]
    capacity = min(row_count, max(2, 2 * row_count * top_count // experts))
    is_fresh = jnp.any(changed[0] == owner_index)
    fresh = [lax.all_gather(part, "group", axis=0, tiled=True) for part in learner]
    newer = [jnp.where(is_fresh, new, old) for new, old in zip(fresh, stale)]
    state = tokens[0].astype(jnp.float32)
    buffer_ids = jnp.arange(experts * capacity, dtype=jnp.int32)
    expert_ids = jnp.arange(experts, dtype=jnp.int32)
    for step in range(routes.shape[0]):
        normed = normalize(state, norm_gain)
        chosen = routes[step, 0]
        weights = route_scale[step, 0]
        hits = (chosen.reshape(-1)[:, None] == expert_ids[None, :]).astype(jnp.int32)
        before = jnp.cumsum(hits, axis=0) - hits
        slot_pos = jnp.sum(before * hits, axis=1).reshape(chosen.shape)
        target = chosen * capacity + slot_pos
        placed = (target[:, :, None] == buffer_ids[None, None, :]).astype(jnp.float32)
        merge_weights = jnp.sum(placed * weights[:, :, None], axis=1)
        send_matrix = jnp.sum(placed, axis=1).astype(jnp.bfloat16)
        outgoing = lax.dot_general(
            send_matrix, normed, (((0,), (0,)), ((), ())), preferred_element_type=jnp.float32
        )
        outgoing = outgoing.astype(jnp.bfloat16).reshape(experts, capacity, -1)
        received = lax.all_to_all(outgoing, "expert", split_axis=0, concat_axis=0, tiled=True)
        flat = received.reshape(-1, received.shape[-1])
        result = expert_apply(flat, *(stale if step == 0 else newer))
        answer = result.astype(jnp.bfloat16).reshape(received.shape)
        returned = lax.all_to_all(answer, "expert", split_axis=0, concat_axis=0, tiled=True)
        flat_back = returned.reshape(experts * capacity, -1).astype(jnp.float32)
        state = state + jnp.dot(merge_weights, flat_back, precision=lax.Precision.HIGHEST)
    return state.astype(jnp.bfloat16)[None]


def local(
    tokens,
    norm_gain,
    routes,
    route_scale,
    changed,
    rollout_up,
    rollout_down,
    learner_up,
    learner_down,
):
    experts = lax.axis_size("expert")
    groups = lax.axis_size("group")
    fewer = tokens.shape[1] * experts < learner_up.shape[1]
    paired = experts % 4 == 0 and groups == 2
    plan = exchange_plan if fewer and paired else gather_plan
    stale = (rollout_up[0], rollout_down[0])
    learner = (learner_up[0], learner_down[0])
    return plan(tokens, norm_gain, routes, route_scale, changed, stale, learner)


def solution(mesh):
    placed = (
        P("group", "expert", None),
        P(),
        P(None, "group", "expert", None),
        P(None, "group", "expert", None),
        P("group", None),
        P("expert", None, None),
        P("expert", None, None),
        P("expert", "group", None),
        P("expert", "group", None),
    )
    return jax.shard_map(
        local, mesh=mesh, in_specs=placed, out_specs=P("group", "expert", None), check_vma=False
    )
```

```python
import functools
import jax
import jax.numpy as jnp
from jax import lax
from jax.experimental import pallas as pl
from jax.experimental.pallas import tpu as pltpu
from jax.sharding import PartitionSpec as P

LANES = 128
MATMUL_ROWS = 128
MIB = 1 << 20


def normalize(state, norm_gain):
    scale = lax.rsqrt(jnp.mean(state * state, axis=-1, keepdims=True) + 1e-06)
    return (state * scale * norm_gain).astype(jnp.bfloat16)


def expert_apply(inputs, up_rows, down_rows):
    pre_act = lax.dot_general(
        inputs, up_rows, (((1,), (1,)), ((), ())), preferred_element_type=jnp.float32
    )
    hidden = jax.nn.silu(pre_act).astype(jnp.bfloat16)
    return jnp.dot(hidden, down_rows, preferred_element_type=jnp.float32)


def table_width(experts, steps_total):
    sections = 2 + 4 * (steps_total - 1)
    return -(-sections * experts // LANES) * LANES


def first_section(step, fresh):
    return 0 if step == 0 else 4 * step - 2 + 2 * fresh


def lane_kernel(experts, section_out, expert_out):
    lane = lax.broadcasted_iota(jnp.int32, section_out.shape, 1)
    section_out[...] = lane // experts
    expert_out[...] = lane % experts


def weight_table(section, expert, chosen, weights, changed):
    steps_total, _, _, top_count = chosen.shape
    shape = section.shape
    fresh = section < 0
    for i in range(changed.shape[1]):
        fresh = fresh | (expert == changed[:, i : i + 1])
    table = jnp.zeros(shape, jnp.float32)
    for step in range(steps_total):
        dense = jnp.zeros(shape, jnp.float32)
        for k in range(top_count):
            hit = chosen[step, 0, :, k : k + 1] == expert
            dense = jnp.where(hit, weights[step, 0, :, k : k + 1], dense)
        high = dense.astype(jnp.bfloat16).astype(jnp.float32)
        value = jnp.where(section % 2 == 0, high, dense - high)
        start = first_section(step, False)
        if step == 0:
            table = jnp.where(section < 2, value, table)
        else:
            old = jnp.where(fresh, 0.0, value)
            new = jnp.where(fresh, value, 0.0)
            table = jnp.where((section >= start) & (section < start + 2), old, table)
            table = jnp.where((section >= start + 2) & (section < start + 4), new, table)
    return table.astype(jnp.bfloat16)


def row_weights(experts, table, owner, step, fresh):
    lane = lax.broadcasted_iota(jnp.int32, table.shape, 1)
    section = lane // experts
    first = first_section(step, fresh)
    mine = (lane % experts == owner) & (section >= first) & (section < first + 2)
    return jnp.sum(jnp.where(mine, table.astype(jnp.float32), 0.0), axis=1, keepdims=True)


def pack_kernel(section, expert, tokens, gain, routes, scales, changed, out):
    width = tokens.shape[1]
    normed = normalize(tokens[...].astype(jnp.float32), gain[...])
    table = weight_table(section[...], expert[...], routes, scales, changed)
    for chip in range(out.shape[0]):
        out[chip, :, :width] = normed
        out[chip, :, width:] = table


def sum_blocks(blocks):
    total = blocks[0].astype(jnp.float32)
    for chip in range(1, blocks.shape[0]):
        total = total + blocks[chip].astype(jnp.float32)
    return total


def next_kernel(previous, returned, gain, state_out, out):
    state = previous[...].astype(jnp.float32) + sum_blocks(returned)
    state_out[...] = state
    normed = normalize(state, gain[...])
    for chip in range(out.shape[0]):
        out[chip] = normed


def last_kernel(previous, returned, out):
    out[...] = (previous[...] + sum_blocks(returned)).astype(jnp.bfloat16)


def join_kernel(rows, tables, out):
    width = rows.shape[1]
    out[:, :width] = rows[...]
    out[:, width:] = tables[:, width:]


def weighted_outputs(experts, step, fresh, sources, weights, width):
    rows = jnp.concatenate([source[:, :width] for source in sources], axis=0)
    table = jnp.concatenate([source[:, width:] for source in sources], axis=0)
    inputs = jnp.concatenate([rows] * max(1, MATMUL_ROWS // rows.shape[0]), axis=0)
    own = lax.axis_index("expert")
    total = None
    for core in range(2):
        up, down = weights[2 * core : 2 * core + 2]
        owner = own if core == 0 else own + 1 - 2 * lax.rem(own, 2)
        pre_act = lax.dot_general(
            inputs, up[...], (((1,), (1,)), ((), ())), preferred_element_type=jnp.float32
        )
        hidden = (pre_act / (1.0 + jnp.exp(-pre_act))).astype(jnp.bfloat16)
        result = jnp.dot(hidden, down[...], preferred_element_type=jnp.float32)
        result = result[: rows.shape[0]] * row_weights(experts, table, owner, step, fresh)
        total = result if total is None else total + result
    return total


def stale_kernel(experts, step, rows, *refs):
    weights, out = refs[:4], refs[4]
    total = weighted_outputs(experts, step, False, [rows], weights, out.shape[1])
    out[...] = total.astype(out.dtype)


def fresh_kernel(experts, step, rows, other, *refs):
    weights, old, out = refs[:4], refs[4], refs[5]
    _, count, width = out.shape
    total = weighted_outputs(experts, step, True, [rows, other], weights, width)
    group = lax.axis_index("group")
    out[group] = (old[...] + total[:count]).astype(out.dtype)
    out[1 - group] = total[count:].astype(out.dtype)


def on_vmem(kernel, inputs, outputs, limit=4 * MIB, cost=None, after=()):
    in_vmem = pl.BlockSpec(memory_space=pltpu.VMEM)
    count = len(inputs)

    def body(*refs):
        kernel(*refs[:count], *refs[count + len(after) :])

    return pl.pallas_call(
        body,
        out_shape=[jax.ShapeDtypeStruct(shape, kind) for shape, kind in outputs],
        in_specs=[in_vmem] * count + [pl.BlockSpec(memory_space=pl.ANY)] * len(after),
        out_specs=[in_vmem] * len(outputs),
        compiler_params=pltpu.CompilerParams(vmem_limit_bytes=limit),
        cost_estimate=cost,
    )(*inputs, *after)


def run_mlp(kernel, step, row_sets, weights, output, before=(), after=()):
    size = sum(part.size for part in weights)
    cost = pl.CostEstimate(
        flops=4 * MATMUL_ROWS * size, bytes_accessed=4 * size, transcendentals=0
    )
    kernel = functools.partial(kernel, lax.axis_size("expert"), step)
    inputs = tuple(row_sets) + tuple(weights) + tuple(before)
    return on_vmem(kernel, inputs, [output], 8 * MIB, cost, after)[0]


def swap_core(value):
    size = lax.axis_size("expert")
    return lax.ppermute(value, "expert", [(i, i ^ 1) for i in range(size)])


def swap_group(value):
    return lax.ppermute(value, "group", [(0, 1), (1, 0)])


def spread(blocks):
    size = lax.axis_size("expert")
    groups = [
        [start + core for y in range(2) for start in range(2 * y, size, 4)] for core in range(2)
    ]
    return lax.all_to_all(blocks, "expert", 0, 0, axis_index_groups=groups, tiled=True)


def spread_groups(blocks):
    size = lax.axis_size("expert")
    groups = [
        [
            group * size + start + core
            for group in range(2)
            for y in range(2)
            for start in range(2 * y, size, 4)
        ]
        for core in range(2)
    ]
    axes = ("group", "expert")
    return lax.all_to_all(blocks, axes, 0, 0, axis_index_groups=groups, tiled=True)


def exchange_plan(tokens, norm_gain, routes, route_scale, changed, stale, learner):
    experts = lax.axis_size("expert")
    chips = experts // 2
    row_count, width = tokens.shape[1], tokens.shape[2]
    half = chips * row_count
    steps_total = routes.shape[0]
    packed = width + table_width(experts, steps_total)
    gain = norm_gain[None]
    state_shape = ((row_count, width), jnp.float32)
    weight_bytes = 2 * sum(part.size for part in stale + learner)
    long = pl.CostEstimate(
        flops=1280 * weight_bytes, bytes_accessed=2 * weight_bytes, transcendentals=0
    )
    lanes = ((row_count, table_width(experts, steps_total)), jnp.int32)
    section, expert = on_vmem(
        functools.partial(lane_kernel, experts), (), [lanes, lanes], cost=long
    )
    stale = stale + tuple(swap_core(part) for part in stale)
    learner = learner + tuple(swap_core(part) for part in learner)
    (blocks,) = on_vmem(
        pack_kernel,
        (section, expert, tokens[0], gain, routes, route_scale, changed),
        [((chips, row_count, packed), jnp.bfloat16)],
    )
    tables = spread(blocks).reshape(half, packed)
    rows, state = tables, tokens[0]
    for step in range(steps_total):
        if step == 0:
            output = ((half, width), jnp.bfloat16)
            share = run_mlp(stale_kernel, step, [rows], stale, output, after=learner[2:])
            returned = spread(share.reshape(chips, row_count, width))
        else:
            state, blocks = on_vmem(
                next_kernel,
                (state, returned, gain),
                [state_shape, ((chips, row_count, width), jnp.bfloat16)],
            )
            rows = spread(blocks).reshape(half, width)
            (rows,) = on_vmem(join_kernel, (rows, tables), [((half, packed), jnp.bfloat16)])
            other = swap_group(rows)
            old = run_mlp(stale_kernel, step, [rows], stale, ((half, width), jnp.float32))
            other, old = lax.optimization_barrier((other, old))
            output = ((2, half, width), jnp.bfloat16)
            share = run_mlp(fresh_kernel, step, [rows, other], learner, output, (old,))
            returned = spread_groups(share.reshape(2 * chips, row_count, width))
    (updated,) = on_vmem(last_kernel, (state, returned), [((row_count, width), jnp.bfloat16)])
    return updated[None]


def gather_plan(tokens, norm_gain, routes, route_scale, changed, stale, learner):
    experts = lax.axis_size("expert")
    owner_index = lax.axis_index("expert")
    row_count = tokens.shape[1]
    top_count = routes.shape[3]
    capacity = min(row_count, max(2, 2 * row_count * top_count // experts))
    is_fresh = jnp.any(changed[0] == owner_index)
    fresh = [lax.all_gather(part, "group", axis=0, tiled=True) for part in learner]
    newer = [jnp.where(is_fresh, new, old) for new, old in zip(fresh, stale)]
    state = tokens[0].astype(jnp.float32)
    buffer_ids = jnp.arange(experts * capacity, dtype=jnp.int32)
    expert_ids = jnp.arange(experts, dtype=jnp.int32)
    for step in range(routes.shape[0]):
        normed = normalize(state, norm_gain)
        chosen = routes[step, 0]
        weights = route_scale[step, 0]
        hits = (chosen.reshape(-1)[:, None] == expert_ids[None, :]).astype(jnp.int32)
        before = jnp.cumsum(hits, axis=0) - hits
        slot_pos = jnp.sum(before * hits, axis=1).reshape(chosen.shape)
        target = chosen * capacity + slot_pos
        placed = (target[:, :, None] == buffer_ids[None, None, :]).astype(jnp.float32)
        merge_weights = jnp.sum(placed * weights[:, :, None], axis=1)
        send_matrix = jnp.sum(placed, axis=1).astype(jnp.bfloat16)
        outgoing = lax.dot_general(
            send_matrix, normed, (((0,), (0,)), ((), ())), preferred_element_type=jnp.float32
        )
        outgoing = outgoing.astype(jnp.bfloat16).reshape(experts, capacity, -1)
        received = lax.all_to_all(outgoing, "expert", split_axis=0, concat_axis=0, tiled=True)
        flat = received.reshape(-1, received.shape[-1])
        result = expert_apply(flat, *(stale if step == 0 else newer))
        answer = result.astype(jnp.bfloat16).reshape(received.shape)
        returned = lax.all_to_all(answer, "expert", split_axis=0, concat_axis=0, tiled=True)
        flat_back = returned.reshape(experts * capacity, -1).astype(jnp.float32)
        state = state + jnp.dot(merge_weights, flat_back, precision=lax.Precision.HIGHEST)
    return state.astype(jnp.bfloat16)[None]


def local(
    tokens,
    norm_gain,
    routes,
    route_scale,
    changed,
    rollout_up,
    rollout_down,
    learner_up,
    learner_down,
):
    experts = lax.axis_size("expert")
    groups = lax.axis_size("group")
    fewer = tokens.shape[1] * experts < learner_up.shape[1]
    paired = experts % 4 == 0 and groups == 2
    plan = exchange_plan if fewer and paired else gather_plan
    stale = (rollout_up[0], rollout_down[0])
    learner = (learner_up[0], learner_down[0])
    return plan(tokens, norm_gain, routes, route_scale, changed, stale, learner)


def solution(mesh):
    placed = (
        P("group", "expert", None),
        P(),
        P(None, "group", "expert", None),
        P(None, "group", "expert", None),
        P("group", None),
        P("expert", None, None),
        P("expert", None, None),
        P("expert", "group", None),
        P("expert", "group", None),
    )
    return jax.shard_map(
        local, mesh=mesh, in_specs=placed, out_specs=P("group", "expert", None), check_vma=False
    )
```

```python
import functools
import jax
import jax.numpy as jnp
from jax import lax
from jax.experimental import pallas as pl
from jax.experimental.pallas import tpu as pltpu
from jax.sharding import PartitionSpec as P

LANES = 128
MATMUL_ROWS = 128
MIB = 1 << 20


def normalize(state, norm_gain):
    scale = lax.rsqrt(jnp.mean(state * state, axis=-1, keepdims=True) + 1e-06)
    return (state * scale * norm_gain).astype(jnp.bfloat16)


def expert_apply(inputs, up_rows, down_rows):
    pre_act = lax.dot_general(
        inputs, up_rows, (((1,), (1,)), ((), ())), preferred_element_type=jnp.float32
    )
    hidden = jax.nn.silu(pre_act).astype(jnp.bfloat16)
    return jnp.dot(hidden, down_rows, preferred_element_type=jnp.float32)


def table_width(experts, steps_total):
    sections = 2 + 4 * (steps_total - 1)
    return -(-sections * experts // LANES) * LANES


def first_section(step, fresh):
    return 0 if step == 0 else 4 * step - 2 + 2 * fresh


def lane_kernel(experts, section_out, expert_out):
    lane = lax.broadcasted_iota(jnp.int32, section_out.shape, 1)
    section_out[...] = lane // experts
    expert_out[...] = lane % experts


def weight_table(section, expert, chosen, weights, changed):
    steps_total, _, _, top_count = chosen.shape
    shape = section.shape
    fresh = section < 0
    for i in range(changed.shape[1]):
        fresh = fresh | (expert == changed[:, i : i + 1])
    table = jnp.zeros(shape, jnp.float32)
    for step in range(steps_total):
        dense = jnp.zeros(shape, jnp.float32)
        for k in range(top_count):
            hit = chosen[step, 0, :, k : k + 1] == expert
            dense = jnp.where(hit, weights[step, 0, :, k : k + 1], dense)
        high = dense.astype(jnp.bfloat16).astype(jnp.float32)
        value = jnp.where(section % 2 == 0, high, dense - high)
        start = first_section(step, False)
        if step == 0:
            table = jnp.where(section < 2, value, table)
        else:
            old = jnp.where(fresh, 0.0, value)
            new = jnp.where(fresh, value, 0.0)
            table = jnp.where((section >= start) & (section < start + 2), old, table)
            table = jnp.where((section >= start + 2) & (section < start + 4), new, table)
    return table.astype(jnp.bfloat16)


def row_weights(experts, table, owner, step, fresh):
    lane = lax.broadcasted_iota(jnp.int32, table.shape, 1)
    section = lane // experts
    first = first_section(step, fresh)
    mine = (lane % experts == owner) & (section >= first) & (section < first + 2)
    return jnp.sum(jnp.where(mine, table.astype(jnp.float32), 0.0), axis=1, keepdims=True)


def pack_kernel(section, expert, tokens, gain, routes, scales, changed, out):
    width = tokens.shape[1]
    normed = normalize(tokens[...].astype(jnp.float32), gain[...])
    table = weight_table(section[...], expert[...], routes, scales, changed)
    for chip in range(out.shape[0]):
        out[chip, :, :width] = normed
        out[chip, :, width:] = table


def sum_blocks(blocks):
    total = blocks[0].astype(jnp.float32)
    for chip in range(1, blocks.shape[0]):
        total = total + blocks[chip].astype(jnp.float32)
    return total


def next_kernel(previous, returned, gain, state_out, out):
    state = previous[...].astype(jnp.float32) + sum_blocks(returned)
    state_out[...] = state
    normed = normalize(state, gain[...])
    for chip in range(out.shape[0]):
        out[chip] = normed


def last_kernel(previous, returned, out):
    out[...] = (previous[...] + sum_blocks(returned)).astype(jnp.bfloat16)


def join_kernel(rows, tables, out):
    width = rows.shape[1]
    out[:, :width] = rows[...]
    out[:, width:] = tables[:, width:]


def mlp_kernel(experts, step, fresh, set_count, *refs):
    sources, refs = refs[:set_count], refs[set_count:]
    weights, outs = refs[:4], refs[4:]
    count, width = outs[0].shape
    rows = jnp.concatenate([source[:, :width] for source in sources], axis=0)
    table = jnp.concatenate([source[:, width:] for source in sources], axis=0)
    inputs = jnp.concatenate([rows] * max(1, MATMUL_ROWS // rows.shape[0]), axis=0)
    own = lax.axis_index("expert")
    total = None
    for core in range(2):
        up, down = weights[2 * core : 2 * core + 2]
        owner = own if core == 0 else own + 1 - 2 * lax.rem(own, 2)
        pre_act = lax.dot_general(
            inputs, up[...], (((1,), (1,)), ((), ())), preferred_element_type=jnp.float32
        )
        hidden = (pre_act / (1.0 + jnp.exp(-pre_act))).astype(jnp.bfloat16)
        result = jnp.dot(hidden, down[...], preferred_element_type=jnp.float32)
        result = result[: rows.shape[0]] * row_weights(experts, table, owner, step, fresh)
        total = result if total is None else total + result
    for i, out in enumerate(outs):
        out[...] = total[i * count : (i + 1) * count].astype(out.dtype)


def on_vmem(kernel, inputs, outputs, limit=4 * MIB, cost=None, after=()):
    in_vmem = pl.BlockSpec(memory_space=pltpu.VMEM)
    count = len(inputs)

    def body(*refs):
        kernel(*refs[:count], *refs[count + len(after) :])

    return pl.pallas_call(
        body,
        out_shape=[jax.ShapeDtypeStruct(shape, kind) for shape, kind in outputs],
        in_specs=[in_vmem] * count + [pl.BlockSpec(memory_space=pl.ANY)] * len(after),
        out_specs=[in_vmem] * len(outputs),
        compiler_params=pltpu.CompilerParams(vmem_limit_bytes=limit),
        cost_estimate=cost,
    )(*inputs, *after)


def run_mlp(row_sets, weights, step, fresh, out_types, after=()):
    count, width = row_sets[0].shape[0], weights[0].shape[1]
    size = sum(part.size for part in weights)
    cost = pl.CostEstimate(
        flops=4 * MATMUL_ROWS * size, bytes_accessed=4 * size, transcendentals=0
    )
    kernel = functools.partial(mlp_kernel, lax.axis_size("expert"), step, fresh, len(row_sets))
    outputs = [((count, width), out_type) for out_type in out_types]
    return on_vmem(kernel, tuple(row_sets) + tuple(weights), outputs, 8 * MIB, cost, after)


def swap_core(value):
    size = lax.axis_size("expert")
    return lax.ppermute(value, "expert", [(i, i ^ 1) for i in range(size)])


def swap_group(value):
    return lax.ppermute(value, "group", [(0, 1), (1, 0)])


def hop_core(value):
    size = lax.axis_size("expert")
    return lax.ppermute(value, "expert", [(i, i - 1) for i in range(1, size, 2)])


def spread(blocks):
    size = lax.axis_size("expert")
    groups = [
        [start + core for y in range(2) for start in range(2 * y, size, 4)] for core in range(2)
    ]
    return lax.all_to_all(blocks, "expert", 0, 0, axis_index_groups=groups, tiled=True)


def exchange_plan(tokens, norm_gain, routes, route_scale, changed, stale, learner):
    experts = lax.axis_size("expert")
    chips = experts // 2
    row_count, width = tokens.shape[1], tokens.shape[2]
    half = chips * row_count
    steps_total = routes.shape[0]
    packed = width + table_width(experts, steps_total)
    gain = norm_gain[None]
    state_shape = ((row_count, width), jnp.float32)
    weight_bytes = 2 * sum(part.size for part in stale + learner)
    long = pl.CostEstimate(
        flops=1280 * weight_bytes, bytes_accessed=2 * weight_bytes, transcendentals=0
    )
    lanes = ((row_count, table_width(experts, steps_total)), jnp.int32)
    section, expert = on_vmem(
        functools.partial(lane_kernel, experts), (), [lanes, lanes], cost=long
    )
    stale = stale + tuple(swap_core(part) for part in stale)
    learner = learner + tuple(swap_core(part) for part in learner)
    turn = hop_core(section.astype(jnp.bfloat16))
    (blocks,) = on_vmem(
        pack_kernel,
        (section, expert, tokens[0], gain, routes, route_scale, changed),
        [((chips, row_count, packed), jnp.bfloat16)],
        after=(turn,),
    )
    tables = spread(blocks).reshape(half, packed)
    rows, state = tables, tokens[0]
    for step in range(steps_total):
        if step == 0:
            (share,) = run_mlp([rows], stale, step, False, [jnp.bfloat16], learner[2:])
        else:
            state, blocks = on_vmem(
                next_kernel,
                (state, returned, gain),
                [state_shape, ((chips, row_count, width), jnp.bfloat16)],
            )
            rows = spread(blocks).reshape(half, width)
            (rows,) = on_vmem(join_kernel, (rows, tables), [((half, packed), jnp.bfloat16)])
            other = swap_group(rows)
            (old,) = run_mlp([rows], stale, step, False, [jnp.float32])
            other, old = lax.optimization_barrier((other, old))
            new, away = run_mlp([rows, other], learner, step, True, [jnp.float32, jnp.bfloat16])
            share = old + new + swap_group(away).astype(jnp.float32)
            share = share.astype(jnp.bfloat16)
        returned = spread(share.reshape(chips, row_count, width))
    (updated,) = on_vmem(last_kernel, (state, returned), [((row_count, width), jnp.bfloat16)])
    return updated[None]


def gather_plan(tokens, norm_gain, routes, route_scale, changed, stale, learner):
    experts = lax.axis_size("expert")
    owner_index = lax.axis_index("expert")
    row_count = tokens.shape[1]
    top_count = routes.shape[3]
    capacity = min(row_count, max(2, 2 * row_count * top_count // experts))
    is_fresh = jnp.any(changed[0] == owner_index)
    fresh = [lax.all_gather(part, "group", axis=0, tiled=True) for part in learner]
    newer = [jnp.where(is_fresh, new, old) for new, old in zip(fresh, stale)]
    state = tokens[0].astype(jnp.float32)
    buffer_ids = jnp.arange(experts * capacity, dtype=jnp.int32)
    expert_ids = jnp.arange(experts, dtype=jnp.int32)
    for step in range(routes.shape[0]):
        normed = normalize(state, norm_gain)
        chosen = routes[step, 0]
        weights = route_scale[step, 0]
        hits = (chosen.reshape(-1)[:, None] == expert_ids[None, :]).astype(jnp.int32)
        before = jnp.cumsum(hits, axis=0) - hits
        slot_pos = jnp.sum(before * hits, axis=1).reshape(chosen.shape)
        target = chosen * capacity + slot_pos
        placed = (target[:, :, None] == buffer_ids[None, None, :]).astype(jnp.float32)
        merge_weights = jnp.sum(placed * weights[:, :, None], axis=1)
        send_matrix = jnp.sum(placed, axis=1).astype(jnp.bfloat16)
        outgoing = lax.dot_general(
            send_matrix, normed, (((0,), (0,)), ((), ())), preferred_element_type=jnp.float32
        )
        outgoing = outgoing.astype(jnp.bfloat16).reshape(experts, capacity, -1)
        received = lax.all_to_all(outgoing, "expert", split_axis=0, concat_axis=0, tiled=True)
        flat = received.reshape(-1, received.shape[-1])
        result = expert_apply(flat, *(stale if step == 0 else newer))
        answer = result.astype(jnp.bfloat16).reshape(received.shape)
        returned = lax.all_to_all(answer, "expert", split_axis=0, concat_axis=0, tiled=True)
        flat_back = returned.reshape(experts * capacity, -1).astype(jnp.float32)
        state = state + jnp.dot(merge_weights, flat_back, precision=lax.Precision.HIGHEST)
    return state.astype(jnp.bfloat16)[None]


def local(
    tokens,
    norm_gain,
    routes,
    route_scale,
    changed,
    rollout_up,
    rollout_down,
    learner_up,
    learner_down,
):
    experts = lax.axis_size("expert")
    groups = lax.axis_size("group")
    fewer = tokens.shape[1] * experts < learner_up.shape[1]
    paired = experts % 4 == 0 and groups == 2
    plan = exchange_plan if fewer and paired else gather_plan
    stale = (rollout_up[0], rollout_down[0])
    learner = (learner_up[0], learner_down[0])
    return plan(tokens, norm_gain, routes, route_scale, changed, stale, learner)


def solution(mesh):
    placed = (
        P("group", "expert", None),
        P(),
        P(None, "group", "expert", None),
        P(None, "group", "expert", None),
        P("group", None),
        P("expert", None, None),
        P("expert", None, None),
        P("expert", "group", None),
        P("expert", "group", None),
    )
    return jax.shard_map(
        local, mesh=mesh, in_specs=placed, out_specs=P("group", "expert", None), check_vma=False
    )
```

```python
import functools
import jax
import jax.numpy as jnp
from jax import lax
from jax.experimental import pallas as pl
from jax.experimental.pallas import tpu as pltpu
from jax.sharding import PartitionSpec as P

LANES = 128
MATMUL_ROWS = 128
MIB = 1 << 20


def normalize(state, norm_gain):
    scale = lax.rsqrt(jnp.mean(state * state, axis=-1, keepdims=True) + 1e-06)
    return (state * scale * norm_gain).astype(jnp.bfloat16)


def expert_apply(inputs, up_rows, down_rows):
    pre_act = lax.dot_general(
        inputs, up_rows, (((1,), (1,)), ((), ())), preferred_element_type=jnp.float32
    )
    hidden = jax.nn.silu(pre_act).astype(jnp.bfloat16)
    return jnp.dot(hidden, down_rows, preferred_element_type=jnp.float32)


def table_width(experts, steps_total):
    sections = 2 + 4 * (steps_total - 1)
    return -(-sections * experts // LANES) * LANES


def first_section(step, fresh):
    return 0 if step == 0 else 4 * step - 2 + 2 * fresh


def lane_kernel(experts, section_out, expert_out):
    lane = lax.broadcasted_iota(jnp.int32, section_out.shape, 1)
    section_out[...] = lane // experts
    expert_out[...] = lane % experts


def weight_table(section, expert, chosen, weights, changed):
    steps_total, _, _, top_count = chosen.shape
    shape = section.shape
    fresh = section < 0
    for i in range(changed.shape[1]):
        fresh = fresh | (expert == changed[:, i : i + 1])
    table = jnp.zeros(shape, jnp.float32)
    for step in range(steps_total):
        dense = jnp.zeros(shape, jnp.float32)
        for k in range(top_count):
            hit = chosen[step, 0, :, k : k + 1] == expert
            dense = jnp.where(hit, weights[step, 0, :, k : k + 1], dense)
        high = dense.astype(jnp.bfloat16).astype(jnp.float32)
        value = jnp.where(section % 2 == 0, high, dense - high)
        start = first_section(step, False)
        if step == 0:
            table = jnp.where(section < 2, value, table)
        else:
            old = jnp.where(fresh, 0.0, value)
            new = jnp.where(fresh, value, 0.0)
            table = jnp.where((section >= start) & (section < start + 2), old, table)
            table = jnp.where((section >= start + 2) & (section < start + 4), new, table)
    return table.astype(jnp.bfloat16)


def row_weights(experts, table, owner, step, fresh):
    lane = lax.broadcasted_iota(jnp.int32, table.shape, 1)
    section = lane // experts
    first = first_section(step, fresh)
    mine = (lane % experts == owner) & (section >= first) & (section < first + 2)
    return jnp.sum(jnp.where(mine, table.astype(jnp.float32), 0.0), axis=1, keepdims=True)


def pack_kernel(section, expert, tokens, gain, routes, scales, changed, out):
    width = tokens.shape[1]
    normed = normalize(tokens[...].astype(jnp.float32), gain[...])
    out[:, :width] = normed
    out[:, width:] = weight_table(section[...], expert[...], routes, scales, changed)


def double_kernel(first, second, out):
    out[0] = first[...]
    out[1] = second[...]


def sum_blocks(blocks):
    total = blocks[0].astype(jnp.float32)
    for chip in range(1, blocks.shape[0]):
        total = total + blocks[chip].astype(jnp.float32)
    return total


def next_kernel(previous, returned, gain, state_out, out):
    state = previous[...].astype(jnp.float32) + sum_blocks(returned)
    state_out[...] = state
    normed = normalize(state, gain[...])
    for chip in range(out.shape[0]):
        out[chip] = normed


def last_kernel(previous, returned, out):
    out[...] = (previous[...] + sum_blocks(returned)).astype(jnp.bfloat16)


def join_kernel(rows, tables, out):
    width = rows.shape[1]
    out[:, :width] = rows[...]
    out[:, width:] = tables[...]


def weighted_outputs(experts, step, fresh, sources, weights, width):
    rows = jnp.concatenate([source[:, :width] for source in sources], axis=0)
    table = jnp.concatenate([source[:, width:] for source in sources], axis=0)
    inputs = jnp.concatenate([rows] * max(1, MATMUL_ROWS // rows.shape[0]), axis=0)
    own = lax.axis_index("expert")
    total = None
    for core in range(2):
        up, down = weights[2 * core : 2 * core + 2]
        owner = own if core == 0 else own + 1 - 2 * lax.rem(own, 2)
        pre_act = lax.dot_general(
            inputs, up[...], (((1,), (1,)), ((), ())), preferred_element_type=jnp.float32
        )
        hidden = (pre_act / (1.0 + jnp.exp(-pre_act))).astype(jnp.bfloat16)
        result = jnp.dot(hidden, down[...], preferred_element_type=jnp.float32)
        result = result[: rows.shape[0]] * row_weights(experts, table, owner, step, fresh)
        total = result if total is None else total + result
    return table, total


def first_kernel(experts, step, orders, rows, across, *refs):
    weights, (out, tables_out) = refs[:4], refs[4:]
    table, total = weighted_outputs(experts, step, False, [rows, across], weights, out.shape[2])
    chips, count, _ = out.shape
    own = lax.div(lax.axis_index("expert"), 2)
    for block, distance in enumerate(orders):
        chip = jnp.bitwise_xor(own, distance)
        place = lax.rem(chip, 2) * (chips // 2) + lax.div(chip, 2)
        span = slice(block * count, (block + 1) * count)
        out[place] = total[span].astype(out.dtype)
        tables_out[place] = table[span]


def mlp_kernel(experts, step, fresh, set_count, *refs):
    sources, weights, outs = refs[:set_count], refs[set_count:][:4], refs[set_count + 4 :]
    count, width = outs[0].shape
    _, total = weighted_outputs(experts, step, fresh, sources, weights, width)
    for i, out in enumerate(outs):
        out[...] = total[i * count : (i + 1) * count].astype(out.dtype)


def on_vmem(kernel, inputs, outputs, limit=4 * MIB, cost=None, after=()):
    in_vmem = pl.BlockSpec(memory_space=pltpu.VMEM)
    count = len(inputs)

    def body(*refs):
        kernel(*refs[:count], *refs[count + len(after) :])

    return pl.pallas_call(
        body,
        out_shape=[jax.ShapeDtypeStruct(shape, kind) for shape, kind in outputs],
        in_specs=[in_vmem] * count + [pl.BlockSpec(memory_space=pl.ANY)] * len(after),
        out_specs=[in_vmem] * len(outputs),
        compiler_params=pltpu.CompilerParams(vmem_limit_bytes=limit),
        cost_estimate=cost,
    )(*inputs, *after)


def run_mlp(kernel, row_sets, weights, outputs, after=()):
    size = sum(part.size for part in weights)
    cost = pl.CostEstimate(
        flops=4 * MATMUL_ROWS * size, bytes_accessed=4 * size, transcendentals=0
    )
    return on_vmem(kernel, tuple(row_sets) + tuple(weights), outputs, 8 * MIB, cost, after)


def swap_core(value):
    size = lax.axis_size("expert")
    return lax.ppermute(value, "expert", [(i, i ^ 1) for i in range(size)])


def swap_group(value):
    return lax.ppermute(value, "group", [(0, 1), (1, 0)])


def swap_chip(value, distance):
    size = lax.axis_size("expert")
    return lax.ppermute(value, "expert", [(i, i ^ 2 * distance) for i in range(size)])


def gather(block, chips):
    distance, orders = chips // 2, [0]
    while distance > 1:
        rows, width = block.shape
        joined = ((2, rows, width), block.dtype)
        (block,) = on_vmem(double_kernel, (block, swap_chip(block, distance)), [joined])
        block = block.reshape(2 * rows, width)
        orders = orders + [order ^ distance for order in orders]
        distance = distance // 2
    return block, swap_chip(block, 1), orders + [order ^ 1 for order in orders]


def spread(blocks):
    size = lax.axis_size("expert")
    groups = [
        [start + core for y in range(2) for start in range(2 * y, size, 4)] for core in range(2)
    ]
    return lax.all_to_all(blocks, "expert", 0, 0, axis_index_groups=groups, tiled=True)


def exchange_plan(tokens, norm_gain, routes, route_scale, changed, stale, learner):
    experts = lax.axis_size("expert")
    chips = experts // 2
    row_count, width = tokens.shape[1], tokens.shape[2]
    half = chips * row_count
    steps_total = routes.shape[0]
    packed = width + table_width(experts, steps_total)
    gain = norm_gain[None]
    state_shape = ((row_count, width), jnp.float32)
    weight_bytes = 2 * sum(part.size for part in stale + learner)
    long = pl.CostEstimate(
        flops=1280 * weight_bytes, bytes_accessed=2 * weight_bytes, transcendentals=0
    )
    lanes = ((row_count, table_width(experts, steps_total)), jnp.int32)
    section, expert = on_vmem(
        functools.partial(lane_kernel, experts), (), [lanes, lanes], cost=long
    )
    stale = stale + tuple(swap_core(part) for part in stale)
    learner = learner + tuple(swap_core(part) for part in learner)
    (block,) = on_vmem(
        pack_kernel,
        (section, expert, tokens[0], gain, routes, route_scale, changed),
        [((row_count, packed), jnp.bfloat16)],
    )
    state = tokens[0]
    for step in range(steps_total):
        if step == 0:
            rows, across, orders = gather(block, chips)
            share, tables = run_mlp(
                functools.partial(first_kernel, experts, step, orders),
                [rows, across],
                stale,
                [
                    ((chips, row_count, width), jnp.bfloat16),
                    ((chips, row_count, packed - width), jnp.bfloat16),
                ],
                learner[2:],
            )
            tables = tables.reshape(half, packed - width)
        else:
            state, blocks = on_vmem(
                next_kernel,
                (state, returned, gain),
                [state_shape, ((chips, row_count, width), jnp.bfloat16)],
            )
            rows = spread(blocks).reshape(half, width)
            (rows,) = on_vmem(join_kernel, (rows, tables), [((half, packed), jnp.bfloat16)])
            other = swap_group(rows)
            kept = ((half, width), jnp.float32)
            kernel = functools.partial(mlp_kernel, experts, step, False, 1)
            (old,) = run_mlp(kernel, [rows], stale, [kept])
            other, old = lax.optimization_barrier((other, old))
            kernel = functools.partial(mlp_kernel, experts, step, True, 2)
            sent = ((half, width), jnp.bfloat16)
            new, away = run_mlp(kernel, [rows, other], learner, [kept, sent])
            share = old + new + swap_group(away).astype(jnp.float32)
            share = share.astype(jnp.bfloat16).reshape(chips, row_count, width)
        returned = spread(share)
    (updated,) = on_vmem(last_kernel, (state, returned), [((row_count, width), jnp.bfloat16)])
    return updated[None]


def gather_plan(tokens, norm_gain, routes, route_scale, changed, stale, learner):
    experts = lax.axis_size("expert")
    owner_index = lax.axis_index("expert")
    row_count = tokens.shape[1]
    top_count = routes.shape[3]
    capacity = min(row_count, max(2, 2 * row_count * top_count // experts))
    is_fresh = jnp.any(changed[0] == owner_index)
    fresh = [lax.all_gather(part, "group", axis=0, tiled=True) for part in learner]
    newer = [jnp.where(is_fresh, new, old) for new, old in zip(fresh, stale)]
    state = tokens[0].astype(jnp.float32)
    buffer_ids = jnp.arange(experts * capacity, dtype=jnp.int32)
    expert_ids = jnp.arange(experts, dtype=jnp.int32)
    for step in range(routes.shape[0]):
        normed = normalize(state, norm_gain)
        chosen = routes[step, 0]
        weights = route_scale[step, 0]
        hits = (chosen.reshape(-1)[:, None] == expert_ids[None, :]).astype(jnp.int32)
        before = jnp.cumsum(hits, axis=0) - hits
        slot_pos = jnp.sum(before * hits, axis=1).reshape(chosen.shape)
        target = chosen * capacity + slot_pos
        placed = (target[:, :, None] == buffer_ids[None, None, :]).astype(jnp.float32)
        merge_weights = jnp.sum(placed * weights[:, :, None], axis=1)
        send_matrix = jnp.sum(placed, axis=1).astype(jnp.bfloat16)
        outgoing = lax.dot_general(
            send_matrix, normed, (((0,), (0,)), ((), ())), preferred_element_type=jnp.float32
        )
        outgoing = outgoing.astype(jnp.bfloat16).reshape(experts, capacity, -1)
        received = lax.all_to_all(outgoing, "expert", split_axis=0, concat_axis=0, tiled=True)
        flat = received.reshape(-1, received.shape[-1])
        result = expert_apply(flat, *(stale if step == 0 else newer))
        answer = result.astype(jnp.bfloat16).reshape(received.shape)
        returned = lax.all_to_all(answer, "expert", split_axis=0, concat_axis=0, tiled=True)
        flat_back = returned.reshape(experts * capacity, -1).astype(jnp.float32)
        state = state + jnp.dot(merge_weights, flat_back, precision=lax.Precision.HIGHEST)
    return state.astype(jnp.bfloat16)[None]


def local(
    tokens,
    norm_gain,
    routes,
    route_scale,
    changed,
    rollout_up,
    rollout_down,
    learner_up,
    learner_down,
):
    experts = lax.axis_size("expert")
    groups = lax.axis_size("group")
    fewer = tokens.shape[1] * experts < learner_up.shape[1]
    paired = experts & (experts - 1) == 0 and experts >= 4 and groups == 2
    plan = exchange_plan if fewer and paired else gather_plan
    stale = (rollout_up[0], rollout_down[0])
    learner = (learner_up[0], learner_down[0])
    return plan(tokens, norm_gain, routes, route_scale, changed, stale, learner)


def solution(mesh):
    placed = (
        P("group", "expert", None),
        P(),
        P(None, "group", "expert", None),
        P(None, "group", "expert", None),
        P("group", None),
        P("expert", None, None),
        P("expert", None, None),
        P("expert", "group", None),
        P("expert", "group", None),
    )
    return jax.shard_map(
        local, mesh=mesh, in_specs=placed, out_specs=P("group", "expert", None), check_vma=False
    )
```

```python
import functools
import jax
import jax.numpy as jnp
from jax import lax
from jax.experimental import pallas as pl
from jax.experimental.pallas import tpu as pltpu
from jax.sharding import PartitionSpec as P

LANES = 128
MATMUL_ROWS = 128
MIB = 1 << 20


def normalize(state, norm_gain):
    scale = lax.rsqrt(jnp.mean(state * state, axis=-1, keepdims=True) + 1e-06)
    return (state * scale * norm_gain).astype(jnp.bfloat16)


def expert_apply(inputs, up_rows, down_rows):
    pre_act = lax.dot_general(
        inputs, up_rows, (((1,), (1,)), ((), ())), preferred_element_type=jnp.float32
    )
    hidden = jax.nn.silu(pre_act).astype(jnp.bfloat16)
    return jnp.dot(hidden, down_rows, preferred_element_type=jnp.float32)


def table_width(experts, steps_total):
    sections = 2 + 4 * (steps_total - 1)
    return -(-sections * experts // LANES) * LANES


def first_section(step, fresh):
    return 0 if step == 0 else 4 * step - 2 + 2 * fresh


def lane_kernel(experts, section_out, expert_out):
    lane = lax.broadcasted_iota(jnp.int32, section_out.shape, 1)
    section_out[...] = lane // experts
    expert_out[...] = lane % experts


def weight_table(section, expert, chosen, weights, changed):
    steps_total, _, _, top_count = chosen.shape
    shape = section.shape
    fresh = section < 0
    for i in range(changed.shape[1]):
        fresh = fresh | (expert == changed[:, i : i + 1])
    table = jnp.zeros(shape, jnp.float32)
    for step in range(steps_total):
        dense = jnp.zeros(shape, jnp.float32)
        for k in range(top_count):
            hit = chosen[step, 0, :, k : k + 1] == expert
            dense = jnp.where(hit, weights[step, 0, :, k : k + 1], dense)
        high = dense.astype(jnp.bfloat16).astype(jnp.float32)
        value = jnp.where(section % 2 == 0, high, dense - high)
        start = first_section(step, False)
        if step == 0:
            table = jnp.where(section < 2, value, table)
        else:
            old = jnp.where(fresh, 0.0, value)
            new = jnp.where(fresh, value, 0.0)
            table = jnp.where((section >= start) & (section < start + 2), old, table)
            table = jnp.where((section >= start + 2) & (section < start + 4), new, table)
    return table.astype(jnp.bfloat16)


def row_weights(experts, table, owner, step, fresh):
    lane = lax.broadcasted_iota(jnp.int32, table.shape, 1)
    section = lane // experts
    first = first_section(step, fresh)
    mine = (lane % experts == owner) & (section >= first) & (section < first + 2)
    return jnp.sum(jnp.where(mine, table.astype(jnp.float32), 0.0), axis=1, keepdims=True)


def pack_kernel(section, expert, tokens, gain, routes, scales, changed, out):
    width = tokens.shape[1]
    normed = normalize(tokens[...].astype(jnp.float32), gain[...])
    out[:, :width] = normed
    out[:, width:] = weight_table(section[...], expert[...], routes, scales, changed)


def double_kernel(first, second, out):
    out[0] = first[...]
    out[1] = second[...]


def sum_blocks(blocks):
    total = blocks[0].astype(jnp.float32)
    for chip in range(1, blocks.shape[0]):
        total = total + blocks[chip].astype(jnp.float32)
    return total


def next_kernel(previous, returned, gain, state_out, out):
    state = previous[...].astype(jnp.float32) + sum_blocks(returned)
    state_out[...] = state
    normed = normalize(state, gain[...])
    for chip in range(out.shape[0]):
        out[chip] = normed


def last_kernel(previous, returned, out):
    out[...] = (previous[...] + sum_blocks(returned)).astype(jnp.bfloat16)


def join_kernel(rows, tables, out):
    width = rows.shape[1]
    out[:, :width] = rows[...]
    out[:, width:] = tables[...]


def weighted_outputs(experts, step, fresh, sources, weights, width):
    rows = jnp.concatenate([source[:, :width] for source in sources], axis=0)
    table = jnp.concatenate([source[:, width:] for source in sources], axis=0)
    inputs = jnp.concatenate([rows] * max(1, MATMUL_ROWS // rows.shape[0]), axis=0)
    own = lax.axis_index("expert")
    total = None
    for core in range(2):
        up, down = weights[2 * core : 2 * core + 2]
        owner = own if core == 0 else own + 1 - 2 * lax.rem(own, 2)
        pre_act = lax.dot_general(
            inputs, up[...], (((1,), (1,)), ((), ())), preferred_element_type=jnp.float32
        )
        hidden = (pre_act / (1.0 + jnp.exp(-pre_act))).astype(jnp.bfloat16)
        result = jnp.dot(hidden, down[...], preferred_element_type=jnp.float32)
        result = result[: rows.shape[0]] * row_weights(experts, table, owner, step, fresh)
        total = result if total is None else total + result
    return table, total


def first_kernel(experts, step, orders, rows, across, *refs):
    weights, (out, tables_out) = refs[:4], refs[4:]
    table, total = weighted_outputs(experts, step, False, [rows, across], weights, out.shape[2])
    chips, count, _ = out.shape
    device = lax.axis_index("expert")
    core = lax.rem(device, 2)
    for block, distances in enumerate(zip(*orders)):
        distance = distances[0] + core * (distances[1] - distances[0])
        chip = jnp.bitwise_xor(lax.div(device, 2), distance)
        place = lax.rem(chip, 2) * (chips // 2) + lax.div(chip, 2)
        span = slice(block * count, (block + 1) * count)
        out[place] = total[span].astype(out.dtype)
        tables_out[place] = table[span]


def mlp_kernel(experts, step, fresh, set_count, *refs):
    sources, weights, outs = refs[:set_count], refs[set_count:][:4], refs[set_count + 4 :]
    count, width = outs[0].shape
    _, total = weighted_outputs(experts, step, fresh, sources, weights, width)
    for i, out in enumerate(outs):
        out[...] = total[i * count : (i + 1) * count].astype(out.dtype)


def on_vmem(kernel, inputs, outputs, limit=4 * MIB, cost=None, after=()):
    in_vmem = pl.BlockSpec(memory_space=pltpu.VMEM)
    count = len(inputs)

    def body(*refs):
        kernel(*refs[:count], *refs[count + len(after) :])

    return pl.pallas_call(
        body,
        out_shape=[jax.ShapeDtypeStruct(shape, kind) for shape, kind in outputs],
        in_specs=[in_vmem] * count + [pl.BlockSpec(memory_space=pl.ANY)] * len(after),
        out_specs=[in_vmem] * len(outputs),
        compiler_params=pltpu.CompilerParams(vmem_limit_bytes=limit),
        cost_estimate=cost,
    )(*inputs, *after)


def run_mlp(kernel, row_sets, weights, outputs, after=()):
    size = sum(part.size for part in weights)
    cost = pl.CostEstimate(
        flops=4 * MATMUL_ROWS * size, bytes_accessed=4 * size, transcendentals=0
    )
    return on_vmem(kernel, tuple(row_sets) + tuple(weights), outputs, 8 * MIB, cost, after)


def swap_core(value):
    size = lax.axis_size("expert")
    return lax.ppermute(value, "expert", [(i, i ^ 1) for i in range(size)])


def swap_group(value):
    return lax.ppermute(value, "group", [(0, 1), (1, 0)])


def gather(block, chips):
    size = 2 * chips
    far = [1 << i for i in range(chips.bit_length() - 2, -1, -1)]
    stages = list(zip(far[-1:] + far[:-1], far))
    orders = [[0], [0]]
    for distances in stages:
        pairs = [(i, i ^ 2 * distances[i % 2]) for i in range(size)]
        received = lax.ppermute(block, "expert", pairs)
        orders = [
            order + [held ^ distance for held in order]
            for order, distance in zip(orders, distances)
        ]
        if distances is stages[-1]:
            return block, received, orders
        rows, width = block.shape
        joined = ((2, rows, width), block.dtype)
        block = on_vmem(double_kernel, (block, received), [joined])[0].reshape(2 * rows, width)


def spread(blocks):
    size = lax.axis_size("expert")
    groups = [
        [start + core for y in range(2) for start in range(2 * y, size, 4)] for core in range(2)
    ]
    return lax.all_to_all(blocks, "expert", 0, 0, axis_index_groups=groups, tiled=True)


def exchange_plan(tokens, norm_gain, routes, route_scale, changed, stale, learner):
    experts = lax.axis_size("expert")
    chips = experts // 2
    row_count, width = tokens.shape[1], tokens.shape[2]
    half = chips * row_count
    steps_total = routes.shape[0]
    packed = width + table_width(experts, steps_total)
    gain = norm_gain[None]
    state_shape = ((row_count, width), jnp.float32)
    weight_bytes = 2 * sum(part.size for part in stale + learner)
    long = pl.CostEstimate(
        flops=1280 * weight_bytes, bytes_accessed=2 * weight_bytes, transcendentals=0
    )
    lanes = ((row_count, table_width(experts, steps_total)), jnp.int32)
    section, expert = on_vmem(
        functools.partial(lane_kernel, experts), (), [lanes, lanes], cost=long
    )
    stale = stale + tuple(swap_core(part) for part in stale)
    learner = learner + tuple(swap_core(part) for part in learner)
    (block,) = on_vmem(
        pack_kernel,
        (section, expert, tokens[0], gain, routes, route_scale, changed),
        [((row_count, packed), jnp.bfloat16)],
    )
    state = tokens[0]
    for step in range(steps_total):
        if step == 0:
            rows, across, orders = gather(block, chips)
            share, tables = run_mlp(
                functools.partial(first_kernel, experts, step, orders),
                [rows, across],
                stale,
                [
                    ((chips, row_count, width), jnp.bfloat16),
                    ((chips, row_count, packed - width), jnp.bfloat16),
                ],
                learner[2:],
            )
            tables = tables.reshape(half, packed - width)
        else:
            state, blocks = on_vmem(
                next_kernel,
                (state, returned, gain),
                [state_shape, ((chips, row_count, width), jnp.bfloat16)],
            )
            rows = spread(blocks).reshape(half, width)
            (rows,) = on_vmem(join_kernel, (rows, tables), [((half, packed), jnp.bfloat16)])
            other = swap_group(rows)
            kept = ((half, width), jnp.float32)
            kernel = functools.partial(mlp_kernel, experts, step, False, 1)
            (old,) = run_mlp(kernel, [rows], stale, [kept])
            other, old = lax.optimization_barrier((other, old))
            kernel = functools.partial(mlp_kernel, experts, step, True, 2)
            sent = ((half, width), jnp.bfloat16)
            new, away = run_mlp(kernel, [rows, other], learner, [kept, sent])
            share = old + new + swap_group(away).astype(jnp.float32)
            share = share.astype(jnp.bfloat16).reshape(chips, row_count, width)
        returned = spread(share)
    (updated,) = on_vmem(last_kernel, (state, returned), [((row_count, width), jnp.bfloat16)])
    return updated[None]


def gather_plan(tokens, norm_gain, routes, route_scale, changed, stale, learner):
    experts = lax.axis_size("expert")
    owner_index = lax.axis_index("expert")
    row_count = tokens.shape[1]
    top_count = routes.shape[3]
    capacity = min(row_count, max(2, 2 * row_count * top_count // experts))
    is_fresh = jnp.any(changed[0] == owner_index)
    fresh = [lax.all_gather(part, "group", axis=0, tiled=True) for part in learner]
    newer = [jnp.where(is_fresh, new, old) for new, old in zip(fresh, stale)]
    state = tokens[0].astype(jnp.float32)
    buffer_ids = jnp.arange(experts * capacity, dtype=jnp.int32)
    expert_ids = jnp.arange(experts, dtype=jnp.int32)
    for step in range(routes.shape[0]):
        normed = normalize(state, norm_gain)
        chosen = routes[step, 0]
        weights = route_scale[step, 0]
        hits = (chosen.reshape(-1)[:, None] == expert_ids[None, :]).astype(jnp.int32)
        before = jnp.cumsum(hits, axis=0) - hits
        slot_pos = jnp.sum(before * hits, axis=1).reshape(chosen.shape)
        target = chosen * capacity + slot_pos
        placed = (target[:, :, None] == buffer_ids[None, None, :]).astype(jnp.float32)
        merge_weights = jnp.sum(placed * weights[:, :, None], axis=1)
        send_matrix = jnp.sum(placed, axis=1).astype(jnp.bfloat16)
        outgoing = lax.dot_general(
            send_matrix, normed, (((0,), (0,)), ((), ())), preferred_element_type=jnp.float32
        )
        outgoing = outgoing.astype(jnp.bfloat16).reshape(experts, capacity, -1)
        received = lax.all_to_all(outgoing, "expert", split_axis=0, concat_axis=0, tiled=True)
        flat = received.reshape(-1, received.shape[-1])
        result = expert_apply(flat, *(stale if step == 0 else newer))
        answer = result.astype(jnp.bfloat16).reshape(received.shape)
        returned = lax.all_to_all(answer, "expert", split_axis=0, concat_axis=0, tiled=True)
        flat_back = returned.reshape(experts * capacity, -1).astype(jnp.float32)
        state = state + jnp.dot(merge_weights, flat_back, precision=lax.Precision.HIGHEST)
    return state.astype(jnp.bfloat16)[None]


def local(
    tokens,
    norm_gain,
    routes,
    route_scale,
    changed,
    rollout_up,
    rollout_down,
    learner_up,
    learner_down,
):
    experts = lax.axis_size("expert")
    groups = lax.axis_size("group")
    fewer = tokens.shape[1] * experts < learner_up.shape[1]
    paired = experts & (experts - 1) == 0 and experts >= 4 and groups == 2
    plan = exchange_plan if fewer and paired else gather_plan
    stale = (rollout_up[0], rollout_down[0])
    learner = (learner_up[0], learner_down[0])
    return plan(tokens, norm_gain, routes, route_scale, changed, stale, learner)


def solution(mesh):
    placed = (
        P("group", "expert", None),
        P(),
        P(None, "group", "expert", None),
        P(None, "group", "expert", None),
        P("group", None),
        P("expert", None, None),
        P("expert", None, None),
        P("expert", "group", None),
        P("expert", "group", None),
    )
    return jax.shard_map(
        local, mesh=mesh, in_specs=placed, out_specs=P("group", "expert", None), check_vma=False
    )
```

```python
import functools
import jax
import jax.numpy as jnp
from jax import lax
from jax.experimental import pallas as pl
from jax.experimental.pallas import tpu as pltpu
from jax.sharding import PartitionSpec as P

LANES = 128
MATMUL_ROWS = 128
MIB = 1 << 20


def normalize(state, norm_gain):
    scale = lax.rsqrt(jnp.mean(state * state, axis=-1, keepdims=True) + 1e-06)
    return (state * scale * norm_gain).astype(jnp.bfloat16)


def expert_apply(inputs, up_rows, down_rows):
    pre_act = lax.dot_general(
        inputs, up_rows, (((1,), (1,)), ((), ())), preferred_element_type=jnp.float32
    )
    hidden = jax.nn.silu(pre_act).astype(jnp.bfloat16)
    return jnp.dot(hidden, down_rows, preferred_element_type=jnp.float32)


def table_width(experts, steps_total):
    sections = 2 + 4 * (steps_total - 1)
    return -(-sections * experts // LANES) * LANES


def first_section(step, fresh):
    return 0 if step == 0 else 4 * step - 2 + 2 * fresh


def lane_kernel(experts, section_out, expert_out):
    lane = lax.broadcasted_iota(jnp.int32, section_out.shape, 1)
    section_out[...] = lane // experts
    expert_out[...] = lane % experts


def weight_table(section, expert, chosen, weights, changed):
    steps_total, _, _, top_count = chosen.shape
    shape = section.shape
    fresh = section < 0
    for i in range(changed.shape[1]):
        fresh = fresh | (expert == changed[:, i : i + 1])
    table = jnp.zeros(shape, jnp.float32)
    for step in range(steps_total):
        dense = jnp.zeros(shape, jnp.float32)
        for k in range(top_count):
            hit = chosen[step, 0, :, k : k + 1] == expert
            dense = jnp.where(hit, weights[step, 0, :, k : k + 1], dense)
        high = dense.astype(jnp.bfloat16).astype(jnp.float32)
        value = jnp.where(section % 2 == 0, high, dense - high)
        start = first_section(step, False)
        if step == 0:
            table = jnp.where(section < 2, value, table)
        else:
            old = jnp.where(fresh, 0.0, value)
            new = jnp.where(fresh, value, 0.0)
            table = jnp.where((section >= start) & (section < start + 2), old, table)
            table = jnp.where((section >= start + 2) & (section < start + 4), new, table)
    return table.astype(jnp.bfloat16)


def row_weights(experts, table, owner, step, fresh):
    lane = lax.broadcasted_iota(jnp.int32, table.shape, 1)
    section = lane // experts
    first = first_section(step, fresh)
    mine = (lane % experts == owner) & (section >= first) & (section < first + 2)
    return jnp.sum(jnp.where(mine, table.astype(jnp.float32), 0.0), axis=1, keepdims=True)


def pack_kernel(section, expert, tokens, gain, routes, scales, changed, out):
    width = tokens.shape[1]
    normed = normalize(tokens[...].astype(jnp.float32), gain[...])
    out[:, :width] = normed
    out[:, width:] = weight_table(section[...], expert[...], routes, scales, changed)


def stack_kernel(*refs):
    for i, part in enumerate(refs[:-1]):
        refs[-1][i] = part[...]


def sum_blocks(blocks):
    total = blocks[0].astype(jnp.float32)
    for chip in range(1, blocks.shape[0]):
        total = total + blocks[chip].astype(jnp.float32)
    return total


def next_kernel(previous, returned, gain, state_out, out):
    state = previous[...].astype(jnp.float32) + sum_blocks(returned)
    state_out[...] = state
    normed = normalize(state, gain[...])
    for chip in range(out.shape[0]):
        out[chip] = normed


def last_kernel(previous, returned, out):
    out[...] = (previous[...] + sum_blocks(returned)).astype(jnp.bfloat16)


def join_kernel(rows, tables, out):
    width = rows.shape[1]
    out[:, :width] = rows[...]
    out[:, width:] = tables[...]


def weighted_outputs(experts, step, fresh, sources, weights, width):
    rows = jnp.concatenate([source[:, :width] for source in sources], axis=0)
    table = jnp.concatenate([source[:, width:] for source in sources], axis=0)
    inputs = jnp.concatenate([rows] * max(1, MATMUL_ROWS // rows.shape[0]), axis=0)
    own = lax.axis_index("expert")
    total = None
    for core in range(2):
        up, down = weights[2 * core : 2 * core + 2]
        owner = own if core == 0 else own + 1 - 2 * lax.rem(own, 2)
        pre_act = lax.dot_general(
            inputs, up[...], (((1,), (1,)), ((), ())), preferred_element_type=jnp.float32
        )
        hidden = (pre_act / (1.0 + jnp.exp(-pre_act))).astype(jnp.bfloat16)
        result = jnp.dot(hidden, down[...], preferred_element_type=jnp.float32)
        result = result[: rows.shape[0]] * row_weights(experts, table, owner, step, fresh)
        total = result if total is None else total + result
    return table, total


def first_kernel(experts, step, orders, rows, across, *refs):
    weights, (out, tables_out) = refs[:4], refs[4:]
    table, total = weighted_outputs(experts, step, False, [rows, across], weights, out.shape[2])
    chips, count, _ = out.shape
    own = lax.div(lax.axis_index("expert"), 2)
    for block, distance in enumerate(orders):
        chip = jnp.bitwise_xor(own, distance)
        place = lax.rem(chip, 2) * (chips // 2) + lax.div(chip, 2)
        span = slice(block * count, (block + 1) * count)
        out[place] = total[span].astype(out.dtype)
        tables_out[place] = table[span]


def mlp_kernel(experts, step, fresh, set_count, *refs):
    sources, weights, outs = refs[:set_count], refs[set_count:][:4], refs[set_count + 4 :]
    count, width = outs[0].shape
    _, total = weighted_outputs(experts, step, fresh, sources, weights, width)
    for i, out in enumerate(outs):
        out[...] = total[i * count : (i + 1) * count].astype(out.dtype)


def on_vmem(kernel, inputs, outputs, limit=4 * MIB, cost=None, after=()):
    in_vmem = pl.BlockSpec(memory_space=pltpu.VMEM)
    count = len(inputs)

    def body(*refs):
        kernel(*refs[:count], *refs[count + len(after) :])

    return pl.pallas_call(
        body,
        out_shape=[jax.ShapeDtypeStruct(shape, kind) for shape, kind in outputs],
        in_specs=[in_vmem] * count + [pl.BlockSpec(memory_space=pl.ANY)] * len(after),
        out_specs=[in_vmem] * len(outputs),
        compiler_params=pltpu.CompilerParams(vmem_limit_bytes=limit),
        cost_estimate=cost,
    )(*inputs, *after)


def run_mlp(kernel, row_sets, weights, outputs, after=()):
    size = sum(part.size for part in weights)
    cost = pl.CostEstimate(
        flops=4 * MATMUL_ROWS * size, bytes_accessed=4 * size, transcendentals=0
    )
    return on_vmem(kernel, tuple(row_sets) + tuple(weights), outputs, 8 * MIB, cost, after)


def swap_core(value):
    size = lax.axis_size("expert")
    return lax.ppermute(value, "expert", [(i, i ^ 1) for i in range(size)])


def swap_group(value):
    return lax.ppermute(value, "group", [(0, 1), (1, 0)])


def swap_chip(value, distance):
    size = lax.axis_size("expert")
    return lax.ppermute(value, "expert", [(i, i ^ 2 * distance) for i in range(size)])


def gather(block, chips, waiting):
    orders = [0] + list(range(chips - 2, 0, -2))
    received = [swap_chip(block, distance) for distance in orders[1:]]
    received = lax.optimization_barrier(tuple(received) + tuple(waiting))
    parts, waiting = (block,) + received[: len(orders) - 1], received[len(orders) - 1 :]
    rows, width = block.shape
    (block,) = on_vmem(stack_kernel, parts, [((len(parts), rows, width), block.dtype)])
    block = block.reshape(len(parts) * rows, width)
    return block, swap_chip(block, 1), orders + [order ^ 1 for order in orders], waiting


def spread(blocks):
    size = lax.axis_size("expert")
    groups = [
        [start + core for y in range(2) for start in range(2 * y, size, 4)] for core in range(2)
    ]
    return lax.all_to_all(blocks, "expert", 0, 0, axis_index_groups=groups, tiled=True)


def exchange_plan(tokens, norm_gain, routes, route_scale, changed, stale, learner):
    experts = lax.axis_size("expert")
    chips = experts // 2
    row_count, width = tokens.shape[1], tokens.shape[2]
    half = chips * row_count
    steps_total = routes.shape[0]
    packed = width + table_width(experts, steps_total)
    gain = norm_gain[None]
    state_shape = ((row_count, width), jnp.float32)
    weight_bytes = 2 * sum(part.size for part in stale + learner)
    long = pl.CostEstimate(
        flops=1280 * weight_bytes, bytes_accessed=2 * weight_bytes, transcendentals=0
    )
    lanes = ((row_count, table_width(experts, steps_total)), jnp.int32)
    section, expert = on_vmem(
        functools.partial(lane_kernel, experts), (), [lanes, lanes], cost=long
    )
    stale = stale + tuple(swap_core(part) for part in stale)
    (block,) = on_vmem(
        pack_kernel,
        (section, expert, tokens[0], gain, routes, route_scale, changed),
        [((row_count, packed), jnp.bfloat16)],
    )
    state = tokens[0]
    for step in range(steps_total):
        if step == 0:
            rows, across, orders, learner = gather(block, chips, learner)
            learner = learner + tuple(swap_core(part) for part in learner)
            share, tables = run_mlp(
                functools.partial(first_kernel, experts, step, orders),
                [rows, across],
                stale,
                [
                    ((chips, row_count, width), jnp.bfloat16),
                    ((chips, row_count, packed - width), jnp.bfloat16),
                ],
                learner[2:],
            )
            tables = tables.reshape(half, packed - width)
        else:
            state, blocks = on_vmem(
                next_kernel,
                (state, returned, gain),
                [state_shape, ((chips, row_count, width), jnp.bfloat16)],
            )
            rows = spread(blocks).reshape(half, width)
            (rows,) = on_vmem(join_kernel, (rows, tables), [((half, packed), jnp.bfloat16)])
            other = swap_group(rows)
            kept = ((half, width), jnp.float32)
            kernel = functools.partial(mlp_kernel, experts, step, False, 1)
            (old,) = run_mlp(kernel, [rows], stale, [kept])
            other, old = lax.optimization_barrier((other, old))
            kernel = functools.partial(mlp_kernel, experts, step, True, 2)
            sent = ((half, width), jnp.bfloat16)
            new, away = run_mlp(kernel, [rows, other], learner, [kept, sent])
            share = old + new + swap_group(away).astype(jnp.float32)
            share = share.astype(jnp.bfloat16).reshape(chips, row_count, width)
        returned = spread(share)
    (updated,) = on_vmem(last_kernel, (state, returned), [((row_count, width), jnp.bfloat16)])
    return updated[None]


def gather_plan(tokens, norm_gain, routes, route_scale, changed, stale, learner):
    experts = lax.axis_size("expert")
    owner_index = lax.axis_index("expert")
    row_count = tokens.shape[1]
    top_count = routes.shape[3]
    capacity = min(row_count, max(2, 2 * row_count * top_count // experts))
    is_fresh = jnp.any(changed[0] == owner_index)
    fresh = [lax.all_gather(part, "group", axis=0, tiled=True) for part in learner]
    newer = [jnp.where(is_fresh, new, old) for new, old in zip(fresh, stale)]
    state = tokens[0].astype(jnp.float32)
    buffer_ids = jnp.arange(experts * capacity, dtype=jnp.int32)
    expert_ids = jnp.arange(experts, dtype=jnp.int32)
    for step in range(routes.shape[0]):
        normed = normalize(state, norm_gain)
        chosen = routes[step, 0]
        weights = route_scale[step, 0]
        hits = (chosen.reshape(-1)[:, None] == expert_ids[None, :]).astype(jnp.int32)
        before = jnp.cumsum(hits, axis=0) - hits
        slot_pos = jnp.sum(before * hits, axis=1).reshape(chosen.shape)
        target = chosen * capacity + slot_pos
        placed = (target[:, :, None] == buffer_ids[None, None, :]).astype(jnp.float32)
        merge_weights = jnp.sum(placed * weights[:, :, None], axis=1)
        send_matrix = jnp.sum(placed, axis=1).astype(jnp.bfloat16)
        outgoing = lax.dot_general(
            send_matrix, normed, (((0,), (0,)), ((), ())), preferred_element_type=jnp.float32
        )
        outgoing = outgoing.astype(jnp.bfloat16).reshape(experts, capacity, -1)
        received = lax.all_to_all(outgoing, "expert", split_axis=0, concat_axis=0, tiled=True)
        flat = received.reshape(-1, received.shape[-1])
        result = expert_apply(flat, *(stale if step == 0 else newer))
        answer = result.astype(jnp.bfloat16).reshape(received.shape)
        returned = lax.all_to_all(answer, "expert", split_axis=0, concat_axis=0, tiled=True)
        flat_back = returned.reshape(experts * capacity, -1).astype(jnp.float32)
        state = state + jnp.dot(merge_weights, flat_back, precision=lax.Precision.HIGHEST)
    return state.astype(jnp.bfloat16)[None]


def local(
    tokens,
    norm_gain,
    routes,
    route_scale,
    changed,
    rollout_up,
    rollout_down,
    learner_up,
    learner_down,
):
    experts = lax.axis_size("expert")
    groups = lax.axis_size("group")
    fewer = tokens.shape[1] * experts < learner_up.shape[1]
    paired = experts & (experts - 1) == 0 and experts >= 8 and groups == 2
    plan = exchange_plan if fewer and paired else gather_plan
    stale = (rollout_up[0], rollout_down[0])
    learner = (learner_up[0], learner_down[0])
    return plan(tokens, norm_gain, routes, route_scale, changed, stale, learner)


def solution(mesh):
    placed = (
        P("group", "expert", None),
        P(),
        P(None, "group", "expert", None),
        P(None, "group", "expert", None),
        P("group", None),
        P("expert", None, None),
        P("expert", None, None),
        P("expert", "group", None),
        P("expert", "group", None),
    )
    return jax.shard_map(
        local, mesh=mesh, in_specs=placed, out_specs=P("group", "expert", None), check_vma=False
    )
```

```python
import functools
import jax
import jax.numpy as jnp
from jax import lax
from jax.experimental import pallas as pl
from jax.experimental.pallas import tpu as pltpu
from jax.sharding import PartitionSpec as P

LANES = 128
MATMUL_ROWS = 128
MIB = 1 << 20


def normalize(state, norm_gain):
    scale = lax.rsqrt(jnp.mean(state * state, axis=-1, keepdims=True) + 1e-06)
    return (state * scale * norm_gain).astype(jnp.bfloat16)


def expert_apply(inputs, up_rows, down_rows):
    pre_act = lax.dot_general(
        inputs, up_rows, (((1,), (1,)), ((), ())), preferred_element_type=jnp.float32
    )
    hidden = jax.nn.silu(pre_act).astype(jnp.bfloat16)
    return jnp.dot(hidden, down_rows, preferred_element_type=jnp.float32)


def table_width(experts, steps_total):
    sections = 2 + 4 * (steps_total - 1)
    return -(-sections * experts // LANES) * LANES


def first_section(step, fresh):
    return 0 if step == 0 else 4 * step - 2 + 2 * fresh


def lane_kernel(experts, section_out, expert_out):
    lane = lax.broadcasted_iota(jnp.int32, section_out.shape, 1)
    section_out[...] = lane // experts
    expert_out[...] = lane % experts


def weight_table(section, expert, chosen, weights, changed):
    steps_total, _, _, top_count = chosen.shape
    shape = section.shape
    fresh = section < 0
    for i in range(changed.shape[1]):
        fresh = fresh | (expert == changed[:, i : i + 1])
    table = jnp.zeros(shape, jnp.float32)
    for step in range(steps_total):
        dense = jnp.zeros(shape, jnp.float32)
        for k in range(top_count):
            hit = chosen[step, 0, :, k : k + 1] == expert
            dense = jnp.where(hit, weights[step, 0, :, k : k + 1], dense)
        high = dense.astype(jnp.bfloat16).astype(jnp.float32)
        value = jnp.where(section % 2 == 0, high, dense - high)
        start = first_section(step, False)
        if step == 0:
            table = jnp.where(section < 2, value, table)
        else:
            old = jnp.where(fresh, 0.0, value)
            new = jnp.where(fresh, value, 0.0)
            table = jnp.where((section >= start) & (section < start + 2), old, table)
            table = jnp.where((section >= start + 2) & (section < start + 4), new, table)
    return table.astype(jnp.bfloat16)


def row_weights(experts, table, owner, step, fresh):
    lane = lax.broadcasted_iota(jnp.int32, table.shape, 1)
    section = lane // experts
    first = first_section(step, fresh)
    mine = (lane % experts == owner) & (section >= first) & (section < first + 2)
    return jnp.sum(jnp.where(mine, table.astype(jnp.float32), 0.0), axis=1, keepdims=True)


def pack_kernel(section, expert, tokens, gain, routes, scales, changed, out):
    width = tokens.shape[1]
    normed = normalize(tokens[...].astype(jnp.float32), gain[...])
    table = weight_table(section[...], expert[...], routes, scales, changed)
    for i in range(out.shape[0]):
        out[i, :, :width] = normed
        out[i, :, width:] = table


def sum_blocks(blocks):
    total = blocks[0].astype(jnp.float32)
    for chip in range(1, blocks.shape[0]):
        total = total + blocks[chip].astype(jnp.float32)
    return total


def next_kernel(previous, returned, gain, state_out, out):
    state = previous[...].astype(jnp.float32) + sum_blocks(returned)
    state_out[...] = state
    normed = normalize(state, gain[...])
    for chip in range(out.shape[0]):
        out[chip] = normed


def last_kernel(previous, returned, out):
    out[...] = (previous[...] + sum_blocks(returned)).astype(jnp.bfloat16)


def join_kernel(rows, tables, out):
    width = rows.shape[1]
    out[:, :width] = rows[...]
    out[:, width:] = tables[...]


def weighted_outputs(experts, step, fresh, sources, weights, width):
    rows = jnp.concatenate([source[:, :width] for source in sources], axis=0)
    table = jnp.concatenate([source[:, width:] for source in sources], axis=0)
    inputs = jnp.concatenate([rows] * max(1, MATMUL_ROWS // rows.shape[0]), axis=0)
    own = lax.axis_index("expert")
    total = None
    for core in range(2):
        up, down = weights[2 * core : 2 * core + 2]
        owner = own if core == 0 else own + 1 - 2 * lax.rem(own, 2)
        pre_act = lax.dot_general(
            inputs, up[...], (((1,), (1,)), ((), ())), preferred_element_type=jnp.float32
        )
        hidden = (pre_act / (1.0 + jnp.exp(-pre_act))).astype(jnp.bfloat16)
        result = jnp.dot(hidden, down[...], preferred_element_type=jnp.float32)
        result = result[: rows.shape[0]] * row_weights(experts, table, owner, step, fresh)
        total = result if total is None else total + result
    return table, total


def first_kernel(experts, step, rows, across, *refs):
    weights, (out, tables_out) = refs[:4], refs[4:]
    table, total = weighted_outputs(experts, step, False, [rows, across], weights, out.shape[2])
    chips, count, _ = out.shape
    line = chips // 2
    own = lax.rem(lax.div(lax.axis_index("expert"), 2), 2)
    for block in range(chips):
        place = (own if block < line else 1 - own) * line + block % line
        span = slice(block * count, (block + 1) * count)
        out[place] = total[span].astype(out.dtype)
        tables_out[place] = table[span]


def mlp_kernel(experts, step, fresh, set_count, *refs):
    sources, weights, outs = refs[:set_count], refs[set_count:][:4], refs[set_count + 4 :]
    count, width = outs[0].shape
    _, total = weighted_outputs(experts, step, fresh, sources, weights, width)
    for i, out in enumerate(outs):
        out[...] = total[i * count : (i + 1) * count].astype(out.dtype)


def on_vmem(kernel, inputs, outputs, limit=4 * MIB, cost=None, after=()):
    in_vmem = pl.BlockSpec(memory_space=pltpu.VMEM)
    count = len(inputs)

    def body(*refs):
        kernel(*refs[:count], *refs[count + len(after) :])

    return pl.pallas_call(
        body,
        out_shape=[jax.ShapeDtypeStruct(shape, kind) for shape, kind in outputs],
        in_specs=[in_vmem] * count + [pl.BlockSpec(memory_space=pl.ANY)] * len(after),
        out_specs=[in_vmem] * len(outputs),
        compiler_params=pltpu.CompilerParams(vmem_limit_bytes=limit),
        cost_estimate=cost,
    )(*inputs, *after)


def run_mlp(kernel, row_sets, weights, outputs, after=()):
    size = sum(part.size for part in weights)
    cost = pl.CostEstimate(
        flops=4 * MATMUL_ROWS * size, bytes_accessed=4 * size, transcendentals=0
    )
    return on_vmem(kernel, tuple(row_sets) + tuple(weights), outputs, 8 * MIB, cost, after)


def swap_core(value):
    size = lax.axis_size("expert")
    return lax.ppermute(value, "expert", [(i, i ^ 1) for i in range(size)])


def swap_group(value):
    return lax.ppermute(value, "group", [(0, 1), (1, 0)])


def gather(blocks):
    size = lax.axis_size("expert")
    lines = [list(range(start, size, 4)) for start in range(4)]
    rows = lax.all_to_all(blocks, "expert", 0, 0, axis_index_groups=lines, tiled=True)
    rows = rows.reshape(-1, blocks.shape[-1])
    across = lax.ppermute(rows, "expert", [(i, i ^ 2) for i in range(size)])
    return rows, across


def spread(blocks):
    size = lax.axis_size("expert")
    groups = [
        [start + core for y in range(2) for start in range(2 * y, size, 4)] for core in range(2)
    ]
    return lax.all_to_all(blocks, "expert", 0, 0, axis_index_groups=groups, tiled=True)


def exchange_plan(tokens, norm_gain, routes, route_scale, changed, stale, learner):
    experts = lax.axis_size("expert")
    chips = experts // 2
    row_count, width = tokens.shape[1], tokens.shape[2]
    half = chips * row_count
    steps_total = routes.shape[0]
    packed = width + table_width(experts, steps_total)
    gain = norm_gain[None]
    state_shape = ((row_count, width), jnp.float32)
    weight_bytes = 2 * sum(part.size for part in stale + learner)
    long = pl.CostEstimate(
        flops=1280 * weight_bytes, bytes_accessed=2 * weight_bytes, transcendentals=0
    )
    lanes = ((row_count, table_width(experts, steps_total)), jnp.int32)
    section, expert = on_vmem(
        functools.partial(lane_kernel, experts), (), [lanes, lanes], cost=long
    )
    stale = stale + tuple(swap_core(part) for part in stale)
    learner = learner + tuple(swap_core(part) for part in learner)
    (blocks,) = on_vmem(
        pack_kernel,
        (section, expert, tokens[0], gain, routes, route_scale, changed),
        [((chips // 2, row_count, packed), jnp.bfloat16)],
    )
    state = tokens[0]
    for step in range(steps_total):
        if step == 0:
            rows, across = gather(blocks)
            share, tables = run_mlp(
                functools.partial(first_kernel, experts, step),
                [rows, across],
                stale,
                [
                    ((chips, row_count, width), jnp.bfloat16),
                    ((chips, row_count, packed - width), jnp.bfloat16),
                ],
                learner[2:],
            )
            tables = tables.reshape(half, packed - width)
        else:
            state, blocks = on_vmem(
                next_kernel,
                (state, returned, gain),
                [state_shape, ((chips, row_count, width), jnp.bfloat16)],
            )
            rows = spread(blocks).reshape(half, width)
            (rows,) = on_vmem(join_kernel, (rows, tables), [((half, packed), jnp.bfloat16)])
            other = swap_group(rows)
            kept = ((half, width), jnp.float32)
            kernel = functools.partial(mlp_kernel, experts, step, False, 1)
            (old,) = run_mlp(kernel, [rows], stale, [kept])
            other, old = lax.optimization_barrier((other, old))
            kernel = functools.partial(mlp_kernel, experts, step, True, 2)
            sent = ((half, width), jnp.bfloat16)
            new, away = run_mlp(kernel, [rows, other], learner, [kept, sent])
            share = old + new + swap_group(away).astype(jnp.float32)
            share = share.astype(jnp.bfloat16).reshape(chips, row_count, width)
        returned = spread(share)
    (updated,) = on_vmem(last_kernel, (state, returned), [((row_count, width), jnp.bfloat16)])
    return updated[None]


def gather_plan(tokens, norm_gain, routes, route_scale, changed, stale, learner):
    experts = lax.axis_size("expert")
    owner_index = lax.axis_index("expert")
    row_count = tokens.shape[1]
    top_count = routes.shape[3]
    capacity = min(row_count, max(2, 2 * row_count * top_count // experts))
    is_fresh = jnp.any(changed[0] == owner_index)
    fresh = [lax.all_gather(part, "group", axis=0, tiled=True) for part in learner]
    newer = [jnp.where(is_fresh, new, old) for new, old in zip(fresh, stale)]
    state = tokens[0].astype(jnp.float32)
    buffer_ids = jnp.arange(experts * capacity, dtype=jnp.int32)
    expert_ids = jnp.arange(experts, dtype=jnp.int32)
    for step in range(routes.shape[0]):
        normed = normalize(state, norm_gain)
        chosen = routes[step, 0]
        weights = route_scale[step, 0]
        hits = (chosen.reshape(-1)[:, None] == expert_ids[None, :]).astype(jnp.int32)
        before = jnp.cumsum(hits, axis=0) - hits
        slot_pos = jnp.sum(before * hits, axis=1).reshape(chosen.shape)
        target = chosen * capacity + slot_pos
        placed = (target[:, :, None] == buffer_ids[None, None, :]).astype(jnp.float32)
        merge_weights = jnp.sum(placed * weights[:, :, None], axis=1)
        send_matrix = jnp.sum(placed, axis=1).astype(jnp.bfloat16)
        outgoing = lax.dot_general(
            send_matrix, normed, (((0,), (0,)), ((), ())), preferred_element_type=jnp.float32
        )
        outgoing = outgoing.astype(jnp.bfloat16).reshape(experts, capacity, -1)
        received = lax.all_to_all(outgoing, "expert", split_axis=0, concat_axis=0, tiled=True)
        flat = received.reshape(-1, received.shape[-1])
        result = expert_apply(flat, *(stale if step == 0 else newer))
        answer = result.astype(jnp.bfloat16).reshape(received.shape)
        returned = lax.all_to_all(answer, "expert", split_axis=0, concat_axis=0, tiled=True)
        flat_back = returned.reshape(experts * capacity, -1).astype(jnp.float32)
        state = state + jnp.dot(merge_weights, flat_back, precision=lax.Precision.HIGHEST)
    return state.astype(jnp.bfloat16)[None]


def local(
    tokens,
    norm_gain,
    routes,
    route_scale,
    changed,
    rollout_up,
    rollout_down,
    learner_up,
    learner_down,
):
    experts = lax.axis_size("expert")
    groups = lax.axis_size("group")
    fewer = tokens.shape[1] * experts < learner_up.shape[1]
    paired = experts % 4 == 0 and groups == 2
    plan = exchange_plan if fewer and paired else gather_plan
    stale = (rollout_up[0], rollout_down[0])
    learner = (learner_up[0], learner_down[0])
    return plan(tokens, norm_gain, routes, route_scale, changed, stale, learner)


def solution(mesh):
    placed = (
        P("group", "expert", None),
        P(),
        P(None, "group", "expert", None),
        P(None, "group", "expert", None),
        P("group", None),
        P("expert", None, None),
        P("expert", None, None),
        P("expert", "group", None),
        P("expert", "group", None),
    )
    return jax.shard_map(
        local, mesh=mesh, in_specs=placed, out_specs=P("group", "expert", None), check_vma=False
    )
```

```python
import functools
import jax
import jax.numpy as jnp
from jax import lax
from jax.experimental import pallas as pl
from jax.experimental.pallas import tpu as pltpu
from jax.sharding import PartitionSpec as P

LANES = 128
MATMUL_ROWS = 128
MIB = 1 << 20


def normalize(state, norm_gain):
    scale = lax.rsqrt(jnp.mean(state * state, axis=-1, keepdims=True) + 1e-06)
    return (state * scale * norm_gain).astype(jnp.bfloat16)


def expert_apply(inputs, up_rows, down_rows):
    pre_act = lax.dot_general(
        inputs, up_rows, (((1,), (1,)), ((), ())), preferred_element_type=jnp.float32
    )
    hidden = jax.nn.silu(pre_act).astype(jnp.bfloat16)
    return jnp.dot(hidden, down_rows, preferred_element_type=jnp.float32)


def table_width(experts, steps_total):
    sections = 2 + 4 * (steps_total - 1)
    return -(-sections * experts // LANES) * LANES


def first_section(step, fresh):
    return 0 if step == 0 else 4 * step - 2 + 2 * fresh


def lane_kernel(experts, section_out, expert_out):
    lane = lax.broadcasted_iota(jnp.int32, section_out.shape, 1)
    section_out[...] = lane // experts
    expert_out[...] = lane % experts


def weight_table(section, expert, chosen, weights, changed):
    steps_total, _, _, top_count = chosen.shape
    shape = section.shape
    fresh = section < 0
    for i in range(changed.shape[1]):
        fresh = fresh | (expert == changed[:, i : i + 1])
    table = jnp.zeros(shape, jnp.float32)
    for step in range(steps_total):
        dense = jnp.zeros(shape, jnp.float32)
        for k in range(top_count):
            hit = chosen[step, 0, :, k : k + 1] == expert
            dense = jnp.where(hit, weights[step, 0, :, k : k + 1], dense)
        high = dense.astype(jnp.bfloat16).astype(jnp.float32)
        value = jnp.where(section % 2 == 0, high, dense - high)
        start = first_section(step, False)
        if step == 0:
            table = jnp.where(section < 2, value, table)
        else:
            old = jnp.where(fresh, 0.0, value)
            new = jnp.where(fresh, value, 0.0)
            table = jnp.where((section >= start) & (section < start + 2), old, table)
            table = jnp.where((section >= start + 2) & (section < start + 4), new, table)
    return table.astype(jnp.bfloat16)


def row_weights(experts, table, owner, step, fresh):
    lane = lax.broadcasted_iota(jnp.int32, table.shape, 1)
    section = lane // experts
    first = first_section(step, fresh)
    mine = (lane % experts == owner) & (section >= first) & (section < first + 2)
    return jnp.sum(jnp.where(mine, table.astype(jnp.float32), 0.0), axis=1, keepdims=True)


def pack_kernel(section, expert, tokens, gain, routes, scales, changed, out):
    width = tokens.shape[1]
    normed = normalize(tokens[...].astype(jnp.float32), gain[...])
    out[:, :width] = normed
    out[:, width:] = weight_table(section[...], expert[...], routes, scales, changed)


def stack_kernel(*refs):
    for i, part in enumerate(refs[:-1]):
        refs[-1][i] = part[...]


def sum_blocks(blocks):
    total = blocks[0].astype(jnp.float32)
    for chip in range(1, blocks.shape[0]):
        total = total + blocks[chip].astype(jnp.float32)
    return total


def next_kernel(previous, returned, gain, state_out, out):
    state = previous[...].astype(jnp.float32) + sum_blocks(returned)
    state_out[...] = state
    normed = normalize(state, gain[...])
    for chip in range(out.shape[0]):
        out[chip] = normed


def last_kernel(previous, returned, out):
    out[...] = (previous[...] + sum_blocks(returned)).astype(jnp.bfloat16)


def join_kernel(rows, tables, out):
    width = rows.shape[1]
    out[:, :width] = rows[...]
    out[:, width:] = tables[...]


def weighted_outputs(experts, step, fresh, sources, weights, width):
    rows = jnp.concatenate([source[:, :width] for source in sources], axis=0)
    table = jnp.concatenate([source[:, width:] for source in sources], axis=0)
    inputs = jnp.concatenate([rows] * max(1, MATMUL_ROWS // rows.shape[0]), axis=0)
    own = lax.axis_index("expert")
    total = None
    for core in range(2):
        up, down = weights[2 * core : 2 * core + 2]
        owner = own if core == 0 else own + 1 - 2 * lax.rem(own, 2)
        pre_act = lax.dot_general(
            inputs, up[...], (((1,), (1,)), ((), ())), preferred_element_type=jnp.float32
        )
        hidden = (pre_act / (1.0 + jnp.exp(-pre_act))).astype(jnp.bfloat16)
        result = jnp.dot(hidden, down[...], preferred_element_type=jnp.float32)
        result = result[: rows.shape[0]] * row_weights(experts, table, owner, step, fresh)
        total = result if total is None else total + result
    return table, total


def first_kernel(experts, step, orders, rows, across, *refs):
    weights, (out, tables_out) = refs[:4], refs[4:]
    table, total = weighted_outputs(experts, step, False, [rows, across], weights, out.shape[2])
    chips, count, _ = out.shape
    own = lax.div(lax.axis_index("expert"), 2)
    for block, distance in enumerate(orders):
        chip = jnp.bitwise_xor(own, distance)
        place = lax.rem(chip, 2) * (chips // 2) + lax.div(chip, 2)
        span = slice(block * count, (block + 1) * count)
        out[place] = total[span].astype(out.dtype)
        tables_out[place] = table[span]


def mlp_kernel(experts, step, fresh, set_count, *refs):
    sources, weights, outs = refs[:set_count], refs[set_count:][:4], refs[set_count + 4 :]
    count, width = outs[0].shape
    _, total = weighted_outputs(experts, step, fresh, sources, weights, width)
    for i, out in enumerate(outs):
        out[...] = total[i * count : (i + 1) * count].astype(out.dtype)


def on_vmem(kernel, inputs, outputs, limit=4 * MIB, cost=None, after=()):
    in_vmem = pl.BlockSpec(memory_space=pltpu.VMEM)
    count = len(inputs)

    def body(*refs):
        kernel(*refs[:count], *refs[count + len(after) :])

    return pl.pallas_call(
        body,
        out_shape=[jax.ShapeDtypeStruct(shape, kind) for shape, kind in outputs],
        in_specs=[in_vmem] * count + [pl.BlockSpec(memory_space=pl.ANY)] * len(after),
        out_specs=[in_vmem] * len(outputs),
        compiler_params=pltpu.CompilerParams(vmem_limit_bytes=limit),
        cost_estimate=cost,
    )(*inputs, *after)


def run_mlp(kernel, row_sets, weights, outputs, after=()):
    size = sum(part.size for part in weights)
    cost = pl.CostEstimate(
        flops=4 * MATMUL_ROWS * size, bytes_accessed=4 * size, transcendentals=0
    )
    return on_vmem(kernel, tuple(row_sets) + tuple(weights), outputs, 8 * MIB, cost, after)


def swap_core(value):
    size = lax.axis_size("expert")
    return lax.ppermute(value, "expert", [(i, i ^ 1) for i in range(size)])


def swap_group(value):
    return lax.ppermute(value, "group", [(0, 1), (1, 0)])


def swap_chip(value, distance):
    size = lax.axis_size("expert")
    return lax.ppermute(value, "expert", [(i, i ^ 2 * distance) for i in range(size)])


def gather(block, chips, waiting):
    orders = [0] + list(range(chips - 2, 0, -2))
    received = [swap_chip(block, distance) for distance in orders[1:]]
    received = lax.optimization_barrier(tuple(received) + tuple(waiting))
    parts, waiting = (block,) + received[: len(orders) - 1], received[len(orders) - 1 :]
    rows, width = block.shape
    (block,) = on_vmem(stack_kernel, parts, [((len(parts), rows, width), block.dtype)])
    block = block.reshape(len(parts) * rows, width)
    return block, swap_chip(block, 1), orders + [order ^ 1 for order in orders], waiting


def spread(blocks):
    size = lax.axis_size("expert")
    groups = [
        [start + core for y in range(2) for start in range(2 * y, size, 4)] for core in range(2)
    ]
    return lax.all_to_all(blocks, "expert", 0, 0, axis_index_groups=groups, tiled=True)


def exchange_plan(tokens, norm_gain, routes, route_scale, changed, stale, learner):
    experts = lax.axis_size("expert")
    chips = experts // 2
    row_count, width = tokens.shape[1], tokens.shape[2]
    half = chips * row_count
    steps_total = routes.shape[0]
    packed = width + table_width(experts, steps_total)
    gain = norm_gain[None]
    state_shape = ((row_count, width), jnp.float32)
    weight_bytes = 2 * sum(part.size for part in stale + learner)
    long = pl.CostEstimate(
        flops=1280 * weight_bytes, bytes_accessed=2 * weight_bytes, transcendentals=0
    )
    lanes = ((row_count, table_width(experts, steps_total)), jnp.int32)
    section, expert = on_vmem(
        functools.partial(lane_kernel, experts), (), [lanes, lanes], cost=long
    )
    stale = stale + tuple(swap_core(part) for part in stale)
    (block,) = on_vmem(
        pack_kernel,
        (section, expert, tokens[0], gain, routes, route_scale, changed),
        [((row_count, packed), jnp.bfloat16)],
    )
    state = tokens[0]
    for step in range(steps_total):
        if step == 0:
            rows, across, orders, learner = gather(block, chips, learner)
            learner = learner + tuple(swap_core(part) for part in learner)
            share, tables = run_mlp(
                functools.partial(first_kernel, experts, step, orders),
                [rows, across],
                stale,
                [
                    ((chips, row_count, width), jnp.bfloat16),
                    ((chips, row_count, packed - width), jnp.bfloat16),
                ],
            )
            tables = tables.reshape(half, packed - width)
        else:
            state, blocks = on_vmem(
                next_kernel,
                (state, returned, gain),
                [state_shape, ((chips, row_count, width), jnp.bfloat16)],
            )
            rows = spread(blocks).reshape(half, width)
            (rows,) = on_vmem(join_kernel, (rows, tables), [((half, packed), jnp.bfloat16)])
            other = swap_group(rows)
            kept = ((half, width), jnp.float32)
            kernel = functools.partial(mlp_kernel, experts, step, False, 1)
            (old,) = run_mlp(kernel, [rows], stale, [kept])
            other, old = lax.optimization_barrier((other, old))
            kernel = functools.partial(mlp_kernel, experts, step, True, 2)
            sent = ((half, width), jnp.bfloat16)
            new, away = run_mlp(kernel, [rows, other], learner, [kept, sent])
            share = old + new + swap_group(away).astype(jnp.float32)
            share = share.astype(jnp.bfloat16).reshape(chips, row_count, width)
        returned = spread(share)
    (updated,) = on_vmem(last_kernel, (state, returned), [((row_count, width), jnp.bfloat16)])
    return updated[None]


def gather_plan(tokens, norm_gain, routes, route_scale, changed, stale, learner):
    experts = lax.axis_size("expert")
    owner_index = lax.axis_index("expert")
    row_count = tokens.shape[1]
    top_count = routes.shape[3]
    capacity = min(row_count, max(2, 2 * row_count * top_count // experts))
    is_fresh = jnp.any(changed[0] == owner_index)
    fresh = [lax.all_gather(part, "group", axis=0, tiled=True) for part in learner]
    newer = [jnp.where(is_fresh, new, old) for new, old in zip(fresh, stale)]
    state = tokens[0].astype(jnp.float32)
    buffer_ids = jnp.arange(experts * capacity, dtype=jnp.int32)
    expert_ids = jnp.arange(experts, dtype=jnp.int32)
    for step in range(routes.shape[0]):
        normed = normalize(state, norm_gain)
        chosen = routes[step, 0]
        weights = route_scale[step, 0]
        hits = (chosen.reshape(-1)[:, None] == expert_ids[None, :]).astype(jnp.int32)
        before = jnp.cumsum(hits, axis=0) - hits
        slot_pos = jnp.sum(before * hits, axis=1).reshape(chosen.shape)
        target = chosen * capacity + slot_pos
        placed = (target[:, :, None] == buffer_ids[None, None, :]).astype(jnp.float32)
        merge_weights = jnp.sum(placed * weights[:, :, None], axis=1)
        send_matrix = jnp.sum(placed, axis=1).astype(jnp.bfloat16)
        outgoing = lax.dot_general(
            send_matrix, normed, (((0,), (0,)), ((), ())), preferred_element_type=jnp.float32
        )
        outgoing = outgoing.astype(jnp.bfloat16).reshape(experts, capacity, -1)
        received = lax.all_to_all(outgoing, "expert", split_axis=0, concat_axis=0, tiled=True)
        flat = received.reshape(-1, received.shape[-1])
        result = expert_apply(flat, *(stale if step == 0 else newer))
        answer = result.astype(jnp.bfloat16).reshape(received.shape)
        returned = lax.all_to_all(answer, "expert", split_axis=0, concat_axis=0, tiled=True)
        flat_back = returned.reshape(experts * capacity, -1).astype(jnp.float32)
        state = state + jnp.dot(merge_weights, flat_back, precision=lax.Precision.HIGHEST)
    return state.astype(jnp.bfloat16)[None]


def local(
    tokens,
    norm_gain,
    routes,
    route_scale,
    changed,
    rollout_up,
    rollout_down,
    learner_up,
    learner_down,
):
    experts = lax.axis_size("expert")
    groups = lax.axis_size("group")
    fewer = tokens.shape[1] * experts < learner_up.shape[1]
    paired = experts & (experts - 1) == 0 and experts >= 8 and groups == 2
    plan = exchange_plan if fewer and paired else gather_plan
    stale = (rollout_up[0], rollout_down[0])
    learner = (learner_up[0], learner_down[0])
    return plan(tokens, norm_gain, routes, route_scale, changed, stale, learner)


def solution(mesh):
    placed = (
        P("group", "expert", None),
        P(),
        P(None, "group", "expert", None),
        P(None, "group", "expert", None),
        P("group", None),
        P("expert", None, None),
        P("expert", None, None),
        P("expert", "group", None),
        P("expert", "group", None),
    )
    return jax.shard_map(
        local, mesh=mesh, in_specs=placed, out_specs=P("group", "expert", None), check_vma=False
    )
```

```python
import functools
import jax
import jax.numpy as jnp
from jax import lax
from jax.experimental import pallas as pl
from jax.experimental.pallas import tpu as pltpu
from jax.sharding import PartitionSpec as P

LANES = 128
MATMUL_ROWS = 128
MIB = 1 << 20


def normalize(state, norm_gain):
    scale = lax.rsqrt(jnp.mean(state * state, axis=-1, keepdims=True) + 1e-06)
    return (state * scale * norm_gain).astype(jnp.bfloat16)


def expert_apply(inputs, up_rows, down_rows):
    pre_act = lax.dot_general(
        inputs, up_rows, (((1,), (1,)), ((), ())), preferred_element_type=jnp.float32
    )
    hidden = jax.nn.silu(pre_act).astype(jnp.bfloat16)
    return jnp.dot(hidden, down_rows, preferred_element_type=jnp.float32)


def table_width(experts, steps_total):
    sections = 2 + 4 * (steps_total - 1)
    return -(-sections * experts // LANES) * LANES


def first_section(step, fresh):
    return 0 if step == 0 else 4 * step - 2 + 2 * fresh


def lane_kernel(experts, section_out, expert_out):
    lane = lax.broadcasted_iota(jnp.int32, section_out.shape, 1)
    section_out[...] = lane // experts
    expert_out[...] = lane % experts


def weight_table(section, expert, chosen, weights, changed):
    steps_total, _, _, top_count = chosen.shape
    shape = section.shape
    fresh = section < 0
    for i in range(changed.shape[1]):
        fresh = fresh | (expert == changed[:, i : i + 1])
    table = jnp.zeros(shape, jnp.float32)
    for step in range(steps_total):
        dense = jnp.zeros(shape, jnp.float32)
        for k in range(top_count):
            hit = chosen[step, 0, :, k : k + 1] == expert
            dense = jnp.where(hit, weights[step, 0, :, k : k + 1], dense)
        high = dense.astype(jnp.bfloat16).astype(jnp.float32)
        value = jnp.where(section % 2 == 0, high, dense - high)
        start = first_section(step, False)
        if step == 0:
            table = jnp.where(section < 2, value, table)
        else:
            old = jnp.where(fresh, 0.0, value)
            new = jnp.where(fresh, value, 0.0)
            table = jnp.where((section >= start) & (section < start + 2), old, table)
            table = jnp.where((section >= start + 2) & (section < start + 4), new, table)
    return table.astype(jnp.bfloat16)


def row_weights(experts, table, owner, step, fresh):
    lane = lax.broadcasted_iota(jnp.int32, table.shape, 1)
    section = lane // experts
    first = first_section(step, fresh)
    mine = (lane % experts == owner) & (section >= first) & (section < first + 2)
    return jnp.sum(jnp.where(mine, table.astype(jnp.float32), 0.0), axis=1, keepdims=True)


def pack_kernel(section, expert, tokens, gain, routes, scales, changed, out):
    width = tokens.shape[1]
    normed = normalize(tokens[...].astype(jnp.float32), gain[...])
    out[:, :width] = normed
    out[:, width:] = weight_table(section[...], expert[...], routes, scales, changed)


def stack_kernel(*refs):
    for i, part in enumerate(refs[:-1]):
        refs[-1][i] = part[...]


def sum_blocks(blocks):
    total = blocks[0].astype(jnp.float32)
    for chip in range(1, blocks.shape[0]):
        total = total + blocks[chip].astype(jnp.float32)
    return total


def next_kernel(previous, returned, gain, block, state_out, out):
    width = previous.shape[1]
    state = previous[...].astype(jnp.float32) + sum_blocks(returned)
    state_out[...] = state
    out[:, :width] = normalize(state, gain[...])
    out[:, width:] = block[:, width:]


def part_kernel(kept, received, away, own_out, *sent_outs):
    total = kept[...] + received[...].astype(jnp.float32) + away[...].astype(jnp.float32)
    count = own_out.shape[0]
    own_out[...] = total[:count]
    for i, sent in enumerate(sent_outs):
        sent[...] = total[(i + 1) * count : (i + 2) * count].astype(sent.dtype)


def last_kernel(previous, own, *refs):
    total = own[...]
    for received in refs[:-1]:
        total = total + received[...].astype(jnp.float32)
    refs[-1][...] = (previous[...] + total).astype(jnp.bfloat16)


def weighted_outputs(experts, step, fresh, sources, weights, width):
    rows = jnp.concatenate([source[:, :width] for source in sources], axis=0)
    table = jnp.concatenate([source[:, width:] for source in sources], axis=0)
    inputs = jnp.concatenate([rows] * max(1, MATMUL_ROWS // rows.shape[0]), axis=0)
    own = lax.axis_index("expert")
    total = None
    for core in range(2):
        up, down = weights[2 * core : 2 * core + 2]
        owner = own if core == 0 else own + 1 - 2 * lax.rem(own, 2)
        pre_act = lax.dot_general(
            inputs, up[...], (((1,), (1,)), ((), ())), preferred_element_type=jnp.float32
        )
        hidden = (pre_act / (1.0 + jnp.exp(-pre_act))).astype(jnp.bfloat16)
        result = jnp.dot(hidden, down[...], preferred_element_type=jnp.float32)
        result = result[: rows.shape[0]] * row_weights(experts, table, owner, step, fresh)
        total = result if total is None else total + result
    return total


def first_kernel(experts, step, orders, rows, across, *refs):
    weights, out = refs[:4], refs[4]
    total = weighted_outputs(experts, step, False, [rows, across], weights, out.shape[2])
    chips, count, _ = out.shape
    own = lax.div(lax.axis_index("expert"), 2)
    for block, distance in enumerate(orders):
        chip = jnp.bitwise_xor(own, distance)
        place = lax.rem(chip, 2) * (chips // 2) + lax.div(chip, 2)
        span = slice(block * count, (block + 1) * count)
        out[place] = total[span].astype(out.dtype)


def mlp_kernel(experts, step, fresh, set_count, before, *refs):
    sources, weights, refs = refs[:set_count], refs[set_count : set_count + 4], refs[set_count + 4 :]
    earlier, outs = refs[:before], refs[before:]
    total = weighted_outputs(experts, step, fresh, sources, weights, outs[0].shape[1])
    start = 0
    for out in outs:
        end = start + out.shape[0]
        part = total[start:end]
        if before and end <= earlier[0].shape[0]:
            part = part + earlier[0][start:end]
        out[...] = part.astype(out.dtype)
        start = end


def on_vmem(kernel, inputs, outputs, limit=4 * MIB, cost=None, after=()):
    in_vmem = pl.BlockSpec(memory_space=pltpu.VMEM)
    count = len(inputs)

    def body(*refs):
        kernel(*refs[:count], *refs[count + len(after) :])

    return pl.pallas_call(
        body,
        out_shape=[jax.ShapeDtypeStruct(shape, kind) for shape, kind in outputs],
        in_specs=[in_vmem] * count + [pl.BlockSpec(memory_space=pl.ANY)] * len(after),
        out_specs=[in_vmem] * len(outputs),
        compiler_params=pltpu.CompilerParams(vmem_limit_bytes=limit),
        cost_estimate=cost,
    )(*inputs, *after)


def run_mlp(kernel, row_sets, weights, outputs, after=()):
    size = sum(part.size for part in weights)
    cost = pl.CostEstimate(
        flops=4 * MATMUL_ROWS * size, bytes_accessed=4 * size, transcendentals=0
    )
    return on_vmem(kernel, tuple(row_sets) + tuple(weights), outputs, 8 * MIB, cost, after)


def swap_core(value):
    size = lax.axis_size("expert")
    return lax.ppermute(value, "expert", [(i, i ^ 1) for i in range(size)])


def swap_group(value):
    return lax.ppermute(value, "group", [(0, 1), (1, 0)])


def swap_chip(value, distance):
    size = lax.axis_size("expert")
    return lax.ppermute(value, "expert", [(i, i ^ 2 * distance) for i in range(size)])


def gather(block, chips, waiting):
    orders = [0] + list(range(chips - 2, 0, -2))
    received = [swap_chip(block, distance) for distance in orders[1:]]
    received = lax.optimization_barrier(tuple(received) + tuple(waiting))
    parts, waiting = (block,) + received[: len(orders) - 1], received[len(orders) - 1 :]
    rows, width = block.shape
    (block,) = on_vmem(stack_kernel, parts, [((len(parts), rows, width), block.dtype)])
    block = block.reshape(len(parts) * rows, width)
    return block, swap_chip(block, 1), orders + [order ^ 1 for order in orders], waiting


def spread(blocks):
    size = lax.axis_size("expert")
    groups = [
        [start + core for y in range(2) for start in range(2 * y, size, 4)] for core in range(2)
    ]
    return lax.all_to_all(blocks, "expert", 0, 0, axis_index_groups=groups, tiled=True)


def exchange_plan(tokens, norm_gain, routes, route_scale, changed, stale, learner):
    experts = lax.axis_size("expert")
    chips = experts // 2
    row_count, width = tokens.shape[1], tokens.shape[2]
    half = chips * row_count
    steps_total = routes.shape[0]
    packed = width + table_width(experts, steps_total)
    gain = norm_gain[None]
    state_shape = ((row_count, width), jnp.float32)
    weight_bytes = 2 * sum(part.size for part in stale + learner)
    long = pl.CostEstimate(
        flops=1280 * weight_bytes, bytes_accessed=2 * weight_bytes, transcendentals=0
    )
    lanes = ((row_count, table_width(experts, steps_total)), jnp.int32)
    section, expert = on_vmem(
        functools.partial(lane_kernel, experts), (), [lanes, lanes], cost=long
    )
    stale = stale + tuple(swap_core(part) for part in stale)
    (block,) = on_vmem(
        pack_kernel,
        (section, expert, tokens[0], gain, routes, route_scale, changed),
        [((row_count, packed), jnp.bfloat16)],
    )
    state = tokens[0]
    for step in range(steps_total):
        if step == 0:
            rows, across, orders, learner = gather(block, chips, learner)
            learner = learner + tuple(swap_core(part) for part in learner)
        else:
            state, block = on_vmem(
                next_kernel,
                (state, returned, gain, block),
                [state_shape, ((row_count, packed), jnp.bfloat16)],
            )
            rows, across, orders, _ = gather(block, chips, ())
        if step == 0:
            (share,) = run_mlp(
                functools.partial(first_kernel, experts, step, orders),
                [rows, across],
                stale,
                [((chips, row_count, width), jnp.bfloat16)],
            )
            returned = spread(share)
            continue
        other, other_across = swap_group(rows), swap_group(across)
        kernel = functools.partial(mlp_kernel, experts, step, False, 2, 0)
        (old,) = run_mlp(kernel, [rows, across], stale, [((half, width), jnp.float32)])
        other_across, old = lax.optimization_barrier((other_across, old))
        kernel = functools.partial(mlp_kernel, experts, step, True, 4, 1)
        line = [((half // 2, width), jnp.float32), ((half // 2, width), jnp.bfloat16)]
        kept, sent, away_kept, away_sent = run_mlp(
            kernel,
            [rows, across, other, other_across],
            tuple(learner) + (old,),
            line + line,
        )
        away = away_kept + swap_chip(away_sent, 1).astype(jnp.float32)
        away = swap_group(away.astype(jnp.bfloat16))
        own = [((row_count, width), jnp.float32)]
        others = [((row_count, width), jnp.bfloat16)] * (chips // 2 - 1)
        own, *sent = on_vmem(part_kernel, (kept, swap_chip(sent, 1), away), own + others)
        returned = [swap_chip(part, distance) for part, distance in zip(sent, orders[1:])]
    (updated,) = on_vmem(
        last_kernel, (state, own, *returned), [((row_count, width), jnp.bfloat16)]
    )
    return updated[None]


def gather_plan(tokens, norm_gain, routes, route_scale, changed, stale, learner):
    experts = lax.axis_size("expert")
    owner_index = lax.axis_index("expert")
    row_count = tokens.shape[1]
    top_count = routes.shape[3]
    capacity = min(row_count, max(2, 2 * row_count * top_count // experts))
    is_fresh = jnp.any(changed[0] == owner_index)
    fresh = [lax.all_gather(part, "group", axis=0, tiled=True) for part in learner]
    newer = [jnp.where(is_fresh, new, old) for new, old in zip(fresh, stale)]
    state = tokens[0].astype(jnp.float32)
    buffer_ids = jnp.arange(experts * capacity, dtype=jnp.int32)
    expert_ids = jnp.arange(experts, dtype=jnp.int32)
    for step in range(routes.shape[0]):
        normed = normalize(state, norm_gain)
        chosen = routes[step, 0]
        weights = route_scale[step, 0]
        hits = (chosen.reshape(-1)[:, None] == expert_ids[None, :]).astype(jnp.int32)
        before = jnp.cumsum(hits, axis=0) - hits
        slot_pos = jnp.sum(before * hits, axis=1).reshape(chosen.shape)
        target = chosen * capacity + slot_pos
        placed = (target[:, :, None] == buffer_ids[None, None, :]).astype(jnp.float32)
        merge_weights = jnp.sum(placed * weights[:, :, None], axis=1)
        send_matrix = jnp.sum(placed, axis=1).astype(jnp.bfloat16)
        outgoing = lax.dot_general(
            send_matrix, normed, (((0,), (0,)), ((), ())), preferred_element_type=jnp.float32
        )
        outgoing = outgoing.astype(jnp.bfloat16).reshape(experts, capacity, -1)
        received = lax.all_to_all(outgoing, "expert", split_axis=0, concat_axis=0, tiled=True)
        flat = received.reshape(-1, received.shape[-1])
        result = expert_apply(flat, *(stale if step == 0 else newer))
        answer = result.astype(jnp.bfloat16).reshape(received.shape)
        returned = lax.all_to_all(answer, "expert", split_axis=0, concat_axis=0, tiled=True)
        flat_back = returned.reshape(experts * capacity, -1).astype(jnp.float32)
        state = state + jnp.dot(merge_weights, flat_back, precision=lax.Precision.HIGHEST)
    return state.astype(jnp.bfloat16)[None]


def local(
    tokens,
    norm_gain,
    routes,
    route_scale,
    changed,
    rollout_up,
    rollout_down,
    learner_up,
    learner_down,
):
    experts = lax.axis_size("expert")
    groups = lax.axis_size("group")
    fewer = tokens.shape[1] * experts < learner_up.shape[1]
    paired = experts & (experts - 1) == 0 and experts >= 8 and groups == 2 and routes.shape[0] == 2
    plan = exchange_plan if fewer and paired else gather_plan
    stale = (rollout_up[0], rollout_down[0])
    learner = (learner_up[0], learner_down[0])
    return plan(tokens, norm_gain, routes, route_scale, changed, stale, learner)


def solution(mesh):
    placed = (
        P("group", "expert", None),
        P(),
        P(None, "group", "expert", None),
        P(None, "group", "expert", None),
        P("group", None),
        P("expert", None, None),
        P("expert", None, None),
        P("expert", "group", None),
        P("expert", "group", None),
    )
    return jax.shard_map(
        local, mesh=mesh, in_specs=placed, out_specs=P("group", "expert", None), check_vma=False
    )
```

```python
import functools
import jax
import jax.numpy as jnp
from jax import lax
from jax.experimental import pallas as pl
from jax.experimental.pallas import tpu as pltpu
from jax.sharding import PartitionSpec as P

LANES = 128
MATMUL_ROWS = 128
MIB = 1 << 20


def normalize(state, norm_gain):
    scale = lax.rsqrt(jnp.mean(state * state, axis=-1, keepdims=True) + 1e-06)
    return (state * scale * norm_gain).astype(jnp.bfloat16)


def expert_apply(inputs, up_rows, down_rows):
    pre_act = lax.dot_general(
        inputs, up_rows, (((1,), (1,)), ((), ())), preferred_element_type=jnp.float32
    )
    hidden = jax.nn.silu(pre_act).astype(jnp.bfloat16)
    return jnp.dot(hidden, down_rows, preferred_element_type=jnp.float32)


def table_width(experts, steps_total):
    sections = 2 + 4 * (steps_total - 1)
    return -(-sections * experts // LANES) * LANES


def first_section(step, fresh):
    return 0 if step == 0 else 4 * step - 2 + 2 * fresh


def lane_kernel(experts, section_out, expert_out):
    lane = lax.broadcasted_iota(jnp.int32, section_out.shape, 1)
    section_out[...] = lane // experts
    expert_out[...] = lane % experts


def weight_table(section, expert, chosen, weights, changed):
    steps_total, _, _, top_count = chosen.shape
    shape = section.shape
    fresh = section < 0
    for i in range(changed.shape[1]):
        fresh = fresh | (expert == changed[:, i : i + 1])
    table = jnp.zeros(shape, jnp.float32)
    for step in range(steps_total):
        dense = jnp.zeros(shape, jnp.float32)
        for k in range(top_count):
            hit = chosen[step, 0, :, k : k + 1] == expert
            dense = jnp.where(hit, weights[step, 0, :, k : k + 1], dense)
        high = dense.astype(jnp.bfloat16).astype(jnp.float32)
        value = jnp.where(section % 2 == 0, high, dense - high)
        start = first_section(step, False)
        if step == 0:
            table = jnp.where(section < 2, value, table)
        else:
            old = jnp.where(fresh, 0.0, value)
            new = jnp.where(fresh, value, 0.0)
            table = jnp.where((section >= start) & (section < start + 2), old, table)
            table = jnp.where((section >= start + 2) & (section < start + 4), new, table)
    return table.astype(jnp.bfloat16)


def row_weights(experts, table, owner, step, fresh):
    lane = lax.broadcasted_iota(jnp.int32, table.shape, 1)
    section = lane // experts
    first = first_section(step, fresh)
    mine = (lane % experts == owner) & (section >= first) & (section < first + 2)
    return jnp.sum(jnp.where(mine, table.astype(jnp.float32), 0.0), axis=1, keepdims=True)


def pack_kernel(section, expert, tokens, gain, routes, scales, changed, out):
    width = tokens.shape[1]
    normed = normalize(tokens[...].astype(jnp.float32), gain[...])
    out[:, :width] = normed
    out[:, width:] = weight_table(section[...], expert[...], routes, scales, changed)


def stack_kernel(*refs):
    for i, part in enumerate(refs[:-1]):
        refs[-1][i] = part[...]


def sum_blocks(blocks):
    total = blocks[0].astype(jnp.float32)
    for chip in range(1, blocks.shape[0]):
        total = total + blocks[chip].astype(jnp.float32)
    return total


def next_kernel(previous, returned, gain, state_out, out):
    state = previous[...].astype(jnp.float32) + sum_blocks(returned)
    state_out[...] = state
    normed = normalize(state, gain[...])
    for chip in range(out.shape[0]):
        out[chip] = normed


def fresh_kernel(experts, step, rows, other, *refs):
    weights, old, outs = refs[:4], refs[4], refs[5:]
    line, count, width = outs[0].shape
    half = line * count
    _, total = weighted_outputs(experts, step, True, [rows, other], weights, width)
    y = lax.rem(lax.div(lax.axis_index("expert"), 2), 2)
    low = jnp.full((half, width), y, jnp.int32) == 0
    for i, share in enumerate((total[: 2 * half] + old[...], total[2 * half :])):
        first, second = share[:half], share[half:]
        kept, sent = jnp.where(low, first, second), jnp.where(low, second, first)
        outs[2 * i][...] = kept.reshape(line, count, width)
        outs[2 * i + 1][...] = sent.reshape(line, count, width).astype(jnp.bfloat16)


def part_kernel(distances, kept, received, away, own_out, *sent_outs):
    z = lax.div(lax.axis_index("expert"), 4)
    for distance, out in zip((0,) + distances, (own_out,) + sent_outs):
        place = jnp.bitwise_xor(z, distance)
        total = kept[place] + received[place].astype(jnp.float32)
        out[...] = (total + away[place].astype(jnp.float32)).astype(out.dtype)


def last_kernel(previous, own, *refs):
    total = own[...]
    for received in refs[:-1]:
        total = total + received[...].astype(jnp.float32)
    refs[-1][...] = (previous[...] + total).astype(jnp.bfloat16)


def join_kernel(rows, tables, out):
    width = rows.shape[1]
    out[:, :width] = rows[...]
    out[:, width:] = tables[...]


def weighted_outputs(experts, step, fresh, sources, weights, width):
    rows = jnp.concatenate([source[:, :width] for source in sources], axis=0)
    table = jnp.concatenate([source[:, width:] for source in sources], axis=0)
    inputs = jnp.concatenate([rows] * max(1, MATMUL_ROWS // rows.shape[0]), axis=0)
    own = lax.axis_index("expert")
    total = None
    for core in range(2):
        up, down = weights[2 * core : 2 * core + 2]
        owner = own if core == 0 else own + 1 - 2 * lax.rem(own, 2)
        pre_act = lax.dot_general(
            inputs, up[...], (((1,), (1,)), ((), ())), preferred_element_type=jnp.float32
        )
        hidden = (pre_act / (1.0 + jnp.exp(-pre_act))).astype(jnp.bfloat16)
        result = jnp.dot(hidden, down[...], preferred_element_type=jnp.float32)
        result = result[: rows.shape[0]] * row_weights(experts, table, owner, step, fresh)
        total = result if total is None else total + result
    return table, total


def first_kernel(experts, step, orders, rows, across, *refs):
    weights, (out, tables_out) = refs[:4], refs[4:]
    table, total = weighted_outputs(experts, step, False, [rows, across], weights, out.shape[2])
    chips, count, _ = out.shape
    own = lax.div(lax.axis_index("expert"), 2)
    for block, distance in enumerate(orders):
        chip = jnp.bitwise_xor(own, distance)
        place = lax.rem(chip, 2) * (chips // 2) + lax.div(chip, 2)
        span = slice(block * count, (block + 1) * count)
        out[place] = total[span].astype(out.dtype)
        tables_out[place] = table[span]


def mlp_kernel(experts, step, fresh, set_count, *refs):
    sources, weights, outs = refs[:set_count], refs[set_count:][:4], refs[set_count + 4 :]
    count, width = outs[0].shape
    _, total = weighted_outputs(experts, step, fresh, sources, weights, width)
    for i, out in enumerate(outs):
        out[...] = total[i * count : (i + 1) * count].astype(out.dtype)


def on_vmem(kernel, inputs, outputs, limit=4 * MIB, cost=None, after=()):
    in_vmem = pl.BlockSpec(memory_space=pltpu.VMEM)
    count = len(inputs)

    def body(*refs):
        kernel(*refs[:count], *refs[count + len(after) :])

    return pl.pallas_call(
        body,
        out_shape=[jax.ShapeDtypeStruct(shape, kind) for shape, kind in outputs],
        in_specs=[in_vmem] * count + [pl.BlockSpec(memory_space=pl.ANY)] * len(after),
        out_specs=[in_vmem] * len(outputs),
        compiler_params=pltpu.CompilerParams(vmem_limit_bytes=limit),
        cost_estimate=cost,
    )(*inputs, *after)


def run_mlp(kernel, row_sets, weights, outputs, after=()):
    size = sum(part.size for part in weights)
    cost = pl.CostEstimate(
        flops=4 * MATMUL_ROWS * size, bytes_accessed=4 * size, transcendentals=0
    )
    return on_vmem(kernel, tuple(row_sets) + tuple(weights), outputs, 8 * MIB, cost, after)


def swap_core(value):
    size = lax.axis_size("expert")
    return lax.ppermute(value, "expert", [(i, i ^ 1) for i in range(size)])


def swap_group(value):
    return lax.ppermute(value, "group", [(0, 1), (1, 0)])


def swap_chip(value, distance):
    size = lax.axis_size("expert")
    return lax.ppermute(value, "expert", [(i, i ^ 2 * distance) for i in range(size)])


def gather(block, chips, waiting):
    orders = [0] + list(range(chips - 2, 0, -2))
    received = [swap_chip(block, distance) for distance in orders[1:]]
    received = lax.optimization_barrier(tuple(received) + tuple(waiting))
    parts, waiting = (block,) + received[: len(orders) - 1], received[len(orders) - 1 :]
    rows, width = block.shape
    (block,) = on_vmem(stack_kernel, parts, [((len(parts), rows, width), block.dtype)])
    block = block.reshape(len(parts) * rows, width)
    return block, swap_chip(block, 1), orders + [order ^ 1 for order in orders], waiting


def spread(blocks):
    size = lax.axis_size("expert")
    groups = [
        [start + core for y in range(2) for start in range(2 * y, size, 4)] for core in range(2)
    ]
    return lax.all_to_all(blocks, "expert", 0, 0, axis_index_groups=groups, tiled=True)


def exchange_plan(tokens, norm_gain, routes, route_scale, changed, stale, learner):
    experts = lax.axis_size("expert")
    chips = experts // 2
    row_count, width = tokens.shape[1], tokens.shape[2]
    half = chips * row_count
    steps_total = routes.shape[0]
    packed = width + table_width(experts, steps_total)
    gain = norm_gain[None]
    state_shape = ((row_count, width), jnp.float32)
    weight_bytes = 2 * sum(part.size for part in stale + learner)
    long = pl.CostEstimate(
        flops=1280 * weight_bytes, bytes_accessed=2 * weight_bytes, transcendentals=0
    )
    lanes = ((row_count, table_width(experts, steps_total)), jnp.int32)
    section, expert = on_vmem(
        functools.partial(lane_kernel, experts), (), [lanes, lanes], cost=long
    )
    stale = stale + tuple(swap_core(part) for part in stale)
    (block,) = on_vmem(
        pack_kernel,
        (section, expert, tokens[0], gain, routes, route_scale, changed),
        [((row_count, packed), jnp.bfloat16)],
    )
    state = tokens[0]
    for step in range(steps_total):
        if step == 0:
            rows, across, orders, learner = gather(block, chips, learner)
            learner = learner + tuple(swap_core(part) for part in learner)
            share, tables = run_mlp(
                functools.partial(first_kernel, experts, step, orders),
                [rows, across],
                stale,
                [
                    ((chips, row_count, width), jnp.bfloat16),
                    ((chips, row_count, packed - width), jnp.bfloat16),
                ],
            )
            tables = tables.reshape(half, packed - width)
        else:
            state, blocks = on_vmem(
                next_kernel,
                (state, returned, gain),
                [state_shape, ((chips, row_count, width), jnp.bfloat16)],
            )
            rows = spread(blocks).reshape(half, width)
            (rows,) = on_vmem(join_kernel, (rows, tables), [((half, packed), jnp.bfloat16)])
            other = swap_group(rows)
            kept = ((half, width), jnp.float32)
            kernel = functools.partial(mlp_kernel, experts, step, False, 1)
            (old,) = run_mlp(kernel, [rows], stale, [kept])
            other, old = lax.optimization_barrier((other, old))
            line = (chips // 2, row_count, width)
            kept, sent, away_kept, away_sent = run_mlp(
                functools.partial(fresh_kernel, experts, step),
                [rows, other],
                tuple(learner) + (old,),
                [(line, jnp.float32), (line, jnp.bfloat16)] * 2,
            )
            away = away_kept + swap_chip(away_sent, 1).astype(jnp.float32)
            away = swap_group(away.astype(jnp.bfloat16))
            distances = tuple(range(chips // 2 - 1, 0, -1))
            own, *sent = on_vmem(
                functools.partial(part_kernel, distances),
                (kept, swap_chip(sent, 1), away),
                [state_shape] + [((row_count, width), jnp.bfloat16)] * len(distances),
            )
            received = [swap_chip(part, 2 * d) for part, d in zip(sent, distances)]
            break
        returned = spread(share)
    (updated,) = on_vmem(
        last_kernel, (state, own, *received), [((row_count, width), jnp.bfloat16)]
    )
    return updated[None]


def gather_plan(tokens, norm_gain, routes, route_scale, changed, stale, learner):
    experts = lax.axis_size("expert")
    owner_index = lax.axis_index("expert")
    row_count = tokens.shape[1]
    top_count = routes.shape[3]
    capacity = min(row_count, max(2, 2 * row_count * top_count // experts))
    is_fresh = jnp.any(changed[0] == owner_index)
    fresh = [lax.all_gather(part, "group", axis=0, tiled=True) for part in learner]
    newer = [jnp.where(is_fresh, new, old) for new, old in zip(fresh, stale)]
    state = tokens[0].astype(jnp.float32)
    buffer_ids = jnp.arange(experts * capacity, dtype=jnp.int32)
    expert_ids = jnp.arange(experts, dtype=jnp.int32)
    for step in range(routes.shape[0]):
        normed = normalize(state, norm_gain)
        chosen = routes[step, 0]
        weights = route_scale[step, 0]
        hits = (chosen.reshape(-1)[:, None] == expert_ids[None, :]).astype(jnp.int32)
        before = jnp.cumsum(hits, axis=0) - hits
        slot_pos = jnp.sum(before * hits, axis=1).reshape(chosen.shape)
        target = chosen * capacity + slot_pos
        placed = (target[:, :, None] == buffer_ids[None, None, :]).astype(jnp.float32)
        merge_weights = jnp.sum(placed * weights[:, :, None], axis=1)
        send_matrix = jnp.sum(placed, axis=1).astype(jnp.bfloat16)
        outgoing = lax.dot_general(
            send_matrix, normed, (((0,), (0,)), ((), ())), preferred_element_type=jnp.float32
        )
        outgoing = outgoing.astype(jnp.bfloat16).reshape(experts, capacity, -1)
        received = lax.all_to_all(outgoing, "expert", split_axis=0, concat_axis=0, tiled=True)
        flat = received.reshape(-1, received.shape[-1])
        result = expert_apply(flat, *(stale if step == 0 else newer))
        answer = result.astype(jnp.bfloat16).reshape(received.shape)
        returned = lax.all_to_all(answer, "expert", split_axis=0, concat_axis=0, tiled=True)
        flat_back = returned.reshape(experts * capacity, -1).astype(jnp.float32)
        state = state + jnp.dot(merge_weights, flat_back, precision=lax.Precision.HIGHEST)
    return state.astype(jnp.bfloat16)[None]


def local(
    tokens,
    norm_gain,
    routes,
    route_scale,
    changed,
    rollout_up,
    rollout_down,
    learner_up,
    learner_down,
):
    experts = lax.axis_size("expert")
    groups = lax.axis_size("group")
    fewer = tokens.shape[1] * experts < learner_up.shape[1]
    paired = experts & (experts - 1) == 0 and experts >= 8 and groups == 2 and routes.shape[0] == 2
    plan = exchange_plan if fewer and paired else gather_plan
    stale = (rollout_up[0], rollout_down[0])
    learner = (learner_up[0], learner_down[0])
    return plan(tokens, norm_gain, routes, route_scale, changed, stale, learner)


def solution(mesh):
    placed = (
        P("group", "expert", None),
        P(),
        P(None, "group", "expert", None),
        P(None, "group", "expert", None),
        P("group", None),
        P("expert", None, None),
        P("expert", None, None),
        P("expert", "group", None),
        P("expert", "group", None),
    )
    return jax.shard_map(
        local, mesh=mesh, in_specs=placed, out_specs=P("group", "expert", None), check_vma=False
    )
```

```python
import functools
import jax
import jax.numpy as jnp
from jax import lax
from jax.experimental import pallas as pl
from jax.experimental.pallas import tpu as pltpu
from jax.sharding import PartitionSpec as P

LANES = 128
MATMUL_ROWS = 128
MIB = 1 << 20


def normalize(state, norm_gain):
    scale = lax.rsqrt(jnp.mean(state * state, axis=-1, keepdims=True) + 1e-06)
    return (state * scale * norm_gain).astype(jnp.bfloat16)


def expert_apply(inputs, up_rows, down_rows):
    pre_act = lax.dot_general(
        inputs, up_rows, (((1,), (1,)), ((), ())), preferred_element_type=jnp.float32
    )
    hidden = jax.nn.silu(pre_act).astype(jnp.bfloat16)
    return jnp.dot(hidden, down_rows, preferred_element_type=jnp.float32)


def table_width(experts, steps_total):
    sections = 2 + 4 * (steps_total - 1)
    return -(-sections * experts // LANES) * LANES


def first_section(step, fresh):
    return 0 if step == 0 else 4 * step - 2 + 2 * fresh


def lane_kernel(experts, section_out, expert_out):
    lane = lax.broadcasted_iota(jnp.int32, section_out.shape, 1)
    section_out[...] = lane // experts
    expert_out[...] = lane % experts


def weight_table(section, expert, chosen, weights, changed):
    steps_total, _, _, top_count = chosen.shape
    shape = section.shape
    fresh = section < 0
    for i in range(changed.shape[1]):
        fresh = fresh | (expert == changed[:, i : i + 1])
    table = jnp.zeros(shape, jnp.float32)
    for step in range(steps_total):
        dense = jnp.zeros(shape, jnp.float32)
        for k in range(top_count):
            hit = chosen[step, 0, :, k : k + 1] == expert
            dense = jnp.where(hit, weights[step, 0, :, k : k + 1], dense)
        high = dense.astype(jnp.bfloat16).astype(jnp.float32)
        value = jnp.where(section % 2 == 0, high, dense - high)
        start = first_section(step, False)
        if step == 0:
            table = jnp.where(section < 2, value, table)
        else:
            old = jnp.where(fresh, 0.0, value)
            new = jnp.where(fresh, value, 0.0)
            table = jnp.where((section >= start) & (section < start + 2), old, table)
            table = jnp.where((section >= start + 2) & (section < start + 4), new, table)
    return table.astype(jnp.bfloat16)


def row_weights(experts, table, owner, step, fresh):
    lane = lax.broadcasted_iota(jnp.int32, table.shape, 1)
    section = lane // experts
    first = first_section(step, fresh)
    mine = (lane % experts == owner) & (section >= first) & (section < first + 2)
    return jnp.sum(jnp.where(mine, table.astype(jnp.float32), 0.0), axis=1, keepdims=True)


def pack_kernel(section, expert, tokens, gain, routes, scales, changed, out):
    width = tokens.shape[1]
    normed = normalize(tokens[...].astype(jnp.float32), gain[...])
    out[:, :width] = normed
    out[:, width:] = weight_table(section[...], expert[...], routes, scales, changed)


def stack_kernel(*refs):
    for i, part in enumerate(refs[:-1]):
        refs[-1][i] = part[...]


def sum_blocks(blocks):
    total = blocks[0].astype(jnp.float32)
    for chip in range(1, blocks.shape[0]):
        total = total + blocks[chip].astype(jnp.float32)
    return total


def next_kernel(previous, returned, gain, state_out, out):
    state = previous[...].astype(jnp.float32) + sum_blocks(returned)
    state_out[...] = state
    normed = normalize(state, gain[...])
    for chip in range(out.shape[0]):
        out[chip] = normed


def fresh_kernel(experts, step, rows, other, *refs):
    weights, old, outs = refs[:4], refs[4], refs[5:]
    line, count, width = outs[0].shape
    half = line * count
    _, total = weighted_outputs(experts, step, True, [rows, other], weights, width)
    y = lax.rem(lax.div(lax.axis_index("expert"), 2), 2)
    low = jnp.full((half, width), y, jnp.int32) == 0
    for i, share in enumerate((total[: 2 * half] + old[...], total[2 * half :])):
        first, second = share[:half], share[half:]
        kept, sent = jnp.where(low, first, second), jnp.where(low, second, first)
        outs[2 * i][...] = kept.reshape(line, count, width)
        outs[2 * i + 1][...] = sent.reshape(line, count, width).astype(jnp.bfloat16)


def part_kernel(distances, kept, received, away, own_out, *sent_outs):
    z = lax.div(lax.axis_index("expert"), 4)
    for distance, out in zip((0,) + distances, (own_out,) + sent_outs):
        place = jnp.bitwise_xor(z, distance)
        total = kept[place] + received[place].astype(jnp.float32)
        out[...] = (total + away[place].astype(jnp.float32)).astype(out.dtype)


def last_kernel(previous, own, *refs):
    total = own[...]
    for received in refs[:-1]:
        total = total + received[...].astype(jnp.float32)
    refs[-1][...] = (previous[...] + total).astype(jnp.bfloat16)


def join_kernel(rows, tables, out):
    width = rows.shape[1]
    out[:, :width] = rows[...]
    out[:, width:] = tables[...]


def weighted_outputs(experts, step, fresh, sources, weights, width):
    rows = jnp.concatenate([source[:, :width] for source in sources], axis=0)
    table = jnp.concatenate([source[:, width:] for source in sources], axis=0)
    inputs = jnp.concatenate([rows] * max(1, MATMUL_ROWS // rows.shape[0]), axis=0)
    own = lax.axis_index("expert")
    total = None
    for core in range(2):
        up, down = weights[2 * core : 2 * core + 2]
        owner = own if core == 0 else own + 1 - 2 * lax.rem(own, 2)
        pre_act = lax.dot_general(
            inputs, up[...], (((1,), (1,)), ((), ())), preferred_element_type=jnp.float32
        )
        hidden = (pre_act / (1.0 + jnp.exp(-pre_act))).astype(jnp.bfloat16)
        result = jnp.dot(hidden, down[...], preferred_element_type=jnp.float32)
        result = result[: rows.shape[0]] * row_weights(experts, table, owner, step, fresh)
        total = result if total is None else total + result
    return table, total


def first_kernel(experts, step, orders, rows, across, *refs):
    weights, (out, tables_out) = refs[:4], refs[4:]
    table, total = weighted_outputs(experts, step, False, [rows, across], weights, out.shape[2])
    chips, count, _ = out.shape
    own = lax.div(lax.axis_index("expert"), 2)
    for block, distance in enumerate(orders):
        chip = jnp.bitwise_xor(own, distance)
        place = lax.rem(chip, 2) * (chips // 2) + lax.div(chip, 2)
        span = slice(block * count, (block + 1) * count)
        out[place] = total[span].astype(out.dtype)
        tables_out[place] = table.astype(jnp.float32)[span].astype(tables_out.dtype)


def mlp_kernel(experts, step, fresh, set_count, *refs):
    sources, weights, outs = refs[:set_count], refs[set_count:][:4], refs[set_count + 4 :]
    count, width = outs[0].shape
    _, total = weighted_outputs(experts, step, fresh, sources, weights, width)
    for i, out in enumerate(outs):
        out[...] = total[i * count : (i + 1) * count].astype(out.dtype)


def on_vmem(kernel, inputs, outputs, limit=4 * MIB, cost=None):
    in_vmem = pl.BlockSpec(memory_space=pltpu.VMEM)
    return pl.pallas_call(
        kernel,
        out_shape=[jax.ShapeDtypeStruct(shape, kind) for shape, kind in outputs],
        in_specs=[in_vmem] * len(inputs),
        out_specs=[in_vmem] * len(outputs),
        compiler_params=pltpu.CompilerParams(vmem_limit_bytes=limit),
        cost_estimate=cost,
    )(*inputs)


def run_mlp(kernel, row_sets, weights, outputs):
    size = sum(part.size for part in weights)
    cost = pl.CostEstimate(
        flops=4 * MATMUL_ROWS * size, bytes_accessed=4 * size, transcendentals=0
    )
    return on_vmem(kernel, tuple(row_sets) + tuple(weights), outputs, 8 * MIB, cost)


def swap_core(value):
    size = lax.axis_size("expert")
    return lax.ppermute(value, "expert", [(i, i ^ 1) for i in range(size)])


def swap_group(value):
    return lax.ppermute(value, "group", [(0, 1), (1, 0)])


def swap_chip(value, distance):
    size = lax.axis_size("expert")
    return lax.ppermute(value, "expert", [(i, i ^ 2 * distance) for i in range(size)])


def gather(block, chips, waiting):
    orders = [0] + list(range(chips - 2, 0, -2))
    received = [swap_chip(block, distance) for distance in orders[1:]]
    received = lax.optimization_barrier(tuple(received) + tuple(waiting))
    parts, waiting = (block,) + received[: len(orders) - 1], received[len(orders) - 1 :]
    rows, width = block.shape
    (block,) = on_vmem(stack_kernel, parts, [((len(parts), rows, width), block.dtype)])
    block = block.reshape(len(parts) * rows, width)
    return block, swap_chip(block, 1), orders + [order ^ 1 for order in orders], waiting


def spread(blocks):
    size = lax.axis_size("expert")
    groups = [
        [start + core for y in range(2) for start in range(2 * y, size, 4)] for core in range(2)
    ]
    return lax.all_to_all(blocks, "expert", 0, 0, axis_index_groups=groups, tiled=True)


def exchange_plan(tokens, norm_gain, routes, route_scale, changed, stale, learner):
    experts = lax.axis_size("expert")
    chips = experts // 2
    row_count, width = tokens.shape[1], tokens.shape[2]
    half = chips * row_count
    steps_total = routes.shape[0]
    packed = width + table_width(experts, steps_total)
    gain = norm_gain[None]
    state_shape = ((row_count, width), jnp.float32)
    weight_bytes = 2 * sum(part.size for part in stale + learner)
    long = pl.CostEstimate(
        flops=1280 * weight_bytes, bytes_accessed=2 * weight_bytes, transcendentals=0
    )
    lanes = ((row_count, table_width(experts, steps_total)), jnp.int32)
    section, expert = on_vmem(
        functools.partial(lane_kernel, experts), (), [lanes, lanes], cost=long
    )
    stale = stale + tuple(swap_core(part) for part in stale)
    (block,) = on_vmem(
        pack_kernel,
        (section, expert, tokens[0], gain, routes, route_scale, changed),
        [((row_count, packed), jnp.bfloat16)],
    )
    state = tokens[0]
    for step in range(steps_total):
        if step == 0:
            rows, across, orders, learner = gather(block, chips, learner)
            learner = learner + tuple(swap_core(part) for part in learner)
            share, tables = run_mlp(
                functools.partial(first_kernel, experts, step, orders),
                [rows, across],
                stale,
                [
                    ((chips, row_count, width), jnp.bfloat16),
                    ((chips, row_count, packed - width), jnp.bfloat16),
                ],
            )
            tables = tables.reshape(half, packed - width)
        else:
            state, blocks = on_vmem(
                next_kernel,
                (state, returned, gain),
                [state_shape, ((chips, row_count, width), jnp.bfloat16)],
            )
            rows = spread(blocks).reshape(half, width)
            (rows,) = on_vmem(join_kernel, (rows, tables), [((half, packed), jnp.bfloat16)])
            other = swap_group(rows)
            kept = ((half, width), jnp.float32)
            kernel = functools.partial(mlp_kernel, experts, step, False, 1)
            (old,) = run_mlp(kernel, [rows], stale, [kept])
            other, old = lax.optimization_barrier((other, old))
            line = (chips // 2, row_count, width)
            kept, sent, away_kept, away_sent = run_mlp(
                functools.partial(fresh_kernel, experts, step),
                [rows, other],
                tuple(learner) + (old,),
                [(line, jnp.float32), (line, jnp.bfloat16)] * 2,
            )
            away = away_kept + swap_chip(away_sent, 1).astype(jnp.float32)
            away = swap_group(away.astype(jnp.bfloat16))
            distances = tuple(range(1, chips // 2))
            own, *sent = on_vmem(
                functools.partial(part_kernel, distances),
                (kept, swap_chip(sent, 1), away),
                [state_shape] + [((row_count, width), jnp.bfloat16)] * len(distances),
            )
            received = [swap_chip(part, 2 * d) for part, d in zip(sent, distances)]
            break
        returned = spread(share)
    (updated,) = on_vmem(
        last_kernel, (state, own, *received), [((row_count, width), jnp.bfloat16)]
    )
    return updated[None]


def gather_plan(tokens, norm_gain, routes, route_scale, changed, stale, learner):
    experts = lax.axis_size("expert")
    owner_index = lax.axis_index("expert")
    row_count = tokens.shape[1]
    top_count = routes.shape[3]
    capacity = min(row_count, max(2, 2 * row_count * top_count // experts))
    is_fresh = jnp.any(changed[0] == owner_index)
    fresh = [lax.all_gather(part, "group", axis=0, tiled=True) for part in learner]
    newer = [jnp.where(is_fresh, new, old) for new, old in zip(fresh, stale)]
    state = tokens[0].astype(jnp.float32)
    buffer_ids = jnp.arange(experts * capacity, dtype=jnp.int32)
    expert_ids = jnp.arange(experts, dtype=jnp.int32)
    for step in range(routes.shape[0]):
        normed = normalize(state, norm_gain)
        chosen = routes[step, 0]
        weights = route_scale[step, 0]
        hits = (chosen.reshape(-1)[:, None] == expert_ids[None, :]).astype(jnp.int32)
        before = jnp.cumsum(hits, axis=0) - hits
        slot_pos = jnp.sum(before * hits, axis=1).reshape(chosen.shape)
        target = chosen * capacity + slot_pos
        placed = (target[:, :, None] == buffer_ids[None, None, :]).astype(jnp.float32)
        merge_weights = jnp.sum(placed * weights[:, :, None], axis=1)
        send_matrix = jnp.sum(placed, axis=1).astype(jnp.bfloat16)
        outgoing = lax.dot_general(
            send_matrix, normed, (((0,), (0,)), ((), ())), preferred_element_type=jnp.float32
        )
        outgoing = outgoing.astype(jnp.bfloat16).reshape(experts, capacity, -1)
        received = lax.all_to_all(outgoing, "expert", split_axis=0, concat_axis=0, tiled=True)
        flat = received.reshape(-1, received.shape[-1])
        result = expert_apply(flat, *(stale if step == 0 else newer))
        answer = result.astype(jnp.bfloat16).reshape(received.shape)
        returned = lax.all_to_all(answer, "expert", split_axis=0, concat_axis=0, tiled=True)
        flat_back = returned.reshape(experts * capacity, -1).astype(jnp.float32)
        state = state + jnp.dot(merge_weights, flat_back, precision=lax.Precision.HIGHEST)
    return state.astype(jnp.bfloat16)[None]


def local(
    tokens,
    norm_gain,
    routes,
    route_scale,
    changed,
    rollout_up,
    rollout_down,
    learner_up,
    learner_down,
):
    experts = lax.axis_size("expert")
    groups = lax.axis_size("group")
    fewer = tokens.shape[1] * experts < learner_up.shape[1]
    paired = experts & (experts - 1) == 0 and experts >= 8 and groups == 2 and routes.shape[0] == 2
    plan = exchange_plan if fewer and paired else gather_plan
    stale = (rollout_up[0], rollout_down[0])
    learner = (learner_up[0], learner_down[0])
    return plan(tokens, norm_gain, routes, route_scale, changed, stale, learner)


def solution(mesh):
    placed = (
        P("group", "expert", None),
        P(),
        P(None, "group", "expert", None),
        P(None, "group", "expert", None),
        P("group", None),
        P("expert", None, None),
        P("expert", None, None),
        P("expert", "group", None),
        P("expert", "group", None),
    )
    return jax.shard_map(
        local, mesh=mesh, in_specs=placed, out_specs=P("group", "expert", None), check_vma=False
    )
```

```python
import functools
import jax
import jax.numpy as jnp
from jax import lax
from jax.experimental import pallas as pl
from jax.experimental.pallas import tpu as pltpu
from jax.sharding import PartitionSpec as P

LANES = 128
MATMUL_ROWS = 128
MIB = 1 << 20


def normalize(state, norm_gain):
    scale = lax.rsqrt(jnp.mean(state * state, axis=-1, keepdims=True) + 1e-06)
    return (state * scale * norm_gain).astype(jnp.bfloat16)


def expert_apply(inputs, up_rows, down_rows):
    pre_act = lax.dot_general(
        inputs, up_rows, (((1,), (1,)), ((), ())), preferred_element_type=jnp.float32
    )
    hidden = jax.nn.silu(pre_act).astype(jnp.bfloat16)
    return jnp.dot(hidden, down_rows, preferred_element_type=jnp.float32)


def table_width(experts, steps_total):
    sections = 2 + 4 * (steps_total - 1)
    return -(-sections * experts // LANES) * LANES


def first_section(step, fresh):
    return 0 if step == 0 else 4 * step - 2 + 2 * fresh


def lane_kernel(experts, section_out, expert_out):
    lane = lax.broadcasted_iota(jnp.int32, section_out.shape, 1)
    section_out[...] = lane // experts
    expert_out[...] = lane % experts


def weight_table(section, expert, chosen, weights, changed):
    steps_total, _, _, top_count = chosen.shape
    shape = section.shape
    fresh = section < 0
    for i in range(changed.shape[1]):
        fresh = fresh | (expert == changed[:, i : i + 1])
    table = jnp.zeros(shape, jnp.float32)
    for step in range(steps_total):
        dense = jnp.zeros(shape, jnp.float32)
        for k in range(top_count):
            hit = chosen[step, 0, :, k : k + 1] == expert
            dense = jnp.where(hit, weights[step, 0, :, k : k + 1], dense)
        high = dense.astype(jnp.bfloat16).astype(jnp.float32)
        value = jnp.where(section % 2 == 0, high, dense - high)
        start = first_section(step, False)
        if step == 0:
            table = jnp.where(section < 2, value, table)
        else:
            old = jnp.where(fresh, 0.0, value)
            new = jnp.where(fresh, value, 0.0)
            table = jnp.where((section >= start) & (section < start + 2), old, table)
            table = jnp.where((section >= start + 2) & (section < start + 4), new, table)
    return table.astype(jnp.bfloat16)


def row_weights(experts, table, owner, step, fresh):
    lane = lax.broadcasted_iota(jnp.int32, table.shape, 1)
    section = lane // experts
    first = first_section(step, fresh)
    mine = (lane % experts == owner) & (section >= first) & (section < first + 2)
    return jnp.sum(jnp.where(mine, table.astype(jnp.float32), 0.0), axis=1, keepdims=True)


def pack_kernel(section, expert, tokens, gain, routes, scales, changed, out):
    width = tokens.shape[1]
    normed = normalize(tokens[...].astype(jnp.float32), gain[...])
    out[:, :width] = normed
    out[:, width:] = weight_table(section[...], expert[...], routes, scales, changed)


def stack_kernel(*refs):
    for i, part in enumerate(refs[:-1]):
        refs[-1][i] = part[...]


def sum_blocks(blocks):
    total = blocks[0].astype(jnp.float32)
    for chip in range(1, blocks.shape[0]):
        total = total + blocks[chip].astype(jnp.float32)
    return total


def next_kernel(previous, returned, gain, state_out, out):
    state = previous[...].astype(jnp.float32) + sum_blocks(returned)
    state_out[...] = state
    normed = normalize(state, gain[...])
    for chip in range(out.shape[0]):
        out[chip] = normed


def fresh_kernel(experts, step, rows, other, *refs):
    weights, old, outs = refs[:4], refs[4], refs[5:]
    line, count, width = outs[0].shape
    half = line * count
    _, total = weighted_outputs(experts, step, True, [rows, other], weights, width)
    y = lax.rem(lax.div(lax.axis_index("expert"), 2), 2)
    low = jnp.full((half, width), y, jnp.int32) == 0
    for i, share in enumerate((total[: 2 * half] + old[...], total[2 * half :])):
        first, second = share[:half], share[half:]
        kept, sent = jnp.where(low, first, second), jnp.where(low, second, first)
        outs[2 * i][...] = kept.reshape(line, count, width)
        outs[2 * i + 1][...] = sent.reshape(line, count, width).astype(jnp.bfloat16)


def part_kernel(distances, kept, received, away, own_out, *sent_outs):
    z = lax.div(lax.axis_index("expert"), 4)
    for distance, out in zip((0,) + distances, (own_out,) + sent_outs):
        place = jnp.bitwise_xor(z, distance)
        total = kept[place] + received[place].astype(jnp.float32)
        out[...] = (total + away[place].astype(jnp.float32)).astype(out.dtype)


def last_kernel(previous, own, *refs):
    total = own[...]
    for received in refs[:-1]:
        total = total + received[...].astype(jnp.float32)
    refs[-1][...] = (previous[...] + total).astype(jnp.bfloat16)


def join_kernel(rows, tables, out):
    width = rows.shape[1]
    out[:, :width] = rows[...]
    out[:, width:] = tables[...]


def weighted_outputs(experts, step, fresh, sources, weights, width):
    rows = jnp.concatenate([source[:, :width] for source in sources], axis=0)
    table = jnp.concatenate([source[:, width:] for source in sources], axis=0)
    inputs = jnp.concatenate([rows] * max(1, MATMUL_ROWS // rows.shape[0]), axis=0)
    own = lax.axis_index("expert")
    total = None
    for core in range(2):
        up, down = weights[2 * core : 2 * core + 2]
        owner = own if core == 0 else own + 1 - 2 * lax.rem(own, 2)
        pre_act = lax.dot_general(
            inputs, up[...], (((1,), (1,)), ((), ())), preferred_element_type=jnp.float32
        )
        hidden = (pre_act / (1.0 + jnp.exp(-pre_act))).astype(jnp.bfloat16)
        result = jnp.dot(hidden, down[...], preferred_element_type=jnp.float32)
        result = result[: rows.shape[0]] * row_weights(experts, table, owner, step, fresh)
        total = result if total is None else total + result
    return table, total


def first_kernel(experts, step, orders, rows, across, *refs):
    weights, (out, tables_out) = refs[:4], refs[4:]
    table, total = weighted_outputs(experts, step, False, [rows, across], weights, out.shape[2])
    chips, count, _ = out.shape
    own = lax.div(lax.axis_index("expert"), 2)
    for block, distance in enumerate(orders):
        chip = jnp.bitwise_xor(own, distance)
        place = lax.rem(chip, 2) * (chips // 2) + lax.div(chip, 2)
        span = slice(block * count, (block + 1) * count)
        out[place] = total[span].astype(out.dtype)
        tables_out[place] = table.astype(jnp.float32)[span].astype(tables_out.dtype)


def mlp_kernel(experts, step, fresh, set_count, *refs):
    sources, weights, outs = refs[:set_count], refs[set_count:][:4], refs[set_count + 4 :]
    count, width = outs[0].shape
    _, total = weighted_outputs(experts, step, fresh, sources, weights, width)
    for i, out in enumerate(outs):
        out[...] = total[i * count : (i + 1) * count].astype(out.dtype)


def on_vmem(kernel, inputs, outputs, limit=4 * MIB, cost=None):
    in_vmem = pl.BlockSpec(memory_space=pltpu.VMEM)
    return pl.pallas_call(
        kernel,
        out_shape=[jax.ShapeDtypeStruct(shape, kind) for shape, kind in outputs],
        in_specs=[in_vmem] * len(inputs),
        out_specs=[in_vmem] * len(outputs),
        compiler_params=pltpu.CompilerParams(vmem_limit_bytes=limit),
        cost_estimate=cost,
    )(*inputs)


def run_mlp(kernel, row_sets, weights, outputs):
    size = sum(part.size for part in weights)
    cost = pl.CostEstimate(
        flops=4 * MATMUL_ROWS * size, bytes_accessed=4 * size, transcendentals=0
    )
    return on_vmem(kernel, tuple(row_sets) + tuple(weights), outputs, 8 * MIB, cost)


def swap_core(value):
    size = lax.axis_size("expert")
    return lax.ppermute(value, "expert", [(i, i ^ 1) for i in range(size)])


def swap_group(value):
    return lax.ppermute(value, "group", [(0, 1), (1, 0)])


def swap_chip(value, distance):
    size = lax.axis_size("expert")
    return lax.ppermute(value, "expert", [(i, i ^ 2 * distance) for i in range(size)])


def gather(block, chips, waiting):
    orders = [0] + list(range(chips - 2, 0, -2))
    received = [swap_chip(block, distance) for distance in orders[1:]]
    received = lax.optimization_barrier(tuple(received) + tuple(waiting))
    parts, waiting = (block,) + received[: len(orders) - 1], received[len(orders) - 1 :]
    rows, width = block.shape
    (block,) = on_vmem(stack_kernel, parts, [((len(parts), rows, width), block.dtype)])
    block = block.reshape(len(parts) * rows, width)
    return block, swap_chip(block, 1), orders + [order ^ 1 for order in orders], waiting


def spread(blocks):
    size = lax.axis_size("expert")
    groups = [
        [start + core for y in range(2) for start in range(2 * y, size, 4)] for core in range(2)
    ]
    return lax.all_to_all(blocks, "expert", 0, 0, axis_index_groups=groups, tiled=True)


def exchange_plan(tokens, norm_gain, routes, route_scale, changed, stale, learner):
    experts = lax.axis_size("expert")
    chips = experts // 2
    row_count, width = tokens.shape[1], tokens.shape[2]
    half = chips * row_count
    steps_total = routes.shape[0]
    packed = width + table_width(experts, steps_total)
    gain = norm_gain[None]
    state_shape = ((row_count, width), jnp.float32)
    weight_bytes = 2 * sum(part.size for part in stale + learner)
    long = pl.CostEstimate(
        flops=1280 * weight_bytes, bytes_accessed=2 * weight_bytes, transcendentals=0
    )
    lanes = ((row_count, table_width(experts, steps_total)), jnp.int32)
    section, expert = on_vmem(
        functools.partial(lane_kernel, experts), (), [lanes, lanes], cost=long
    )
    stale = stale + tuple(swap_core(part) for part in stale)
    (block,) = on_vmem(
        pack_kernel,
        (section, expert, tokens[0], gain, routes, route_scale, changed),
        [((row_count, packed), jnp.bfloat16)],
    )
    state = tokens[0]
    for step in range(steps_total):
        if step == 0:
            rows, across, orders, learner = gather(block, chips, learner)
            learner = learner + tuple(swap_core(part) for part in learner)
            share, tables = run_mlp(
                functools.partial(first_kernel, experts, step, orders),
                [rows, across],
                stale,
                [
                    ((chips, row_count, width), jnp.bfloat16),
                    ((chips, row_count, packed - width), jnp.bfloat16),
                ],
            )
            tables = tables.reshape(half, packed - width)
        else:
            state, blocks = on_vmem(
                next_kernel,
                (state, returned, gain),
                [state_shape, ((chips, row_count, width), jnp.bfloat16)],
            )
            rows = spread(blocks).reshape(half, width)
            (rows,) = on_vmem(join_kernel, (rows, tables), [((half, packed), jnp.bfloat16)])
            other = swap_group(rows)
            kept = ((half, width), jnp.float32)
            kernel = functools.partial(mlp_kernel, experts, step, False, 1)
            (old,) = run_mlp(kernel, [rows], stale, [kept])
            other, old = lax.optimization_barrier((other, old))
            line = (chips // 2, row_count, width)
            kept, sent, away_kept, away_sent = run_mlp(
                functools.partial(fresh_kernel, experts, step),
                [rows, other],
                tuple(learner) + (old,),
                [(line, jnp.float32), (line, jnp.bfloat16)] * 2,
            )
            away = away_kept + swap_chip(away_sent, 1).astype(jnp.float32)
            away = swap_group(away.astype(jnp.bfloat16))
            distances = tuple(range(chips // 2 - 1, 0, -1))
            own, *sent = on_vmem(
                functools.partial(part_kernel, distances),
                (kept, swap_chip(sent, 1), away),
                [state_shape] + [((row_count, width), jnp.bfloat16)] * len(distances),
            )
            received = [swap_chip(part, 2 * d) for part, d in zip(sent, distances)]
            break
        returned = spread(share)
    (updated,) = on_vmem(
        last_kernel, (state, own, *received), [((row_count, width), jnp.bfloat16)]
    )
    return updated[None]


def gather_plan(tokens, norm_gain, routes, route_scale, changed, stale, learner):
    experts = lax.axis_size("expert")
    owner_index = lax.axis_index("expert")
    row_count = tokens.shape[1]
    top_count = routes.shape[3]
    capacity = min(row_count, max(2, 2 * row_count * top_count // experts))
    is_fresh = jnp.any(changed[0] == owner_index)
    fresh = [lax.all_gather(part, "group", axis=0, tiled=True) for part in learner]
    newer = [jnp.where(is_fresh, new, old) for new, old in zip(fresh, stale)]
    state = tokens[0].astype(jnp.float32)
    buffer_ids = jnp.arange(experts * capacity, dtype=jnp.int32)
    expert_ids = jnp.arange(experts, dtype=jnp.int32)
    for step in range(routes.shape[0]):
        normed = normalize(state, norm_gain)
        chosen = routes[step, 0]
        weights = route_scale[step, 0]
        hits = (chosen.reshape(-1)[:, None] == expert_ids[None, :]).astype(jnp.int32)
        before = jnp.cumsum(hits, axis=0) - hits
        slot_pos = jnp.sum(before * hits, axis=1).reshape(chosen.shape)
        target = chosen * capacity + slot_pos
        placed = (target[:, :, None] == buffer_ids[None, None, :]).astype(jnp.float32)
        merge_weights = jnp.sum(placed * weights[:, :, None], axis=1)
        send_matrix = jnp.sum(placed, axis=1).astype(jnp.bfloat16)
        outgoing = lax.dot_general(
            send_matrix, normed, (((0,), (0,)), ((), ())), preferred_element_type=jnp.float32
        )
        outgoing = outgoing.astype(jnp.bfloat16).reshape(experts, capacity, -1)
        received = lax.all_to_all(outgoing, "expert", split_axis=0, concat_axis=0, tiled=True)
        flat = received.reshape(-1, received.shape[-1])
        result = expert_apply(flat, *(stale if step == 0 else newer))
        answer = result.astype(jnp.bfloat16).reshape(received.shape)
        returned = lax.all_to_all(answer, "expert", split_axis=0, concat_axis=0, tiled=True)
        flat_back = returned.reshape(experts * capacity, -1).astype(jnp.float32)
        state = state + jnp.dot(merge_weights, flat_back, precision=lax.Precision.HIGHEST)
    return state.astype(jnp.bfloat16)[None]


def local(
    tokens,
    norm_gain,
    routes,
    route_scale,
    changed,
    rollout_up,
    rollout_down,
    learner_up,
    learner_down,
):
    experts = lax.axis_size("expert")
    groups = lax.axis_size("group")
    fewer = tokens.shape[1] * experts < learner_up.shape[1]
    paired = experts & (experts - 1) == 0 and experts >= 8 and groups == 2 and routes.shape[0] == 2
    plan = exchange_plan if fewer and paired else gather_plan
    stale = (rollout_up[0], rollout_down[0])
    learner = (learner_up[0], learner_down[0])
    return plan(tokens, norm_gain, routes, route_scale, changed, stale, learner)


def solution(mesh):
    placed = (
        P("group", "expert", None),
        P(),
        P(None, "group", "expert", None),
        P(None, "group", "expert", None),
        P("group", None),
        P("expert", None, None),
        P("expert", None, None),
        P("expert", "group", None),
        P("expert", "group", None),
    )
    return jax.shard_map(
        local, mesh=mesh, in_specs=placed, out_specs=P("group", "expert", None), check_vma=False
    )
```

```python
import functools
import jax
import jax.numpy as jnp
from jax import lax
from jax.experimental import pallas as pl
from jax.experimental.pallas import tpu as pltpu
from jax.sharding import PartitionSpec as P

LANES = 128
MATMUL_ROWS = 128
MIB = 1 << 20


def normalize(state, norm_gain):
    scale = lax.rsqrt(jnp.mean(state * state, axis=-1, keepdims=True) + 1e-06)
    return (state * scale * norm_gain).astype(jnp.bfloat16)


def expert_apply(inputs, up_rows, down_rows):
    pre_act = lax.dot_general(
        inputs, up_rows, (((1,), (1,)), ((), ())), preferred_element_type=jnp.float32
    )
    hidden = jax.nn.silu(pre_act).astype(jnp.bfloat16)
    return jnp.dot(hidden, down_rows, preferred_element_type=jnp.float32)


def table_width(experts, steps_total):
    sections = 2 + 4 * (steps_total - 1)
    return -(-sections * experts // LANES) * LANES


def first_section(step, fresh):
    return 0 if step == 0 else 4 * step - 2 + 2 * fresh


def lane_kernel(experts, section_out, expert_out):
    lane = lax.broadcasted_iota(jnp.int32, section_out.shape, 1)
    section_out[...] = lane // experts
    expert_out[...] = lane % experts


def weight_table(section, expert, chosen, weights, changed):
    steps_total, _, _, top_count = chosen.shape
    shape = section.shape
    fresh = section < 0
    for i in range(changed.shape[1]):
        fresh = fresh | (expert == changed[:, i : i + 1])
    table = jnp.zeros(shape, jnp.float32)
    for step in range(steps_total):
        dense = jnp.zeros(shape, jnp.float32)
        for k in range(top_count):
            hit = chosen[step, 0, :, k : k + 1] == expert
            dense = jnp.where(hit, weights[step, 0, :, k : k + 1], dense)
        high = dense.astype(jnp.bfloat16).astype(jnp.float32)
        value = jnp.where(section % 2 == 0, high, dense - high)
        start = first_section(step, False)
        if step == 0:
            table = jnp.where(section < 2, value, table)
        else:
            old = jnp.where(fresh, 0.0, value)
            new = jnp.where(fresh, value, 0.0)
            table = jnp.where((section >= start) & (section < start + 2), old, table)
            table = jnp.where((section >= start + 2) & (section < start + 4), new, table)
    return table.astype(jnp.bfloat16)


def row_weights(experts, table, owner, step, fresh):
    lane = lax.broadcasted_iota(jnp.int32, table.shape, 1)
    section = lane // experts
    first = first_section(step, fresh)
    mine = (lane % experts == owner) & (section >= first) & (section < first + 2)
    return jnp.sum(jnp.where(mine, table.astype(jnp.float32), 0.0), axis=1, keepdims=True)


def pack_kernel(section, expert, tokens, gain, routes, scales, changed, out):
    width = tokens.shape[1]
    normed = normalize(tokens[...].astype(jnp.float32), gain[...])
    out[:, :width] = normed
    out[:, width:] = weight_table(section[...], expert[...], routes, scales, changed)


def stack_kernel(*refs):
    for i, part in enumerate(refs[:-1]):
        refs[-1][i] = part[...]


def sum_blocks(blocks):
    total = blocks[0].astype(jnp.float32)
    for chip in range(1, blocks.shape[0]):
        total = total + blocks[chip].astype(jnp.float32)
    return total


def next_kernel(previous, returned, gain, state_out, out):
    state = previous[...].astype(jnp.float32) + sum_blocks(returned)
    state_out[...] = state
    normed = normalize(state, gain[...])
    for chip in range(out.shape[0]):
        out[chip] = normed


def fresh_kernel(experts, step, rows, other, *refs):
    weights, old, outs = refs[:4], refs[4], refs[5:]
    line, count, width = outs[0].shape
    half = line * count
    _, total = weighted_outputs(experts, step, True, [rows, other], weights, width)
    y = lax.rem(lax.div(lax.axis_index("expert"), 2), 2)
    low = jnp.full((half, width), y, jnp.int32) == 0
    for i, share in enumerate((total[: 2 * half] + old[...], total[2 * half :])):
        first, second = share[:half], share[half:]
        kept, sent = jnp.where(low, first, second), jnp.where(low, second, first)
        outs[2 * i][...] = kept.reshape(line, count, width)
        outs[2 * i + 1][...] = sent.reshape(line, count, width).astype(jnp.bfloat16)


def part_kernel(distances, kept, received, away, own_out, *sent_outs):
    z = lax.div(lax.axis_index("expert"), 4)
    for distance, out in zip((0,) + distances, (own_out,) + sent_outs):
        place = jnp.bitwise_xor(z, distance)
        total = kept[place] + received[place].astype(jnp.float32)
        out[...] = (total + away[place].astype(jnp.float32)).astype(out.dtype)


def last_kernel(previous, own, *refs):
    total = own[...]
    for received in refs[:-1]:
        total = total + received[...].astype(jnp.float32)
    refs[-1][...] = (previous[...] + total).astype(jnp.bfloat16)


def join_kernel(rows, tables, out):
    width = rows.shape[1]
    out[:, :width] = rows[...]
    out[:, width:] = tables[...]


def weighted_outputs(experts, step, fresh, sources, weights, width):
    rows = jnp.concatenate([source[:, :width] for source in sources], axis=0)
    table = jnp.concatenate([source[:, width:] for source in sources], axis=0)
    inputs = jnp.concatenate([rows] * max(1, MATMUL_ROWS // rows.shape[0]), axis=0)
    own = lax.axis_index("expert")
    total = None
    for core in range(2):
        up, down = weights[2 * core : 2 * core + 2]
        owner = own if core == 0 else own + 1 - 2 * lax.rem(own, 2)
        pre_act = lax.dot_general(
            inputs, up[...], (((1,), (1,)), ((), ())), preferred_element_type=jnp.float32
        )
        hidden = (pre_act / (1.0 + jnp.exp(-pre_act))).astype(jnp.bfloat16)
        result = jnp.dot(hidden, down[...], preferred_element_type=jnp.float32)
        result = result[: rows.shape[0]] * row_weights(experts, table, owner, step, fresh)
        total = result if total is None else total + result
    return table, total


def first_kernel(experts, step, orders, rows, across, *refs):
    weights, (out, tables_out) = refs[:4], refs[4:]
    table, total = weighted_outputs(experts, step, False, [rows, across], weights, out.shape[2])
    chips, count, _ = out.shape
    own = lax.div(lax.axis_index("expert"), 2)
    for block, distance in enumerate(orders):
        chip = jnp.bitwise_xor(own, distance)
        place = lax.rem(chip, 2) * (chips // 2) + lax.div(chip, 2)
        span = slice(block * count, (block + 1) * count)
        out[place] = total[span].astype(out.dtype)
        tables_out[place] = table.astype(jnp.float32)[span].astype(tables_out.dtype)


def mlp_kernel(experts, step, fresh, set_count, *refs):
    sources, weights, outs = refs[:set_count], refs[set_count:][:4], refs[set_count + 4 :]
    count, width = outs[0].shape
    _, total = weighted_outputs(experts, step, fresh, sources, weights, width)
    for i, out in enumerate(outs):
        out[...] = total[i * count : (i + 1) * count].astype(out.dtype)


def on_vmem(kernel, inputs, outputs, limit=4 * MIB, cost=None):
    in_vmem = pl.BlockSpec(memory_space=pltpu.VMEM)
    return pl.pallas_call(
        kernel,
        out_shape=[jax.ShapeDtypeStruct(shape, kind) for shape, kind in outputs],
        in_specs=[in_vmem] * len(inputs),
        out_specs=[in_vmem] * len(outputs),
        compiler_params=pltpu.CompilerParams(vmem_limit_bytes=limit),
        cost_estimate=cost,
    )(*inputs)


def run_mlp(kernel, row_sets, weights, outputs):
    size = sum(part.size for part in weights)
    cost = pl.CostEstimate(
        flops=4 * MATMUL_ROWS * size, bytes_accessed=4 * size, transcendentals=0
    )
    return on_vmem(kernel, tuple(row_sets) + tuple(weights), outputs, 8 * MIB, cost)


def swap_core(value):
    size = lax.axis_size("expert")
    return lax.ppermute(value, "expert", [(i, i ^ 1) for i in range(size)])


def swap_group(value):
    return lax.ppermute(value, "group", [(0, 1), (1, 0)])


def swap_chip(value, distance):
    size = lax.axis_size("expert")
    return lax.ppermute(value, "expert", [(i, i ^ 2 * distance) for i in range(size)])


def line_distances(chips):
    middle = chips // 4
    return (middle,) + tuple(d for d in range(chips // 2 - 1, 0, -1) if d != middle)


def gather(block, chips, waiting):
    orders = [0] + [2 * distance for distance in line_distances(chips)]
    received = [swap_chip(block, distance) for distance in orders[1:]]
    received = lax.optimization_barrier(tuple(received) + tuple(waiting))
    parts, waiting = (block,) + received[: len(orders) - 1], received[len(orders) - 1 :]
    rows, width = block.shape
    (block,) = on_vmem(stack_kernel, parts, [((len(parts), rows, width), block.dtype)])
    block = block.reshape(len(parts) * rows, width)
    return block, swap_chip(block, 1), orders + [order ^ 1 for order in orders], waiting


def spread(blocks):
    size = lax.axis_size("expert")
    groups = [
        [start + core for y in range(2) for start in range(2 * y, size, 4)] for core in range(2)
    ]
    return lax.all_to_all(blocks, "expert", 0, 0, axis_index_groups=groups, tiled=True)


def exchange_plan(tokens, norm_gain, routes, route_scale, changed, stale, learner):
    experts = lax.axis_size("expert")
    chips = experts // 2
    row_count, width = tokens.shape[1], tokens.shape[2]
    half = chips * row_count
    steps_total = routes.shape[0]
    packed = width + table_width(experts, steps_total)
    gain = norm_gain[None]
    state_shape = ((row_count, width), jnp.float32)
    weight_bytes = 2 * sum(part.size for part in stale + learner)
    long = pl.CostEstimate(
        flops=1280 * weight_bytes, bytes_accessed=2 * weight_bytes, transcendentals=0
    )
    lanes = ((row_count, table_width(experts, steps_total)), jnp.int32)
    section, expert = on_vmem(
        functools.partial(lane_kernel, experts), (), [lanes, lanes], cost=long
    )
    stale = stale + tuple(swap_core(part) for part in stale)
    (block,) = on_vmem(
        pack_kernel,
        (section, expert, tokens[0], gain, routes, route_scale, changed),
        [((row_count, packed), jnp.bfloat16)],
    )
    state = tokens[0]
    for step in range(steps_total):
        if step == 0:
            rows, across, orders, learner = gather(block, chips, learner)
            learner = learner + tuple(swap_core(part) for part in learner)
            share, tables = run_mlp(
                functools.partial(first_kernel, experts, step, orders),
                [rows, across],
                stale,
                [
                    ((chips, row_count, width), jnp.bfloat16),
                    ((chips, row_count, packed - width), jnp.bfloat16),
                ],
            )
            tables = tables.reshape(half, packed - width)
        else:
            state, blocks = on_vmem(
                next_kernel,
                (state, returned, gain),
                [state_shape, ((chips, row_count, width), jnp.bfloat16)],
            )
            rows = spread(blocks).reshape(half, width)
            (rows,) = on_vmem(join_kernel, (rows, tables), [((half, packed), jnp.bfloat16)])
            other = swap_group(rows)
            kept = ((half, width), jnp.float32)
            kernel = functools.partial(mlp_kernel, experts, step, False, 1)
            (old,) = run_mlp(kernel, [rows], stale, [kept])
            other, old = lax.optimization_barrier((other, old))
            line = (chips // 2, row_count, width)
            kept, sent, away_kept, away_sent = run_mlp(
                functools.partial(fresh_kernel, experts, step),
                [rows, other],
                tuple(learner) + (old,),
                [(line, jnp.float32), (line, jnp.bfloat16)] * 2,
            )
            away = away_kept + swap_chip(away_sent, 1).astype(jnp.float32)
            away = swap_group(away.astype(jnp.bfloat16))
            distances = line_distances(chips)
            own, *sent = on_vmem(
                functools.partial(part_kernel, distances),
                (kept, swap_chip(sent, 1), away),
                [state_shape] + [((row_count, width), jnp.bfloat16)] * len(distances),
            )
            received = [swap_chip(part, 2 * d) for part, d in zip(sent, distances)]
            break
        returned = spread(share)
    (updated,) = on_vmem(
        last_kernel, (state, own, *received), [((row_count, width), jnp.bfloat16)]
    )
    return updated[None]


def gather_plan(tokens, norm_gain, routes, route_scale, changed, stale, learner):
    experts = lax.axis_size("expert")
    owner_index = lax.axis_index("expert")
    row_count = tokens.shape[1]
    top_count = routes.shape[3]
    capacity = min(row_count, max(2, 2 * row_count * top_count // experts))
    is_fresh = jnp.any(changed[0] == owner_index)
    fresh = [lax.all_gather(part, "group", axis=0, tiled=True) for part in learner]
    newer = [jnp.where(is_fresh, new, old) for new, old in zip(fresh, stale)]
    state = tokens[0].astype(jnp.float32)
    buffer_ids = jnp.arange(experts * capacity, dtype=jnp.int32)
    expert_ids = jnp.arange(experts, dtype=jnp.int32)
    for step in range(routes.shape[0]):
        normed = normalize(state, norm_gain)
        chosen = routes[step, 0]
        weights = route_scale[step, 0]
        hits = (chosen.reshape(-1)[:, None] == expert_ids[None, :]).astype(jnp.int32)
        before = jnp.cumsum(hits, axis=0) - hits
        slot_pos = jnp.sum(before * hits, axis=1).reshape(chosen.shape)
        target = chosen * capacity + slot_pos
        placed = (target[:, :, None] == buffer_ids[None, None, :]).astype(jnp.float32)
        merge_weights = jnp.sum(placed * weights[:, :, None], axis=1)
        send_matrix = jnp.sum(placed, axis=1).astype(jnp.bfloat16)
        outgoing = lax.dot_general(
            send_matrix, normed, (((0,), (0,)), ((), ())), preferred_element_type=jnp.float32
        )
        outgoing = outgoing.astype(jnp.bfloat16).reshape(experts, capacity, -1)
        received = lax.all_to_all(outgoing, "expert", split_axis=0, concat_axis=0, tiled=True)
        flat = received.reshape(-1, received.shape[-1])
        result = expert_apply(flat, *(stale if step == 0 else newer))
        answer = result.astype(jnp.bfloat16).reshape(received.shape)
        returned = lax.all_to_all(answer, "expert", split_axis=0, concat_axis=0, tiled=True)
        flat_back = returned.reshape(experts * capacity, -1).astype(jnp.float32)
        state = state + jnp.dot(merge_weights, flat_back, precision=lax.Precision.HIGHEST)
    return state.astype(jnp.bfloat16)[None]


def local(
    tokens,
    norm_gain,
    routes,
    route_scale,
    changed,
    rollout_up,
    rollout_down,
    learner_up,
    learner_down,
):
    experts = lax.axis_size("expert")
    groups = lax.axis_size("group")
    fewer = tokens.shape[1] * experts < learner_up.shape[1]
    paired = experts & (experts - 1) == 0 and experts >= 8 and groups == 2 and routes.shape[0] == 2
    plan = exchange_plan if fewer and paired else gather_plan
    stale = (rollout_up[0], rollout_down[0])
    learner = (learner_up[0], learner_down[0])
    return plan(tokens, norm_gain, routes, route_scale, changed, stale, learner)


def solution(mesh):
    placed = (
        P("group", "expert", None),
        P(),
        P(None, "group", "expert", None),
        P(None, "group", "expert", None),
        P("group", None),
        P("expert", None, None),
        P("expert", None, None),
        P("expert", "group", None),
        P("expert", "group", None),
    )
    return jax.shard_map(
        local, mesh=mesh, in_specs=placed, out_specs=P("group", "expert", None), check_vma=False
    )
```

```python
import functools
import jax
import jax.numpy as jnp
from jax import lax
from jax.experimental import pallas as pl
from jax.experimental.pallas import tpu as pltpu
from jax.sharding import PartitionSpec as P

LANES = 128
MATMUL_ROWS = 128
MIB = 1 << 20


def normalize(state, norm_gain):
    scale = lax.rsqrt(jnp.mean(state * state, axis=-1, keepdims=True) + 1e-06)
    return (state * scale * norm_gain).astype(jnp.bfloat16)


def expert_apply(inputs, up_rows, down_rows):
    pre_act = lax.dot_general(
        inputs, up_rows, (((1,), (1,)), ((), ())), preferred_element_type=jnp.float32
    )
    hidden = jax.nn.silu(pre_act).astype(jnp.bfloat16)
    return jnp.dot(hidden, down_rows, preferred_element_type=jnp.float32)


def table_width(experts, steps_total):
    sections = 2 + 4 * (steps_total - 1)
    return -(-sections * experts // LANES) * LANES


def first_section(step, fresh):
    return 0 if step == 0 else 4 * step - 2 + 2 * fresh


def lane_kernel(experts, section_out, expert_out):
    lane = lax.broadcasted_iota(jnp.int32, section_out.shape, 1)
    section_out[...] = lane // experts
    expert_out[...] = lane % experts


def weight_table(section, expert, chosen, weights, changed):
    steps_total, _, _, top_count = chosen.shape
    shape = section.shape
    fresh = section < 0
    for i in range(changed.shape[1]):
        fresh = fresh | (expert == changed[:, i : i + 1])
    table = jnp.zeros(shape, jnp.float32)
    for step in range(steps_total):
        dense = jnp.zeros(shape, jnp.float32)
        for k in range(top_count):
            hit = chosen[step, 0, :, k : k + 1] == expert
            dense = jnp.where(hit, weights[step, 0, :, k : k + 1], dense)
        high = dense.astype(jnp.bfloat16).astype(jnp.float32)
        value = jnp.where(section % 2 == 0, high, dense - high)
        start = first_section(step, False)
        if step == 0:
            table = jnp.where(section < 2, value, table)
        else:
            old = jnp.where(fresh, 0.0, value)
            new = jnp.where(fresh, value, 0.0)
            table = jnp.where((section >= start) & (section < start + 2), old, table)
            table = jnp.where((section >= start + 2) & (section < start + 4), new, table)
    return table.astype(jnp.bfloat16)


def row_weights(experts, table, owner, step, fresh):
    lane = lax.broadcasted_iota(jnp.int32, table.shape, 1)
    section = lane // experts
    first = first_section(step, fresh)
    mine = (lane % experts == owner) & (section >= first) & (section < first + 2)
    return jnp.sum(jnp.where(mine, table.astype(jnp.float32), 0.0), axis=1, keepdims=True)


def pack_kernel(section, expert, tokens, gain, routes, scales, changed, out):
    width = tokens.shape[1]
    normed = normalize(tokens[...].astype(jnp.float32), gain[...])
    out[:, :width] = normed
    out[:, width:] = weight_table(section[...], expert[...], routes, scales, changed)


def stack_kernel(*refs):
    for i, part in enumerate(refs[:-1]):
        refs[-1][i] = part[...]


def sum_blocks(blocks):
    total = blocks[0].astype(jnp.float32)
    for chip in range(1, blocks.shape[0]):
        total = total + blocks[chip].astype(jnp.float32)
    return total


def next_kernel(previous, returned, gain, state_out, out):
    state = previous[...].astype(jnp.float32) + sum_blocks(returned)
    state_out[...] = state
    normed = normalize(state, gain[...])
    for chip in range(out.shape[0]):
        out[chip] = normed


def fresh_kernel(experts, step, rows, other, *refs):
    weights, old, outs = refs[:4], refs[4], refs[5:]
    line, count, width = outs[0].shape
    half = line * count
    _, total = weighted_outputs(experts, step, True, [rows, other], weights, width)
    y = lax.rem(lax.div(lax.axis_index("expert"), 2), 2)
    low = jnp.full((half, width), y, jnp.int32) == 0
    for i, share in enumerate((total[: 2 * half] + old[...], total[2 * half :])):
        first, second = share[:half], share[half:]
        kept, sent = jnp.where(low, first, second), jnp.where(low, second, first)
        outs[2 * i][...] = kept.reshape(line, count, width)
        outs[2 * i + 1][...] = sent.reshape(line, count, width).astype(jnp.bfloat16)


def part_kernel(distances, kept, received, away, own_out, *sent_outs):
    z = lax.div(lax.axis_index("expert"), 4)
    for distance, out in zip((0,) + distances, (own_out,) + sent_outs):
        place = jnp.bitwise_xor(z, distance)
        total = kept[place] + received[place].astype(jnp.float32)
        out[...] = (total + away[place].astype(jnp.float32)).astype(out.dtype)


def last_kernel(previous, own, *refs):
    total = own[...]
    for received in refs[:-1]:
        total = total + received[...].astype(jnp.float32)
    refs[-1][...] = (previous[...] + total).astype(jnp.bfloat16)


def join_kernel(rows, tables, out):
    width = rows.shape[1]
    out[:, :width] = rows[...]
    out[:, width:] = tables[...]


def weighted_outputs(experts, step, fresh, sources, weights, width):
    rows = jnp.concatenate([source[:, :width] for source in sources], axis=0)
    table = jnp.concatenate([source[:, width:] for source in sources], axis=0)
    inputs = jnp.concatenate([rows] * max(1, MATMUL_ROWS // rows.shape[0]), axis=0)
    own = lax.axis_index("expert")
    total = None
    for core in range(2):
        up, down = weights[2 * core : 2 * core + 2]
        owner = own if core == 0 else own + 1 - 2 * lax.rem(own, 2)
        pre_act = lax.dot_general(
            inputs, up[...], (((1,), (1,)), ((), ())), preferred_element_type=jnp.float32
        )
        hidden = (pre_act / (1.0 + jnp.exp(-pre_act))).astype(jnp.bfloat16)
        result = jnp.dot(hidden, down[...], preferred_element_type=jnp.float32)
        result = result[: rows.shape[0]] * row_weights(experts, table, owner, step, fresh)
        total = result if total is None else total + result
    return table, total


def first_kernel(experts, step, orders, rows, across, *refs):
    weights, (out, tables_out) = refs[:4], refs[4:]
    table, total = weighted_outputs(experts, step, False, [rows, across], weights, out.shape[2])
    chips, count, _ = out.shape
    own = lax.div(lax.axis_index("expert"), 2)
    for block, distance in enumerate(orders):
        chip = jnp.bitwise_xor(own, distance)
        place = lax.rem(chip, 2) * (chips // 2) + lax.div(chip, 2)
        span = slice(block * count, (block + 1) * count)
        out[place] = total[span].astype(out.dtype)
        tables_out[place] = table.astype(jnp.float32)[span].astype(tables_out.dtype)


def mlp_kernel(experts, step, fresh, set_count, *refs):
    sources, weights, outs = refs[:set_count], refs[set_count:][:4], refs[set_count + 4 :]
    count, width = outs[0].shape
    _, total = weighted_outputs(experts, step, fresh, sources, weights, width)
    for i, out in enumerate(outs):
        out[...] = total[i * count : (i + 1) * count].astype(out.dtype)


def on_vmem(kernel, inputs, outputs, limit=4 * MIB, cost=None):
    in_vmem = pl.BlockSpec(memory_space=pltpu.VMEM)
    return pl.pallas_call(
        kernel,
        out_shape=[jax.ShapeDtypeStruct(shape, kind) for shape, kind in outputs],
        in_specs=[in_vmem] * len(inputs),
        out_specs=[in_vmem] * len(outputs),
        compiler_params=pltpu.CompilerParams(vmem_limit_bytes=limit),
        cost_estimate=cost,
    )(*inputs)


def run_mlp(kernel, row_sets, weights, outputs):
    size = sum(part.size for part in weights)
    cost = pl.CostEstimate(
        flops=4 * MATMUL_ROWS * size, bytes_accessed=4 * size, transcendentals=0
    )
    return on_vmem(kernel, tuple(row_sets) + tuple(weights), outputs, 8 * MIB, cost)


def swap_core(value):
    size = lax.axis_size("expert")
    return lax.ppermute(value, "expert", [(i, i ^ 1) for i in range(size)])


def swap_group(value):
    return lax.ppermute(value, "group", [(0, 1), (1, 0)])


def swap_chip(value, distance):
    size = lax.axis_size("expert")
    return lax.ppermute(value, "expert", [(i, i ^ 2 * distance) for i in range(size)])


def gather(block, chips, waiting):
    orders = [0] + list(range(chips - 2, 0, -2))
    received = [swap_chip(block, distance) for distance in orders[1:]]
    received = lax.optimization_barrier(tuple(received) + tuple(waiting))
    parts, waiting = (block,) + received[: len(orders) - 1], received[len(orders) - 1 :]
    rows, width = block.shape
    (block,) = on_vmem(stack_kernel, parts, [((len(parts), rows, width), block.dtype)])
    block = block.reshape(len(parts) * rows, width)
    return block, swap_chip(block, 1), orders + [order ^ 1 for order in orders], waiting


def spread(blocks):
    size = lax.axis_size("expert")
    groups = [
        [start + core for y in range(2) for start in range(2 * y, size, 4)] for core in range(2)
    ]
    return lax.all_to_all(blocks, "expert", 0, 0, axis_index_groups=groups, tiled=True)


def exchange_plan(tokens, norm_gain, routes, route_scale, changed, stale, learner):
    experts = lax.axis_size("expert")
    chips = experts // 2
    row_count, width = tokens.shape[1], tokens.shape[2]
    half = chips * row_count
    steps_total = routes.shape[0]
    packed = width + table_width(experts, steps_total)
    gain = norm_gain[None]
    state_shape = ((row_count, width), jnp.float32)
    weight_bytes = 2 * sum(part.size for part in stale + learner)
    long = pl.CostEstimate(
        flops=1280 * weight_bytes, bytes_accessed=2 * weight_bytes, transcendentals=0
    )
    lanes = ((row_count, table_width(experts, steps_total)), jnp.int32)
    section, expert = on_vmem(
        functools.partial(lane_kernel, experts), (), [lanes, lanes], cost=long
    )
    stale = stale + tuple(swap_core(part) for part in stale)
    (block,) = on_vmem(
        pack_kernel,
        (section, expert, tokens[0], gain, routes, route_scale, changed),
        [((row_count, packed), jnp.bfloat16)],
    )
    state = tokens[0]
    for step in range(steps_total):
        if step == 0:
            rows, across, orders, learner = gather(block, chips, learner)
            learner = learner + tuple(swap_core(part) for part in learner)
            share, tables = run_mlp(
                functools.partial(first_kernel, experts, step, orders),
                [rows, across],
                stale,
                [
                    ((chips, row_count, width), jnp.bfloat16),
                    ((chips, row_count, packed - width), jnp.bfloat16),
                ],
            )
            tables = tables.reshape(half, packed - width)
        else:
            state, blocks = on_vmem(
                next_kernel,
                (state, returned, gain),
                [state_shape, ((chips, row_count, width), jnp.bfloat16)],
            )
            rows = spread(blocks).reshape(half, width)
            (rows,) = on_vmem(join_kernel, (rows, tables), [((half, packed), jnp.bfloat16)])
            other = swap_group(rows)
            kept = ((half, width), jnp.float32)
            kernel = functools.partial(mlp_kernel, experts, step, False, 1)
            (old,) = run_mlp(kernel, [rows], stale, [kept])
            other, old = lax.optimization_barrier((other, old))
            line = (chips // 2, row_count, width)
            kept, sent, away_kept, away_sent = run_mlp(
                functools.partial(fresh_kernel, experts, step),
                [rows, other],
                tuple(learner) + (old,),
                [(line, jnp.float32), (line, jnp.bfloat16)] * 2,
            )
            away = away_kept + swap_chip(away_sent, 1).astype(jnp.float32)
            away = swap_group(away.astype(jnp.bfloat16))
            middle = chips // 4
            distances = (middle,) + tuple(d for d in range(chips // 2 - 1, 0, -1) if d != middle)
            own, *sent = on_vmem(
                functools.partial(part_kernel, distances),
                (kept, swap_chip(sent, 1), away),
                [state_shape] + [((row_count, width), jnp.bfloat16)] * len(distances),
            )
            received = [swap_chip(part, 2 * d) for part, d in zip(sent, distances)]
            break
        returned = spread(share)
    (updated,) = on_vmem(
        last_kernel, (state, own, *received), [((row_count, width), jnp.bfloat16)]
    )
    return updated[None]


def gather_plan(tokens, norm_gain, routes, route_scale, changed, stale, learner):
    experts = lax.axis_size("expert")
    owner_index = lax.axis_index("expert")
    row_count = tokens.shape[1]
    top_count = routes.shape[3]
    capacity = min(row_count, max(2, 2 * row_count * top_count // experts))
    is_fresh = jnp.any(changed[0] == owner_index)
    fresh = [lax.all_gather(part, "group", axis=0, tiled=True) for part in learner]
    newer = [jnp.where(is_fresh, new, old) for new, old in zip(fresh, stale)]
    state = tokens[0].astype(jnp.float32)
    buffer_ids = jnp.arange(experts * capacity, dtype=jnp.int32)
    expert_ids = jnp.arange(experts, dtype=jnp.int32)
    for step in range(routes.shape[0]):
        normed = normalize(state, norm_gain)
        chosen = routes[step, 0]
        weights = route_scale[step, 0]
        hits = (chosen.reshape(-1)[:, None] == expert_ids[None, :]).astype(jnp.int32)
        before = jnp.cumsum(hits, axis=0) - hits
        slot_pos = jnp.sum(before * hits, axis=1).reshape(chosen.shape)
        target = chosen * capacity + slot_pos
        placed = (target[:, :, None] == buffer_ids[None, None, :]).astype(jnp.float32)
        merge_weights = jnp.sum(placed * weights[:, :, None], axis=1)
        send_matrix = jnp.sum(placed, axis=1).astype(jnp.bfloat16)
        outgoing = lax.dot_general(
            send_matrix, normed, (((0,), (0,)), ((), ())), preferred_element_type=jnp.float32
        )
        outgoing = outgoing.astype(jnp.bfloat16).reshape(experts, capacity, -1)
        received = lax.all_to_all(outgoing, "expert", split_axis=0, concat_axis=0, tiled=True)
        flat = received.reshape(-1, received.shape[-1])
        result = expert_apply(flat, *(stale if step == 0 else newer))
        answer = result.astype(jnp.bfloat16).reshape(received.shape)
        returned = lax.all_to_all(answer, "expert", split_axis=0, concat_axis=0, tiled=True)
        flat_back = returned.reshape(experts * capacity, -1).astype(jnp.float32)
        state = state + jnp.dot(merge_weights, flat_back, precision=lax.Precision.HIGHEST)
    return state.astype(jnp.bfloat16)[None]


def local(
    tokens,
    norm_gain,
    routes,
    route_scale,
    changed,
    rollout_up,
    rollout_down,
    learner_up,
    learner_down,
):
    experts = lax.axis_size("expert")
    groups = lax.axis_size("group")
    fewer = tokens.shape[1] * experts < learner_up.shape[1]
    paired = experts & (experts - 1) == 0 and experts >= 8 and groups == 2 and routes.shape[0] == 2
    plan = exchange_plan if fewer and paired else gather_plan
    stale = (rollout_up[0], rollout_down[0])
    learner = (learner_up[0], learner_down[0])
    return plan(tokens, norm_gain, routes, route_scale, changed, stale, learner)


def solution(mesh):
    placed = (
        P("group", "expert", None),
        P(),
        P(None, "group", "expert", None),
        P(None, "group", "expert", None),
        P("group", None),
        P("expert", None, None),
        P("expert", None, None),
        P("expert", "group", None),
        P("expert", "group", None),
    )
    return jax.shard_map(
        local, mesh=mesh, in_specs=placed, out_specs=P("group", "expert", None), check_vma=False
    )
```
